256 devices in a mesh: req: 16 (over y_hi, z), tp: 8 (over x, core), pp: 2 (over y_lo).
Axes of the slice: x: 4, y: 4 (y_hi: 2, y_lo: 2; y = y_hi * 2 + y_lo), z: 8, core: 2. Of those that a mesh axis runs over, the one named last changes fastest.
Arguments:
- prompt_states: bfloat16 [32, 128, 8192], P('tp', 'req', 'pp'), may hold values from -6 to 6
- prompt_lengths: int32 [32], replicated, may hold values from 1 to 128, 2560 in all
- adapter_ids: int32 [32], replicated, may hold values from 0 to 15
- w_query: bfloat16 [8192, 8192], P('pp', 'req'), may hold values from -2 to 2
- w_key: bfloat16 [8192, 1024], P('pp', 'req'), may hold values from -2 to 2
- value_weight: bfloat16 [8192, 1024], P('pp', 'req'), may hold values from -0.0625 to 0.0625
- down_query: bfloat16 [16, 8192, 32], P('req', 'pp'), may hold values from -0.0625 to 0.0625
- up_query: bfloat16 [16, 32, 8192], P(None, None, 'req'), may hold values from -1 to 1
- down_value: bfloat16 [16, 8192, 32], P('req', 'pp'), may hold values from -0.0625 to 0.0625
- value_up_weight: bfloat16 [16, 32, 1024], P(None, None, 'req'), may hold values from -1 to 1
- step_queries: bfloat16 [32, 4, 8192], P(('req', 'pp')), may hold values from -6 to 6
- step_keyvals: bfloat16 [32, 4, 2, 1024], P(('req', 'pp')), may hold values from -6 to 6
Outputs:
- prefill_out: bfloat16 [32, 128, 8192], P('tp', 'pp', 'req')
- decoded: bfloat16 [32, 4, 8192], P(('req', 'pp'))
The draws below stay inside these ranges and needn't reach their ends.
Inputs may be any that keep to these rules, and one draw needn't show every extreme that they name: `prompt_lengths`: some prompt holds exactly 128 tokens.
All inputs are finite; a program needn't handle non-finite values.
Results may differ from the reference program's by a relative error of at most 0.011.
Values may be sent and summed in bfloat16 or wider, within the bound.
A program may use at most 64 MiB of HBM per device.

```python
import math
import jax
import jax.numpy as jnp
import numpy as np
from jax import lax

MODEL_WIDTH = 8192
QUERY_HEAD_COUNT = 64
KEY_VALUE_HEADS = 8
HEAD_SIZE = 128
ADAPTER_RANK = 32
ADAPTER_COUNT = 16
PROMPT_SLOTS = 128
DECODE_STEPS = 4
REQUEST_COUNT = 32


def key_columns(key):
    base_output = jax.random.truncated_normal(key, -4.0, 4.0, (MODEL_WIDTH, KEY_VALUE_HEADS * HEAD_SIZE), jnp.float32)
    return base_output * MODEL_WIDTH ** (-0.5)


def draw_w_key(key, part):
    shared_rows = key_columns(key)
    return shared_rows.astype(jnp.bfloat16)


def draw_w_query(key, part):
    key = jax.random.fold_in(key, 5)
    own_key = jax.random.fold_in(key, 0)
    own = jax.random.truncated_normal(own_key, -4.0, 4.0, (MODEL_WIDTH, QUERY_HEAD_COUNT * HEAD_SIZE), jnp.float32) * MODEL_WIDTH ** (-0.5)
    return own.astype(jnp.bfloat16)


def draw_prompt_states(key, part):
    key = jax.random.fold_in(key, 7)
    noise_key = jax.random.fold_in(key, 0)
    return jax.random.truncated_normal(noise_key, -6.0, 6.0, (REQUEST_COUNT, PROMPT_SLOTS, MODEL_WIDTH), jnp.float32).astype(jnp.bfloat16)


def draw_step_queries(key, part):
    key = jax.random.fold_in(key, 9)
    base_key = jax.random.fold_in(key, 0)
    return jax.random.truncated_normal(base_key, -6.0, 6.0, (REQUEST_COUNT, DECODE_STEPS, QUERY_HEAD_COUNT * HEAD_SIZE), jnp.float32).astype(jnp.bfloat16)


def draw_step_keyvals(key, part):
    key = jax.random.fold_in(key, 13)
    return jax.random.truncated_normal(key, -6.0, 6.0, (REQUEST_COUNT, DECODE_STEPS, 2, KEY_VALUE_HEADS * HEAD_SIZE), jnp.float32).astype(jnp.bfloat16)


def plant(result, key, smallest, top_value):
    place = [jax.random.randint(jax.random.fold_in(key, axis), (), 0, length) for axis, length in enumerate(result.shape)]
    main_axis = result.shape.index(max(result.shape))
    neighbour = place[:main_axis] + [(place[main_axis] + 1) % result.shape[main_axis]] + place[main_axis + 1:]
    return result.at[tuple(place)].set(smallest).at[tuple(neighbour)].set(top_value)


def block_scale(key, shape, pieces, low, largest):
    factor_of = 1.0
    for axis_at, shards_of in pieces:
        heights = jax.random.uniform(jax.random.fold_in(jax.random.fold_in(key, 6), axis_at), (shards_of,), jnp.float32, low / len(pieces), largest / len(pieces))
        factor_of = factor_of * jnp.repeat(jnp.exp(heights), shape[axis_at] // shards_of).reshape((-1,) + (1,) * (len(shape) - 1 - axis_at))
    return factor_of


def profile(number_of, total, bound, skew):
    loads = [(1 << 20) // math.isqrt(grade ** skew) + 1 for grade in range(2, number_of + 1)]
    rest, given = total - bound - (number_of - 1), [1] * (number_of - 1)
    while rest > 0:
        candidates = [i for i in range(number_of - 1) if given[i] < bound]
        mass, budget = sum([loads[i] for i in candidates]), rest
        for i in candidates:
            more = min(bound - given[i], max(1, budget * loads[i] // mass), rest)
            given[i] = given[i] + more
            rest = rest - more
    return np.array([bound] + given)


def uneven_parts(stream_key, amount, total, limit, slope):
    if amount == 2:
        one = jax.random.randint(stream_key, (), max(1, total - limit), min(limit, total - 1) + 1)
        return jnp.stack([one, total - one])
    tallies = jnp.asarray(profile(amount, total, limit, slope), jnp.int32)
    pairs = (amount - 1) // 2
    donor, taker = tallies[1:1 + 2 * pairs:2], tallies[2:2 + 2 * pairs:2]
    margin = jnp.minimum(donor - 1, limit - taker)
    passed = jax.random.randint(jax.random.fold_in(stream_key, 1), (pairs,), 0, 1 << 20) % (margin + 1)
    tallies = tallies.at[1:1 + 2 * pairs:2].set(donor - passed).at[2:2 + 2 * pairs:2].set(taker + passed)
    return tallies[jax.random.permutation(jax.random.fold_in(stream_key, 2), amount)]


def gaussian(key, shape, deviation, reach, cuts=(), dtype=jnp.bfloat16):
    array = jax.random.normal(key, shape, jnp.float32) * deviation
    if len(cuts) > 0:
        array = block_scale(key, shape, cuts, -0.22, 0.18) * array
    return jnp.clip(array, min=-reach, max=reach).astype(dtype)


def setup_inputs(seed: int = 0) -> dict:
    splits = jax.random.split(jax.random.key(seed), 13)
    prompt_states = draw_prompt_states(jax.random.fold_in(splits[12], 71), 0)
    prompt_lengths = uneven_parts(splits[1], REQUEST_COUNT, REQUEST_COUNT * PROMPT_SLOTS * 5 // 8, PROMPT_SLOTS, 1).astype(jnp.int32)
    adapter_ids = plant(jax.random.randint(splits[2], (REQUEST_COUNT,), 0, ADAPTER_COUNT), jax.random.fold_in(splits[2], 1), 0, ADAPTER_COUNT - 1).astype(jnp.int32)
    w_query = draw_w_query(jax.random.fold_in(splits[12], 71), 0)
    w_key = draw_w_key(jax.random.fold_in(splits[12], 71), 0)
    value_weight = gaussian(splits[5], (MODEL_WIDTH, KEY_VALUE_HEADS * HEAD_SIZE), MODEL_WIDTH ** -0.5, 0.0625, ((0, 2), (1, 16)))
    down_query = gaussian(splits[6], (ADAPTER_COUNT, MODEL_WIDTH, ADAPTER_RANK), MODEL_WIDTH ** -0.5, 0.0625, ((0, 16), (1, 2)))
    up_query = gaussian(splits[7], (ADAPTER_COUNT, ADAPTER_RANK, QUERY_HEAD_COUNT * HEAD_SIZE), ADAPTER_RANK ** -0.5, 1.0, ((2, 16),))
    down_value = gaussian(splits[8], (ADAPTER_COUNT, MODEL_WIDTH, ADAPTER_RANK), MODEL_WIDTH ** -0.5, 0.0625, ((0, 16), (1, 2)))
    value_up_weight = gaussian(splits[9], (ADAPTER_COUNT, ADAPTER_RANK, KEY_VALUE_HEADS * HEAD_SIZE), ADAPTER_RANK ** -0.5, 1.0, ((2, 16),))
    step_queries = draw_step_queries(jax.random.fold_in(splits[12], 71), 0)
    step_keyvals = draw_step_keyvals(jax.random.fold_in(splits[12], 71), 0)
    return {"prompt_states": prompt_states, "prompt_lengths": prompt_lengths, "adapter_ids": adapter_ids, "w_query": w_query, "w_key": w_key, "value_weight": value_weight, "down_query": down_query, "up_query": up_query, "down_value": down_value, "value_up_weight": value_up_weight, "step_queries": step_queries, "step_keyvals": step_keyvals}


NEG = -1.0e30


def prefill_prompt(states, length, adapter, w_query, w_key, value_weight, down_query, up_query, down_value, value_up_weight):
    single_float = jnp.float32
    bf16 = jnp.bfloat16
    rank_query = jnp.dot(states, down_query[adapter], preferred_element_type=single_float).astype(bf16)
    rank_value = jnp.dot(states, down_value[adapter], preferred_element_type=single_float).astype(bf16)
    query_rows = (jnp.dot(states, w_query, preferred_element_type=single_float) + jnp.dot(rank_query, up_query[adapter], preferred_element_type=single_float)).astype(bf16)
    key_rows = jnp.dot(states, w_key, preferred_element_type=single_float).astype(bf16)
    value_rows = (jnp.dot(states, value_weight, preferred_element_type=single_float) + jnp.dot(rank_value, value_up_weight[adapter], preferred_element_type=single_float)).astype(bf16)
    head_group = QUERY_HEAD_COUNT // KEY_VALUE_HEADS
    query_head_rows = query_rows.astype(single_float).reshape(PROMPT_SLOTS, KEY_VALUE_HEADS, head_group, HEAD_SIZE)
    key_head_rows = key_rows.astype(single_float).reshape(PROMPT_SLOTS, KEY_VALUE_HEADS, HEAD_SIZE)
    value_head_rows = value_rows.astype(single_float).reshape(PROMPT_SLOTS, KEY_VALUE_HEADS, HEAD_SIZE)
    scores = jnp.einsum("ikgd,jkd->kgij", query_head_rows, key_head_rows, precision=lax.Precision.HIGHEST) * (HEAD_SIZE ** -0.5)
    rows = jnp.arange(PROMPT_SLOTS)[:, None]
    cols = jnp.arange(PROMPT_SLOTS)[None, :]
    allowed = (cols <= rows) & (cols < length)
    scores = jnp.where(allowed, scores, NEG)
    weights = jax.nn.softmax(scores, axis=-1).astype(bf16)
    mixed = jnp.einsum("kgij,jkd->ikgd", weights.astype(single_float), value_head_rows, precision=lax.Precision.HIGHEST)
    mixed = jnp.where((jnp.arange(PROMPT_SLOTS) < length)[:, None, None, None], mixed, 0.0)
    return mixed.reshape(PROMPT_SLOTS, QUERY_HEAD_COUNT * HEAD_SIZE).astype(bf16), key_rows, value_rows


def decode_request(query_rows, key_value_pairs, key_rows, value_rows, length):
    single_float = jnp.float32
    head_group = QUERY_HEAD_COUNT // KEY_VALUE_HEADS
    query_head_rows = query_rows.astype(single_float).reshape(DECODE_STEPS, KEY_VALUE_HEADS, head_group, HEAD_SIZE)
    every_key = jnp.concatenate([key_rows.astype(single_float).reshape(PROMPT_SLOTS, KEY_VALUE_HEADS, HEAD_SIZE), key_value_pairs[:, 0].astype(single_float).reshape(DECODE_STEPS, KEY_VALUE_HEADS, HEAD_SIZE)], axis=0)
    every_value = jnp.concatenate([value_rows.astype(single_float).reshape(PROMPT_SLOTS, KEY_VALUE_HEADS, HEAD_SIZE), key_value_pairs[:, 1].astype(single_float).reshape(DECODE_STEPS, KEY_VALUE_HEADS, HEAD_SIZE)], axis=0)
    scores = jnp.einsum("skgd,jkd->kgsj", query_head_rows, every_key, precision=lax.Precision.HIGHEST) * (HEAD_SIZE ** -0.5)
    slots = jnp.arange(PROMPT_SLOTS + DECODE_STEPS)[None, :]
    steps_now = jnp.arange(DECODE_STEPS)[:, None]
    allowed = jnp.where(slots < PROMPT_SLOTS, slots < length, slots - PROMPT_SLOTS <= steps_now)
    scores = jnp.where(allowed, scores, NEG)
    weights = jax.nn.softmax(scores, axis=-1)
    out = jnp.einsum("kgsj,jkd->skgd", weights, every_value, precision=lax.Precision.HIGHEST)
    return out.reshape(DECODE_STEPS, QUERY_HEAD_COUNT * HEAD_SIZE).astype(jnp.bfloat16)


def reference(prompt_states, prompt_lengths, adapter_ids, w_query, w_key, value_weight, down_query, up_query, down_value, value_up_weight, step_queries, step_keyvals):
    def one_prompt(items):
        states, length, adapter = items
        return prefill_prompt(states, length, adapter, w_query, w_key, value_weight, down_query, up_query, down_value, value_up_weight)

    prefill_out, key_rows, value_rows = lax.map(one_prompt, (prompt_states, prompt_lengths, adapter_ids))

    def one_request(items):
        return decode_request(*items)

    decoded = lax.map(one_request, (step_queries, step_keyvals, key_rows, value_rows, prompt_lengths))
    return prefill_out, decoded
```

```python
import functools

import jax
import jax.numpy as jnp
from jax import lax
from jax.experimental import pallas as pl
from jax.experimental.pallas import tpu as pltpu
from jax.sharding import PartitionSpec as P

HEAD = 128
SLOTS = 8
SIDE = 256
NEG = -1e30
F32 = jnp.float32
BF16 = jnp.bfloat16
MESH = pl.DeviceIdType.MESH


def kernel(
    req_count,
    tp_count,
    lens,
    adapters,
    x_hbm,
    wq_hbm,
    wk_hbm,
    wv_hbm,
    dq_hbm,
    dv_hbm,
    uq_hbm,
    uv_hbm,
    msg_ref,
    prefill_ref,
    decoded_ref,
    blocks,
    weights,
    side_w,
    uq,
    uv,
    qbuf,
    qrecv,
    side,
    siderecv,
    kv_own,
    kvsend,
    kvrecv,
    lowsend,
    lowrecv,
    rank_all,
    uv_send,
    uv_recv,
    k_full,
    v_full,
    step_in,
    step_out,
    step_recv,
    load_sem,
    ring_send,
    ring_recv,
    q_send,
    q_recv,
    side_send,
    side_recv,
    kv_send,
    kv_recv,
    low_send,
    low_recv,
    rank_send,
    rank_recv,
    uv_sems,
    step_send,
    step_got,
    out_send,
    out_got,
):
    r, t, p = lax.axis_index("req"), lax.axis_index("tp"), lax.axis_index("pp")
    ring = req_count // 2
    h, z = r // ring, r % ring
    rows = x_hbm.shape[0]
    prompts = rows // SLOTS
    cols = qbuf.shape[3]
    heads = cols // HEAD
    per_dev = msg_ref.shape[0]
    above = h * ring + (z + 1) % ring
    below = h * ring + (z + ring - 1) % ring
    across = (1 - h) * ring + z
    other = 1 - p
    pair = r + 1 - 2 * (r % 2)

    def remote(src, dst, send, recv, req=None, tp=None, pp=None):
        where = (r if req is None else req, t if tp is None else tp, p if pp is None else pp)
        return pltpu.make_async_remote_copy(
            src_ref=src,
            dst_ref=dst,
            send_sem=send,
            recv_sem=recv,
            device_id=where,
            device_id_type=MESH,
        )

    loads = [
        pltpu.make_async_copy(src, dst, load_sem.at[i])
        for i, (src, dst) in enumerate(
            [
                (wk_hbm, side_w.at[pl.ds(0, wk_hbm.shape[0])]),
                (wv_hbm, side_w.at[pl.ds(wk_hbm.shape[0], wk_hbm.shape[0])]),
                (dq_hbm, side_w.at[pl.ds(2 * wk_hbm.shape[0], dq_hbm.shape[0])]),
                (
                    dv_hbm,
                    side_w.at[pl.ds(2 * wk_hbm.shape[0] + dq_hbm.shape[0], dq_hbm.shape[0])],
                ),
                (x_hbm, blocks.at[pl.ds(0, rows)]),
                (wq_hbm, weights),
                (uq_hbm, uq),
                (uv_hbm, uv),
            ]
        )
    ]
    for load in loads:
        load.start()

    barrier = pltpu.get_barrier_semaphore()
    for where in ((above, t, p), (below, t, p), (across, t, p), (r, t, other)):
        pl.semaphore_signal(barrier, inc=1, device_id=where, device_id_type=MESH)
    for o in range(1, tp_count):
        pl.semaphore_signal(
            barrier, inc=1, device_id=(r, (t + o) % tp_count, p), device_id_type=MESH
        )
    pl.semaphore_wait(barrier, 3 + tp_count)

    def block(b):
        return blocks.at[pl.ds(pl.multiple_of(b * rows, rows), rows)]

    def hop(b, src, req):
        return remote(src, block(b), ring_send.at[b], ring_recv.at[b], req=req)

    half = ring // 2
    last = 2 * ring - 2

    hop(1, x_hbm, across).start()
    hop(2, x_hbm, above).start()
    if half > 1:
        hop(3, x_hbm, below).start()

    kv_cols, rank = wk_hbm.shape[0], dq_hbm.shape[0]
    used = 2 * kv_cols + 2 * rank
    side_w[used:] = jnp.zeros((SIDE - used, side_w.shape[1]), BF16)
    for load in loads:
        load.wait()

    def project(c, places):
        a = blocks[pl.ds(pl.multiple_of(c * 2 * rows, 2 * rows), 2 * rows), :]
        for n in range(0, cols, 256):
            width = min(256, cols - n)
            got = jnp.dot(a, weights[:, n : n + width], preferred_element_type=F32)
            for i, (zz, hh) in enumerate(places):
                sent = jnp.where(hh == p, 0, 1)
                qbuf[sent, zz, :, n : n + width] = got[i * rows : (i + 1) * rows]
        got = lax.dot_general(
            a, side_w[...], (((1,), (1,)), ((), ())), preferred_element_type=F32
        )
        for i, (zz, hh) in enumerate(places):
            side[hh, zz] = got[i * rows : (i + 1) * rows]

    def q_copy(zz):
        return remote(qbuf.at[1, zz], qrecv.at[zz], q_send.at[zz], q_recv.at[zz], pp=other)

    def side_copy(zz):
        return remote(
            side.at[:, zz], siderecv.at[:, zz], side_send.at[zz], side_recv.at[zz], pp=other
        )

    def exchange(zz):
        side_copy(zz).start()
        q_copy(zz).start()

    def kv_copy(zz):
        return remote(
            kvsend.at[:, zz], kvrecv.at[:, zz], kv_send.at[zz], kv_recv.at[zz], req=pair
        )

    def low_copy(target):
        return remote(
            lowsend.at[target], lowrecv.at[r], low_send.at[target], low_recv.at[r], req=target
        )

    def low_arrival(source):
        return remote(
            lowsend.at[source], lowrecv.at[source], low_send.at[source], low_recv.at[source], req=source
        )

    prompt_of = lax.broadcasted_iota(jnp.int32, (rows, HEAD), 0) // SLOTS
    match = jnp.zeros((rows, HEAD), F32)
    for i in range(prompts):
        mine = jnp.where(adapters[t * prompts + i] == r, 1.0, 0.0)
        match = jnp.where(prompt_of == i, mine, match)

    def finish(zz, self_too):
        side_copy(zz).wait_recv()
        for hh in range(2):
            total = side[hh, zz] + siderecv[hh, zz]
            kv_own[hh, zz] = total[:, :HEAD]
            kvsend[hh, zz] = total[:, :HEAD].astype(BF16)
            low = jnp.where(match > 0.0, total[:, HEAD:SIDE], 0.0).astype(BF16)
            target = hh * ring + zz
            lowsend[target] = low
            if self_too:

                @pl.when(target == r)
                def _():
                    lowrecv[r] = low

                @pl.when(target != r)
                def _():
                    low_copy(target).start()
            else:
                low_copy(target).start()
        kv_copy(zz).start()

    hop(1, x_hbm, across).wait_recv()
    if half > 1:
        hop(4, block(1), above).start()
        hop(5, block(1), below).start()
    else:
        hop(3, block(1), below).start()

    project(0, [(z, h), (z, 1 - h)])
    exchange(z)

    def step(k, _):
        base = 2 + 4 * (k - 1)
        up, down = (z + ring - k) % ring, (z + k) % ring
        hop(base, x_hbm, above).wait_recv()
        hop(base + 4, block(base), above).start()
        hop(base + 1, x_hbm, below).wait_recv()

        @pl.when(k + 1 < half)
        def _():
            hop(base + 5, block(base + 1), below).start()

        project(1 + 2 * (k - 1), [(up, h), (down, h)])
        hop(base + 2, x_hbm, above).wait_recv()

        @pl.when(k + 1 < half)
        def _():
            hop(base + 6, block(base + 2), above).start()

        hop(base + 3, x_hbm, below).wait_recv()

        @pl.when(k + 1 < half)
        def _():
            hop(base + 7, block(base + 3), below).start()

        @pl.when(k + 1 == half)
        def _():
            hop(last + 1, block(base + 3), below).start()

        project(2 + 2 * (k - 1), [(up, 1 - h), (down, 1 - h)])
        exchange(up)
        exchange(down)

        @pl.when(k == 1)
        def _():
            finish(z, True)

        @pl.when(k > 1)
        def _():
            finish((z + ring - k + 1) % ring, False)
            finish((z + k - 1) % ring, False)

        return 0

    lax.fori_loop(1, half, step, 0)
    far = (z + half) % ring
    if half == 1:
        finish(z, True)
    else:
        finish((z + ring - half + 1) % ring, False)
        finish((z + half - 1) % ring, False)
    hop(last, x_hbm, above).wait_recv()
    hop(last + 1, x_hbm, below).wait_recv()
    project(ring - 1, [(far, h), (far, 1 - h)])
    exchange(far)

    def step_copy(i):
        target = t * per_dev + i
        return remote(
            msg_ref.at[i],
            step_in.at[r % per_dev],
            step_send.at[i],
            step_got.at[r % per_dev],
            req=target,
            tp=r // per_dev,
        )

    def step_self(i):
        return (t * per_dev + i == r) & (r // per_dev == t)

    for i in range(per_dev):

        @pl.when(step_self(i))
        def _():
            step_in[r % per_dev] = msg_ref[i]

        @pl.when(jnp.logical_not(step_self(i)))
        def _():
            step_copy(i).start()

    for i in range(prompts):
        uv_send[i] = uv[adapters[t * prompts + i]]
    uv_copy = remote(uv_send, uv_recv, uv_sems.at[0], uv_sems.at[1], req=pair)
    uv_copy.start()

    finish(far, False)

    def others(body):
        def one(o, _):
            body((r + o) % req_count)
            return 0

        lax.fori_loop(1, req_count, one, 0)

    others(lambda source: low_arrival(source).wait_recv())
    low = lowrecv[0].astype(F32)
    for source in range(1, req_count):
        low = low + lowrecv[source].astype(F32)
    rank_all[r] = low.astype(BF16)

    def rank_copy(target, slot):
        return remote(
            rank_all.at[slot], rank_all.at[slot], rank_send.at[target], rank_recv.at[slot], req=target
        )

    others(lambda target: rank_copy(target, r).start())

    for zz in range(ring):
        kv_copy(zz).wait_recv()
        q_copy(zz).wait_recv()
    uv_copy.wait_recv()
    others(lambda source: rank_copy(source, source).wait_recv())

    even = r % 2 == 0
    slots = req_count * SLOTS
    share = slots // 2
    own = kv_own[...].reshape(req_count, prompts, SLOTS, HEAD)
    oth = kvrecv[...].astype(F32).reshape(req_count, prompts, SLOTS, HEAD)
    ranks = rank_all[...].astype(F32).reshape(req_count, prompts, SLOTS, HEAD)
    base_q = (qbuf[0] + qrecv[...]).reshape(ring, prompts, SLOTS, cols)
    my_ranks = rank_all[pl.ds(p * ring, ring)].astype(F32).reshape(ring, prompts, SLOTS, HEAD)
    lane = lax.broadcasted_iota(jnp.int32, (slots, HEAD), 1)
    low_lane = lane < HEAD // 2
    scale = HEAD ** (-0.5)
    row_pos = lax.broadcasted_iota(jnp.int32, (heads * share, slots), 0) % share + p * share
    col_pos = lax.broadcasted_iota(jnp.int32, (heads * share, slots), 1)
    out_pos = lax.broadcasted_iota(jnp.int32, (heads * share, HEAD), 0) % share + p * share
    for i in range(prompts):
        length = lens[t * prompts + i]
        adapter = adapters[t * prompts + i]
        mine = own[:, i].reshape(slots, HEAD)
        theirs = oth[:, i].reshape(slots, HEAD)
        first = jnp.where(even, mine, theirs)
        second = jnp.where(even, theirs, mine)
        k = jnp.where(low_lane, first, pltpu.roll(second, HEAD // 2, 1)).astype(BF16)
        v_base = jnp.where(low_lane, pltpu.roll(first, HEAD // 2, 1), second)
        uv_mine, uv_theirs = uv_send[i], uv_recv[i]
        up_v = jnp.concatenate(
            [jnp.where(even, uv_mine, uv_theirs), jnp.where(even, uv_theirs, uv_mine)], axis=1
        )
        rank_rows = ranks[:, i].reshape(slots, HEAD).astype(BF16)
        v = v_base + jnp.dot(rank_rows[:, rank : 2 * rank], up_v, preferred_element_type=F32)
        v = v.astype(BF16)
        k_full[i] = k
        v_full[i] = v
        rank_q = my_ranks[:, i].reshape(share, HEAD).astype(BF16)[:, :rank]
        q = base_q[:, i].reshape(share, cols) + jnp.dot(
            rank_q, uq[adapter], preferred_element_type=F32
        )
        q = q.astype(BF16)
        q = jnp.concatenate([q[:, g * HEAD : (g + 1) * HEAD] for g in range(heads)], axis=0)
        s = lax.dot_general(q, k, (((1,), (1,)), ((), ())), preferred_element_type=F32) * scale
        s = jnp.where((col_pos <= row_pos) & (col_pos < length), s, NEG)
        e = jnp.exp(s - jnp.max(s, axis=1, keepdims=True))
        w = (e / jnp.sum(e, axis=1, keepdims=True)).astype(BF16)
        o = jnp.dot(w, v, preferred_element_type=F32)
        o = jnp.where(out_pos < length, o, 0.0).astype(BF16)
        for g in range(heads):
            prefill_ref[i, :, g * HEAD : (g + 1) * HEAD] = o[g * share : (g + 1) * share]

    steps = step_out.shape[1] // heads
    qrows = heads * steps

    def step_arrival(j):
        source_req = t * per_dev + j
        return remote(
            msg_ref.at[0],
            step_in.at[j],
            step_send.at[0],
            step_got.at[j],
            req=source_req,
            tp=r // per_dev,
        )

    def out_copy(j, target):
        return remote(
            step_out.at[j],
            step_recv.at[r],
            out_send.at[j, target],
            out_got.at[r],
            req=t * per_dev + j,
            tp=target,
        )

    def out_arrival(source):
        return remote(
            step_out.at[0],
            step_recv.at[source],
            out_send.at[0, 0],
            out_got.at[source],
            req=source,
            tp=r // per_dev,
        )

    for j in range(per_dev):

        @pl.when(jnp.logical_not((t * per_dev + j == r) & (r // per_dev == t)))
        def _():
            step_arrival(j).wait_recv()

        n = 2 * j + p
        length = lens[t * prompts + n]
        k, v = k_full[n], v_full[n]
        got = step_in[j]
        qs = got[:qrows]
        tail = got[qrows:].astype(F32)
        new_k = tail[:SLOTS].astype(BF16)
        new_v = tail[SLOTS : 2 * SLOTS].astype(BF16)
        s_old = lax.dot_general(qs, k, (((1,), (1,)), ((), ())), preferred_element_type=F32) * scale
        s_new = (
            lax.dot_general(qs, new_k, (((1,), (1,)), ((), ())), preferred_element_type=F32) * scale
        )
        s_old = jnp.where(lax.broadcasted_iota(jnp.int32, (qrows, slots), 1) < length, s_old, NEG)
        at_step = lax.broadcasted_iota(jnp.int32, (qrows, SLOTS), 0) % steps
        at_new = lax.broadcasted_iota(jnp.int32, (qrows, SLOTS), 1)
        s_new = jnp.where(at_new <= at_step, s_new, NEG)
        top = jnp.maximum(
            jnp.max(s_old, axis=1, keepdims=True), jnp.max(s_new, axis=1, keepdims=True)
        )
        e_old, e_new = jnp.exp(s_old - top), jnp.exp(s_new - top)
        total = jnp.sum(e_old, axis=1, keepdims=True) + jnp.sum(e_new, axis=1, keepdims=True)
        mixed = jnp.zeros((qrows, HEAD), F32)
        for e, values in ((e_old, v), (e_new, new_v)):
            coarse = e.astype(BF16)
            fine = (e - coarse.astype(F32)).astype(BF16)
            mixed = mixed + jnp.dot(coarse, values, preferred_element_type=F32)
            mixed = mixed + jnp.dot(fine, values, preferred_element_type=F32)
        step_out[j] = (mixed / total).astype(BF16)
        for o in range(tp_count):
            target = (t + o) % tp_count
            if o == 0:

                @pl.when(t * per_dev + j == r)
                def _():
                    step_recv[r] = step_out[j]

                @pl.when(t * per_dev + j != r)
                def _():
                    out_copy(j, t).start()
            else:
                out_copy(j, target).start()

    for b in range(1, 2 * ring):
        hop(b, x_hbm, above).wait_send()
    for zz in range(ring):
        q_copy(zz).wait_send()
        side_copy(zz).wait_send()
        kv_copy(zz).wait_send()
    others(lambda target: low_copy(target).wait_send())
    others(lambda target: rank_copy(target, r).wait_send())
    uv_copy.wait_send()
    for i in range(per_dev):

        @pl.when(jnp.logical_not(step_self(i)))
        def _():
            step_copy(i).wait_send()

    for j in range(per_dev):
        for target in range(tp_count):

            @pl.when(jnp.logical_not((t * per_dev + j == r) & (target == t)))
            def _():
                out_copy(j, target).wait_send()

    def arrive(source, _):
        @pl.when(jnp.logical_not((source == r) & (r // per_dev == t)))
        def _():
            out_arrival(source).wait_recv()

        return 0

    lax.fori_loop(0, req_count, arrive, 0)
    decoded_ref[...] = step_recv[...]


def local(
    prompt_states,
    prompt_lengths,
    adapter_ids,
    w_query,
    w_key,
    value_weight,
    down_query,
    up_query,
    down_value,
    value_up_weight,
    step_queries,
    step_keyvals,
):
    req_count, tp_count = lax.axis_size("req"), lax.axis_size("tp")
    t = lax.axis_index("tp")
    prompts, slots, width = prompt_states.shape
    rows = prompts * slots
    cols = w_query.shape[1]
    kv_cols = w_key.shape[1]
    rank = down_query.shape[2]
    adapter_count = up_query.shape[0]
    ring = req_count // 2
    heads = cols // HEAD
    steps = step_queries.shape[1]
    per_dev = req_count // tp_count
    total_slots = req_count * slots

    qs = lax.dynamic_slice_in_dim(step_queries[0], t * per_dev * cols, per_dev * cols, 1)
    qs = qs.reshape(steps, per_dev, heads, HEAD).transpose(1, 2, 0, 3)
    qs = qs.reshape(per_dev, heads * steps, HEAD)
    kv = lax.dynamic_slice_in_dim(
        step_keyvals[0], t * per_dev * kv_cols, per_dev * kv_cols, 2
    ).reshape(steps, 2, per_dev // 2, HEAD)
    kv = jnp.repeat(kv.transpose(2, 1, 0, 3), 2, axis=0)
    kv = jnp.pad(kv, ((0, 0), (0, 0), (0, SLOTS - steps), (0, 0))).reshape(per_dev, 2 * SLOTS, HEAD)
    message = jnp.concatenate([qs, kv], axis=1)

    vmem = pl.BlockSpec(memory_space=pltpu.VMEM)
    smem = pl.BlockSpec(memory_space=pltpu.SMEM)
    hbm = pl.BlockSpec(memory_space=pl.ANY)
    dma = pltpu.SemaphoreType.DMA
    prefill, decoded = pl.pallas_call(
        functools.partial(kernel, req_count, tp_count),
        out_shape=(
            jax.ShapeDtypeStruct((prompts, total_slots // 2, cols), BF16),
            jax.ShapeDtypeStruct((req_count, heads * steps, HEAD), BF16),
        ),
        in_specs=[smem, smem] + [hbm] * 8 + [vmem],
        out_specs=(vmem, vmem),
        scratch_shapes=[
            pltpu.VMEM((req_count * rows, width), BF16),
            pltpu.VMEM((width, cols), BF16),
            pltpu.VMEM((SIDE, width), BF16),
            pltpu.VMEM((adapter_count, rank, cols), BF16),
            pltpu.VMEM((adapter_count, rank, kv_cols), BF16),
            pltpu.VMEM((2, ring, rows, cols), F32),
            pltpu.VMEM((ring, rows, cols), F32),
            pltpu.VMEM((2, ring, rows, SIDE), F32),
            pltpu.VMEM((2, ring, rows, SIDE), F32),
            pltpu.VMEM((2, ring, rows, HEAD), F32),
            pltpu.VMEM((2, ring, rows, HEAD), BF16),
            pltpu.VMEM((2, ring, rows, HEAD), BF16),
            pltpu.VMEM((req_count, rows, HEAD), BF16),
            pltpu.VMEM((req_count, rows, HEAD), BF16),
            pltpu.VMEM((req_count, rows, HEAD), BF16),
            pltpu.VMEM((prompts, rank, kv_cols), BF16),
            pltpu.VMEM((prompts, rank, kv_cols), BF16),
            pltpu.VMEM((prompts, total_slots, HEAD), BF16),
            pltpu.VMEM((prompts, total_slots, HEAD), BF16),
            pltpu.VMEM((per_dev, heads * steps + 2 * SLOTS, HEAD), BF16),
            pltpu.VMEM((per_dev, heads * steps, HEAD), BF16),
            pltpu.VMEM((req_count, heads * steps, HEAD), BF16),
            dma((8,)),
            dma((req_count,)),
            dma((req_count,)),
            dma((ring,)),
            dma((ring,)),
            dma((ring,)),
            dma((ring,)),
            dma((ring,)),
            dma((ring,)),
            dma((req_count,)),
            dma((req_count,)),
            dma((req_count,)),
            dma((req_count,)),
            dma((2,)),
            dma((per_dev,)),
            dma((per_dev,)),
            dma((per_dev, tp_count)),
            dma((req_count,)),
        ],
        compiler_params=pltpu.CompilerParams(
            collective_id=0, has_side_effects=True, vmem_limit_bytes=56 * 1024 * 1024
        ),
        cost_estimate=pl.CostEstimate(
            flops=2 * req_count * rows * width * (cols + SIDE),
            bytes_accessed=2 * width * (cols + SIDE),
            transcendentals=0,
        ),
    )(
        prompt_lengths,
        adapter_ids,
        prompt_states.reshape(rows, width),
        w_query,
        w_key.T,
        value_weight.T,
        down_query[0].T,
        down_value[0].T,
        up_query,
        value_up_weight,
        message,
    )
    decoded = decoded.reshape(req_count, heads, steps, HEAD).transpose(2, 0, 1, 3)
    return prefill, decoded.reshape(1, steps, req_count * cols)


def solution(mesh):
    in_specs = (
        P("tp", "req", "pp"),
        P(),
        P(),
        P("pp", "req"),
        P("pp", "req"),
        P("pp", "req"),
        P("req", "pp", None),
        P(None, None, "req"),
        P("req", "pp", None),
        P(None, None, "req"),
        P(("req", "pp"), None, None),
        P(("req", "pp"), None, None, None),
    )
    out_specs = (P("tp", "pp", "req"), P(("req", "pp"), None, None))
    return jax.shard_map(local, mesh=mesh, in_specs=in_specs, out_specs=out_specs, check_vma=False)
```

```python
import functools

import jax
import jax.numpy as jnp
from jax import lax
from jax.experimental import pallas as pl
from jax.experimental.pallas import tpu as pltpu
from jax.sharding import PartitionSpec as P

HEAD = 128
SLOTS = 8
SIDE = 256
NEG = -1e30
F32 = jnp.float32
BF16 = jnp.bfloat16
MESH = pl.DeviceIdType.MESH


def kernel(
    req_count,
    tp_count,
    lens,
    adapters,
    x_hbm,
    wq_hbm,
    wk_hbm,
    wv_hbm,
    dq_hbm,
    dv_hbm,
    uq_hbm,
    uv_hbm,
    msg_ref,
    prefill_ref,
    decoded_ref,
    blocks,
    weights,
    side_w,
    uq,
    uv,
    q_keep,
    q_out,
    qrecv,
    side,
    side_out,
    siderecv,
    kv_own,
    kvsend,
    kvrecv,
    lowsend,
    lowrecv,
    rank_all,
    late_out,
    late_in,
    ranks_f32,
    uv_send,
    uv_recv,
    k_full,
    v_full,
    step_in,
    step_out,
    step_recv,
    load_sem,
    ring_send,
    ring_recv,
    q_send,
    q_recv,
    side_send,
    side_recv,
    kv_send,
    kv_recv,
    low_send,
    low_recv,
    rank_send,
    rank_recv,
    late_send,
    late_recv,
    uv_sems,
    step_send,
    step_got,
    out_send,
    out_got,
):
    r, t, p = lax.axis_index("req"), lax.axis_index("tp"), lax.axis_index("pp")
    ring = req_count // 2
    h, z = r // ring, r % ring
    rows = x_hbm.shape[0]
    prompts = rows // SLOTS
    cols = q_keep.shape[2]
    part = rows // 2
    heads = cols // HEAD
    per_dev = msg_ref.shape[0]
    above = h * ring + (z + 1) % ring
    below = h * ring + (z + ring - 1) % ring
    across = (1 - h) * ring + z
    other = 1 - p
    pair = r + 1 - 2 * (r % 2)

    def remote(src, dst, send, recv, req=None, tp=None, pp=None):
        where = (r if req is None else req, t if tp is None else tp, p if pp is None else pp)
        return pltpu.make_async_remote_copy(
            src_ref=src,
            dst_ref=dst,
            send_sem=send,
            recv_sem=recv,
            device_id=where,
            device_id_type=MESH,
        )

    loads = [
        pltpu.make_async_copy(src, dst, load_sem.at[i])
        for i, (src, dst) in enumerate(
            [
                (wk_hbm, side_w.at[pl.ds(0, wk_hbm.shape[0])]),
                (wv_hbm, side_w.at[pl.ds(wk_hbm.shape[0], wk_hbm.shape[0])]),
                (dq_hbm, side_w.at[pl.ds(2 * wk_hbm.shape[0], dq_hbm.shape[0])]),
                (
                    dv_hbm,
                    side_w.at[pl.ds(2 * wk_hbm.shape[0] + dq_hbm.shape[0], dq_hbm.shape[0])],
                ),
                (x_hbm, blocks.at[pl.ds(0, rows)]),
                (wq_hbm, weights),
                (uq_hbm, uq),
                (uv_hbm, uv),
            ]
        )
    ]
    for load in loads:
        load.start()

    barrier = pltpu.get_barrier_semaphore()
    for where in ((above, t, p), (below, t, p), (across, t, p), (r, t, other)):
        pl.semaphore_signal(barrier, inc=1, device_id=where, device_id_type=MESH)
    for o in range(1, tp_count):
        pl.semaphore_signal(
            barrier, inc=1, device_id=(r, (t + o) % tp_count, p), device_id_type=MESH
        )
    pl.semaphore_wait(barrier, 3 + tp_count)

    def piece(b, s):
        return blocks.at[pl.ds(pl.multiple_of(b * rows + s * part, part), part)]

    def own_piece(s):
        return x_hbm.at[pl.ds(s * part, part)]

    def hop(b, s, src, req):
        return remote(src, piece(b, s), ring_send.at[b, s], ring_recv.at[b, s], req=req)

    def arrive_hop(b, s):
        hop(b, s, own_piece(s), across).wait_recv()

    half = ring // 2
    last = 2 * ring - 2

    for s in range(2):
        hop(2, s, own_piece(s), above).start()
        if half > 1:
            hop(3, s, own_piece(s), below).start()
        hop(1, s, own_piece(s), across).start()

    kv_cols, rank = wk_hbm.shape[0], dq_hbm.shape[0]
    used = 2 * kv_cols + 2 * rank
    side_w[used:] = jnp.zeros((SIDE - used, side_w.shape[1]), BF16)
    for load in loads:
        load.wait()

    def project(c, places):
        a = blocks[pl.ds(pl.multiple_of(c * 2 * rows, 2 * rows), 2 * rows), :]
        got = lax.dot_general(
            a, side_w[...], (((1,), (1,)), ((), ())), preferred_element_type=F32
        )
        for i, (zz, hh) in enumerate(places):
            side[hh, zz] = got[i * rows : (i + 1) * rows]
            side_out[hh, zz] = got[i * rows : (i + 1) * rows].astype(BF16)
        for n in range(0, cols, 256):
            width = min(256, cols - n)
            got = jnp.dot(a, weights[:, n : n + width], preferred_element_type=F32)
            for i, (zz, hh) in enumerate(places):
                mine = got[i * rows : (i + 1) * rows]

                @pl.when(hh == p)
                def _():
                    q_keep[zz, :, n : n + width] = mine

                @pl.when(hh != p)
                def _():
                    q_out[zz, :, n : n + width] = mine.astype(BF16)

    def q_copy(zz):
        return remote(q_out.at[zz], qrecv.at[zz], q_send.at[zz], q_recv.at[zz], pp=other)

    def side_copy(zz):
        return remote(
            side_out.at[:, zz], siderecv.at[:, zz], side_send.at[zz], side_recv.at[zz], pp=other
        )

    def exchange(zz):
        side_copy(zz).start()
        q_copy(zz).start()

    def kv_copy(zz):
        return remote(
            kvsend.at[:, zz], kvrecv.at[:, zz], kv_send.at[zz], kv_recv.at[zz], req=pair
        )

    def low_copy(target):
        return remote(
            lowsend.at[target], lowrecv.at[r], low_send.at[target], low_recv.at[r], req=target
        )

    def low_arrival(source):
        return remote(
            lowsend.at[source], lowrecv.at[source], low_send.at[source], low_recv.at[source], req=source
        )

    near_lane = lax.broadcasted_iota(jnp.int32, (rows, HEAD), 1) < HEAD // 2
    prompt_of = lax.broadcasted_iota(jnp.int32, (rows, HEAD), 0) // SLOTS
    match = jnp.zeros((rows, HEAD), F32)
    for i in range(prompts):
        mine = jnp.where(adapters[t * prompts + i] == r, 1.0, 0.0)
        match = jnp.where(prompt_of == i, mine, match)

    def finish(zz, self_too):
        side_copy(zz).wait_recv()
        for hh in range(2):
            total = side[hh, zz] + siderecv[hh, zz].astype(F32)
            kv_own[hh, zz] = total[:, :HEAD]
            kvsend[hh, zz] = total[:, :HEAD].astype(BF16)
            low = jnp.where(match > 0.0, total[:, HEAD:SIDE], 0.0).astype(BF16)
            target = hh * ring + zz
            lowsend[target] = low
            if self_too:

                @pl.when(target == r)
                def _():
                    lowrecv[r] = low

                @pl.when(target != r)
                def _():
                    low_copy(target).start()
            else:
                low_copy(target).start()
        kv_copy(zz).start()

    def ahead(k):
        return (z + ring - k) % ring, (z + k) % ring

    for s in range(2):
        if half > 1:
            arrive_hop(2, s)
            if half > 2:
                hop(6, s, piece(2, s), above).start()
            hop(4, s, piece(2, s), across).start()
            arrive_hop(3, s)
            if half > 2:
                hop(7, s, piece(3, s), below).start()
            hop(5, s, piece(3, s), across).start()
    for s in range(2):
        arrive_hop(1, s)
        if half == 1:
            hop(3, s, piece(1, s), below).start()
    project(0, [(z, h), (z, 1 - h)])
    exchange(z)
    if half > 1:
        up, down = ahead(1)
        project(1, [(up, h), (down, h)])

    def step(k, _):
        base = 2 + 4 * (k - 1)
        for s in range(2):
            for side_of in range(2):
                arrive_hop(base + 4 + side_of, s)

                @pl.when(k + 2 < half)
                def _():
                    hop(
                        base + 8 + side_of, s, piece(base + 4 + side_of, s), (above, below)[side_of]
                    ).start()

        up, down = ahead(k + 1)
        project(1 + 2 * k, [(up, h), (down, h)])
        for s in range(2):
            for side_of in range(2):
                arrive_hop(base + 2 + side_of, s)
                hop(
                    base + 6 + side_of, s, piece(base + 2 + side_of, s), (above, below)[side_of]
                ).start()
        up, down = ahead(k)
        project(2 + 2 * (k - 1), [(up, 1 - h), (down, 1 - h)])
        exchange(up)
        exchange(down)

        @pl.when(k == 1)
        def _():
            finish(z, True)

        @pl.when(k > 1)
        def _():
            for zz in ahead(k - 1):
                finish(zz, False)

        return 0

    lax.fori_loop(1, half - 1, step, 0)
    if half > 1:
        base = 2 + 4 * (half - 2)
        for s in range(2):
            arrive_hop(base + 2, s)
            hop(last, s, piece(base, s), above).start()
            arrive_hop(base + 3, s)
            hop(last + 1, s, piece(base + 3, s), below).start()
        up, down = ahead(half - 1)
        project(2 + 2 * (half - 2), [(up, 1 - h), (down, 1 - h)])
        exchange(up)
        exchange(down)
        if half == 2:
            finish(z, True)
        else:
            for zz in ahead(half - 2):
                finish(zz, False)
        for zz in ahead(half - 1):
            finish(zz, False)
    else:
        finish(z, True)
    far = (z + half) % ring
    for s in range(2):
        arrive_hop(last, s)
        arrive_hop(last + 1, s)
    project(ring - 1, [(far, h), (far, 1 - h)])
    exchange(far)

    def step_copy(i):
        target = t * per_dev + i
        return remote(
            msg_ref.at[i],
            step_in.at[r % per_dev],
            step_send.at[i],
            step_got.at[r % per_dev],
            req=target,
            tp=r // per_dev,
        )

    def step_self(i):
        return (t * per_dev + i == r) & (r // per_dev == t)

    for i in range(per_dev):

        @pl.when(step_self(i))
        def _():
            step_in[r % per_dev] = msg_ref[i]

        @pl.when(jnp.logical_not(step_self(i)))
        def _():
            step_copy(i).start()

    for i in range(prompts):
        uv_send[i] = uv[adapters[t * prompts + i]]
    uv_copy = remote(uv_send, uv_recv, uv_sems.at[0], uv_sems.at[1], req=pair)
    uv_copy.start()

    def near(body):
        def one(o, _):
            other_z = (z + o) % ring

            @pl.when(other_z != far)
            def _():
                body(h * ring + other_z)
                body((1 - h) * ring + other_z)

            return 0

        body((1 - h) * ring + z)
        lax.fori_loop(1, ring, one, 0)

    def others(body):
        def one(o, _):
            body((r + o) % req_count)
            return 0

        lax.fori_loop(1, req_count, one, 0)

    near(lambda source: low_arrival(source).wait_recv())
    for hh in range(2):
        lowrecv[hh * ring + far] = jnp.zeros((rows, HEAD), BF16)
    low = lowrecv[0].astype(F32)
    for source in range(1, req_count):
        low = low + lowrecv[source].astype(F32)
    rank_all[r] = low.astype(BF16)

    def rank_copy(target, slot):
        return remote(
            rank_all.at[slot], rank_all.at[slot], rank_send.at[target], rank_recv.at[slot], req=target
        )

    def late_copy(target, slot):
        return remote(
            late_out, late_in.at[slot], late_send.at[target], late_recv.at[slot], req=target
        )

    others(lambda target: rank_copy(target, r).start())

    side_copy(far).wait_recv()
    late = []
    for hh in range(2):
        total = side[hh, far] + siderecv[hh, far].astype(F32)
        kv_own[hh, far] = total[:, :HEAD]
        kvsend[hh, far] = total[:, :HEAD].astype(BF16)
        late.append(jnp.where(match > 0.0, total[:, HEAD:SIDE], 0.0))
    packed = jnp.where(near_lane, late[0], pltpu.roll(late[1], HEAD // 2, 1)).astype(BF16)
    late_out[...] = packed
    late_in[r] = packed
    others(lambda target: late_copy(target, r).start())
    kv_copy(far).start()

    for zz in range(ring):
        kv_copy(zz).wait_recv()
    uv_copy.wait_recv()
    others(lambda source: rank_copy(source, source).wait_recv())
    others(lambda source: late_copy(source, source).wait_recv())

    even = r % 2 == 0
    slots = req_count * SLOTS
    share = slots // 2
    own = kv_own[...].reshape(req_count, prompts, SLOTS, HEAD)
    oth = kvrecv[...].astype(F32).reshape(req_count, prompts, SLOTS, HEAD)
    for zz in range(ring):
        sender = (zz + half) % ring
        both = late_in[sender].astype(F32) + late_in[ring + sender].astype(F32)
        ranks_f32[zz] = rank_all[zz].astype(F32) + jnp.where(near_lane, both, 0.0)
        ranks_f32[ring + zz] = rank_all[ring + zz].astype(F32) + jnp.where(
            near_lane, pltpu.roll(both, HEAD // 2, 1), 0.0
        )
    ranks = ranks_f32[...].reshape(req_count, prompts, SLOTS, HEAD)
    lane = lax.broadcasted_iota(jnp.int32, (slots, HEAD), 1)
    low_lane = lane < HEAD // 2
    scale = HEAD ** (-0.5)
    for i in range(prompts):
        mine = own[:, i].reshape(slots, HEAD)
        theirs = oth[:, i].reshape(slots, HEAD)
        first = jnp.where(even, mine, theirs)
        second = jnp.where(even, theirs, mine)
        k = jnp.where(low_lane, first, pltpu.roll(second, HEAD // 2, 1)).astype(BF16)
        v_base = jnp.where(low_lane, pltpu.roll(first, HEAD // 2, 1), second)
        uv_mine, uv_theirs = uv_send[i], uv_recv[i]
        up_v = jnp.concatenate(
            [jnp.where(even, uv_mine, uv_theirs), jnp.where(even, uv_theirs, uv_mine)], axis=1
        )
        rank_rows = ranks[:, i].reshape(slots, HEAD).astype(BF16)
        v = v_base + jnp.dot(rank_rows[:, rank : 2 * rank], up_v, preferred_element_type=F32)
        k_full[i] = k
        v_full[i] = v.astype(BF16)

    steps = step_out.shape[1] // heads
    qrows = heads * steps

    def step_arrival(j):
        source_req = t * per_dev + j
        return remote(
            msg_ref.at[0],
            step_in.at[j],
            step_send.at[0],
            step_got.at[j],
            req=source_req,
            tp=r // per_dev,
        )

    def out_copy(j, target):
        return remote(
            step_out.at[j],
            step_recv.at[r],
            out_send.at[j, target],
            out_got.at[r],
            req=t * per_dev + j,
            tp=target,
        )

    def out_arrival(source):
        return remote(
            step_out.at[0],
            step_recv.at[source],
            out_send.at[0, 0],
            out_got.at[source],
            req=source,
            tp=r // per_dev,
        )

    for j in range(per_dev):

        @pl.when(jnp.logical_not((t * per_dev + j == r) & (r // per_dev == t)))
        def _():
            step_arrival(j).wait_recv()

        n = 2 * j + p
        length = lens[t * prompts + n]
        k, v = k_full[n], v_full[n]
        got = step_in[j]
        qs = got[:qrows]
        tail = got[qrows:].astype(F32)
        new_k = tail[:SLOTS].astype(BF16)
        new_v = tail[SLOTS : 2 * SLOTS].astype(BF16)
        s_old = lax.dot_general(qs, k, (((1,), (1,)), ((), ())), preferred_element_type=F32) * scale
        s_new = (
            lax.dot_general(qs, new_k, (((1,), (1,)), ((), ())), preferred_element_type=F32) * scale
        )
        s_old = jnp.where(lax.broadcasted_iota(jnp.int32, (qrows, slots), 1) < length, s_old, NEG)
        at_step = lax.broadcasted_iota(jnp.int32, (qrows, SLOTS), 0) % steps
        at_new = lax.broadcasted_iota(jnp.int32, (qrows, SLOTS), 1)
        s_new = jnp.where(at_new <= at_step, s_new, NEG)
        top = jnp.maximum(
            jnp.max(s_old, axis=1, keepdims=True), jnp.max(s_new, axis=1, keepdims=True)
        )
        e_old, e_new = jnp.exp(s_old - top), jnp.exp(s_new - top)
        total = jnp.sum(e_old, axis=1, keepdims=True) + jnp.sum(e_new, axis=1, keepdims=True)
        mixed = jnp.zeros((qrows, HEAD), F32)
        for e, values in ((e_old, v), (e_new, new_v)):
            coarse = e.astype(BF16)
            fine = (e - coarse.astype(F32)).astype(BF16)
            mixed = mixed + jnp.dot(coarse, values, preferred_element_type=F32)
            mixed = mixed + jnp.dot(fine, values, preferred_element_type=F32)
        step_out[j] = (mixed / total).astype(BF16)
        for o in range(tp_count):
            target = (t + o) % tp_count
            if o == 0:

                @pl.when(t * per_dev + j == r)
                def _():
                    step_recv[r] = step_out[j]

                @pl.when(t * per_dev + j != r)
                def _():
                    out_copy(j, t).start()
            else:
                out_copy(j, target).start()

    for zz in range(ring):
        q_copy(zz).wait_recv()
    base_q = (q_keep[...] + qrecv[...].astype(F32)).reshape(ring, prompts, SLOTS, cols)
    my_ranks = ranks_f32[pl.ds(p * ring, ring)].reshape(ring, prompts, SLOTS, HEAD)
    row_pos = lax.broadcasted_iota(jnp.int32, (heads * share, slots), 0) % share + p * share
    col_pos = lax.broadcasted_iota(jnp.int32, (heads * share, slots), 1)
    out_pos = lax.broadcasted_iota(jnp.int32, (heads * share, HEAD), 0) % share + p * share
    for i in range(prompts):
        length = lens[t * prompts + i]
        adapter = adapters[t * prompts + i]
        k, v = k_full[i], v_full[i]
        rank_q = my_ranks[:, i].reshape(share, HEAD).astype(BF16)[:, :rank]
        q = base_q[:, i].reshape(share, cols) + jnp.dot(
            rank_q, uq[adapter], preferred_element_type=F32
        )
        q = q.astype(BF16)
        q = jnp.concatenate([q[:, g * HEAD : (g + 1) * HEAD] for g in range(heads)], axis=0)
        s = lax.dot_general(q, k, (((1,), (1,)), ((), ())), preferred_element_type=F32) * scale
        s = jnp.where((col_pos <= row_pos) & (col_pos < length), s, NEG)
        e = jnp.exp(s - jnp.max(s, axis=1, keepdims=True))
        w = (e / jnp.sum(e, axis=1, keepdims=True)).astype(BF16)
        o = jnp.dot(w, v, preferred_element_type=F32)
        o = jnp.where(out_pos < length, o, 0.0).astype(BF16)
        for g in range(heads):
            prefill_ref[i, :, g * HEAD : (g + 1) * HEAD] = o[g * share : (g + 1) * share]

    for b in range(1, 2 * ring):
        for s in range(2):
            hop(b, s, own_piece(s), above).wait_send()
    for zz in range(ring):
        q_copy(zz).wait_send()
        side_copy(zz).wait_send()
        kv_copy(zz).wait_send()
    near(lambda target: low_copy(target).wait_send())
    others(lambda target: late_copy(target, r).wait_send())
    others(lambda target: rank_copy(target, r).wait_send())
    uv_copy.wait_send()
    for i in range(per_dev):

        @pl.when(jnp.logical_not(step_self(i)))
        def _():
            step_copy(i).wait_send()

    for j in range(per_dev):
        for target in range(tp_count):

            @pl.when(jnp.logical_not((t * per_dev + j == r) & (target == t)))
            def _():
                out_copy(j, target).wait_send()

    def arrive(source, _):
        @pl.when(jnp.logical_not((source == r) & (r // per_dev == t)))
        def _():
            out_arrival(source).wait_recv()

        return 0

    lax.fori_loop(0, req_count, arrive, 0)
    decoded_ref[...] = step_recv[...]


def local(
    prompt_states,
    prompt_lengths,
    adapter_ids,
    w_query,
    w_key,
    value_weight,
    down_query,
    up_query,
    down_value,
    value_up_weight,
    step_queries,
    step_keyvals,
):
    req_count, tp_count = lax.axis_size("req"), lax.axis_size("tp")
    t = lax.axis_index("tp")
    prompts, slots, width = prompt_states.shape
    rows = prompts * slots
    cols = w_query.shape[1]
    kv_cols = w_key.shape[1]
    rank = down_query.shape[2]
    adapter_count = up_query.shape[0]
    ring = req_count // 2
    heads = cols // HEAD
    steps = step_queries.shape[1]
    per_dev = req_count // tp_count
    total_slots = req_count * slots

    qs = lax.dynamic_slice_in_dim(step_queries[0], t * per_dev * cols, per_dev * cols, 1)
    qs = qs.reshape(steps, per_dev, heads, HEAD).transpose(1, 2, 0, 3)
    qs = qs.reshape(per_dev, heads * steps, HEAD)
    kv = lax.dynamic_slice_in_dim(
        step_keyvals[0], t * per_dev * kv_cols, per_dev * kv_cols, 2
    ).reshape(steps, 2, per_dev // 2, HEAD)
    kv = jnp.repeat(kv.transpose(2, 1, 0, 3), 2, axis=0)
    kv = jnp.pad(kv, ((0, 0), (0, 0), (0, SLOTS - steps), (0, 0))).reshape(per_dev, 2 * SLOTS, HEAD)
    message = jnp.concatenate([qs, kv], axis=1)

    vmem = pl.BlockSpec(memory_space=pltpu.VMEM)
    smem = pl.BlockSpec(memory_space=pltpu.SMEM)
    hbm = pl.BlockSpec(memory_space=pl.ANY)
    dma = pltpu.SemaphoreType.DMA
    prefill, decoded = pl.pallas_call(
        functools.partial(kernel, req_count, tp_count),
        out_shape=(
            jax.ShapeDtypeStruct((prompts, total_slots // 2, cols), BF16),
            jax.ShapeDtypeStruct((req_count, heads * steps, HEAD), BF16),
        ),
        in_specs=[smem, smem] + [hbm] * 8 + [vmem],
        out_specs=(vmem, vmem),
        scratch_shapes=[
            pltpu.VMEM((req_count * rows, width), BF16),
            pltpu.VMEM((width, cols), BF16),
            pltpu.VMEM((SIDE, width), BF16),
            pltpu.VMEM((adapter_count, rank, cols), BF16),
            pltpu.VMEM((adapter_count, rank, kv_cols), BF16),
            pltpu.VMEM((ring, rows, cols), F32),
            pltpu.VMEM((ring, rows, cols), BF16),
            pltpu.VMEM((ring, rows, cols), BF16),
            pltpu.VMEM((2, ring, rows, SIDE), F32),
            pltpu.VMEM((2, ring, rows, SIDE), BF16),
            pltpu.VMEM((2, ring, rows, SIDE), BF16),
            pltpu.VMEM((2, ring, rows, HEAD), F32),
            pltpu.VMEM((2, ring, rows, HEAD), BF16),
            pltpu.VMEM((2, ring, rows, HEAD), BF16),
            pltpu.VMEM((req_count, rows, HEAD), BF16),
            pltpu.VMEM((req_count, rows, HEAD), BF16),
            pltpu.VMEM((req_count, rows, HEAD), BF16),
            pltpu.VMEM((rows, HEAD), BF16),
            pltpu.VMEM((req_count, rows, HEAD), BF16),
            pltpu.VMEM((req_count, rows, HEAD), F32),
            pltpu.VMEM((prompts, rank, kv_cols), BF16),
            pltpu.VMEM((prompts, rank, kv_cols), BF16),
            pltpu.VMEM((prompts, total_slots, HEAD), BF16),
            pltpu.VMEM((prompts, total_slots, HEAD), BF16),
            pltpu.VMEM((per_dev, heads * steps + 2 * SLOTS, HEAD), BF16),
            pltpu.VMEM((per_dev, heads * steps, HEAD), BF16),
            pltpu.VMEM((req_count, heads * steps, HEAD), BF16),
            dma((8,)),
            dma((req_count, 2)),
            dma((req_count, 2)),
            dma((ring,)),
            dma((ring,)),
            dma((ring,)),
            dma((ring,)),
            dma((ring,)),
            dma((ring,)),
            dma((req_count,)),
            dma((req_count,)),
            dma((req_count,)),
            dma((req_count,)),
            dma((req_count,)),
            dma((req_count,)),
            dma((2,)),
            dma((per_dev,)),
            dma((per_dev,)),
            dma((per_dev, tp_count)),
            dma((req_count,)),
        ],
        compiler_params=pltpu.CompilerParams(
            collective_id=0, has_side_effects=True, vmem_limit_bytes=56 * 1024 * 1024
        ),
        cost_estimate=pl.CostEstimate(
            flops=2 * req_count * rows * width * (cols + SIDE),
            bytes_accessed=2 * width * (cols + SIDE),
            transcendentals=0,
        ),
    )(
        prompt_lengths,
        adapter_ids,
        prompt_states.reshape(rows, width),
        w_query,
        w_key.T,
        value_weight.T,
        down_query[0].T,
        down_value[0].T,
        up_query,
        value_up_weight,
        message,
    )
    decoded = decoded.reshape(req_count, heads, steps, HEAD).transpose(2, 0, 1, 3)
    return prefill, decoded.reshape(1, steps, req_count * cols)


def solution(mesh):
    in_specs = (
        P("tp", "req", "pp"),
        P(),
        P(),
        P("pp", "req"),
        P("pp", "req"),
        P("pp", "req"),
        P("req", "pp", None),
        P(None, None, "req"),
        P("req", "pp", None),
        P(None, None, "req"),
        P(("req", "pp"), None, None),
        P(("req", "pp"), None, None, None),
    )
    out_specs = (P("tp", "pp", "req"), P(("req", "pp"), None, None))
    return jax.shard_map(local, mesh=mesh, in_specs=in_specs, out_specs=out_specs, check_vma=False)
```

```python
import functools

import jax
import jax.numpy as jnp
from jax import lax
from jax.experimental import pallas as pl
from jax.experimental.pallas import tpu as pltpu
from jax.sharding import PartitionSpec as P

HEAD = 128
SLOTS = 8
SIDE = 256
NEG = -1e30
F32 = jnp.float32
BF16 = jnp.bfloat16
MESH = pl.DeviceIdType.MESH


def kernel(
    req_count,
    tp_count,
    lens,
    adapters,
    x_hbm,
    wq_hbm,
    wk_hbm,
    wv_hbm,
    dq_hbm,
    dv_hbm,
    uq_hbm,
    uv_hbm,
    msg_ref,
    prefill_ref,
    decoded_ref,
    blocks,
    weights,
    side_w,
    uq,
    uv,
    q_keep,
    q_out,
    q_in,
    a_own,
    a_out,
    a_in,
    b_own,
    b_out,
    b_in,
    kv_own,
    kv_oth,
    kv_out,
    kv_in,
    late_in,
    low_out,
    low_in,
    rank_all,
    ranks,
    uv_out,
    uv_in,
    k_full,
    v_full,
    step_in,
    step_out,
    step_recv,
    load_sem,
    ring_send,
    ring_recv,
    map_send,
    map_recv,
    q_send,
    q_recv,
    a_send,
    a_recv,
    b_send,
    b_recv,
    kv_send,
    kv_recv,
    late_send,
    late_recv,
    low_send,
    low_recv,
    rank_send,
    rank_recv,
    uv_sems,
    step_send,
    step_got,
    out_send,
    out_got,
):
    r, t, p = lax.axis_index("req"), lax.axis_index("tp"), lax.axis_index("pp")
    ring = req_count // 2
    half = ring // 2
    h, z = r // ring, r % ring
    rows = x_hbm.shape[0]
    part = rows // 2
    prompts = rows // SLOTS
    cols = q_keep.shape[2]
    heads = cols // HEAD
    per_dev = msg_ref.shape[0]
    kv_cols, rank = wk_hbm.shape[0], dq_hbm.shape[0]
    maps = 2 * rank
    above = h * ring + (z + 1) % ring
    below = h * ring + (z + ring - 1) % ring
    across = (1 - h) * ring + z
    other = 1 - p
    pair = r + 1 - 2 * (r % 2)
    far = (z + half) % ring
    pair_far = (pair % ring + half) % ring

    def remote(src, dst, send, recv, req=None, tp=None, pp=None):
        where = (r if req is None else req, t if tp is None else tp, p if pp is None else pp)
        return pltpu.make_async_remote_copy(
            src_ref=src,
            dst_ref=dst,
            send_sem=send,
            recv_sem=recv,
            device_id=where,
            device_id_type=MESH,
        )

    loads = [
        pltpu.make_async_copy(src, dst, load_sem.at[i])
        for i, (src, dst) in enumerate(
            [
                (dq_hbm, side_w.at[pl.ds(2 * kv_cols, rank)]),
                (dv_hbm, side_w.at[pl.ds(2 * kv_cols + rank, rank)]),
                (wk_hbm, side_w.at[pl.ds(0, kv_cols)]),
                (wv_hbm, side_w.at[pl.ds(kv_cols, kv_cols)]),
                (x_hbm, blocks.at[pl.ds(0, rows)]),
                (wq_hbm, weights),
                (uq_hbm, uq),
                (uv_hbm, uv),
            ]
        )
    ]
    for load in loads:
        load.start()

    barrier = pltpu.get_barrier_semaphore()
    for where in ((above, t, p), (below, t, p), (across, t, p), (r, t, other)):
        pl.semaphore_signal(barrier, inc=1, device_id=where, device_id_type=MESH)
    for o in range(1, tp_count):
        pl.semaphore_signal(
            barrier, inc=1, device_id=(r, (t + o) % tp_count, p), device_id_type=MESH
        )
    pl.semaphore_wait(barrier, 3 + tp_count)

    def own(k, way=0):
        return 0 if k == 0 else 2 + 4 * (k - 1) + (way if k < half else -2)

    def cross(k, way=0):
        if k == 0:
            return 1
        if k == half:
            return 2 * ring - 1
        return 2 + 4 * (k - 1) + (2 if k < half - 1 else 3) + way

    def piece(b, s):
        return blocks.at[pl.ds(b * rows + s * part, part)]

    def own_piece(s):
        return x_hbm.at[pl.ds(s * part, part)]

    def hop(b, s, src, req):
        return remote(src, piece(b, s), ring_send.at[b, s], ring_recv.at[b, s], req=req)

    def arrive(b, s):
        hop(b, s, own_piece(s), across).wait_recv()

    toward = (above, below)
    order = ((0, 0), (1, 1), (0, 1), (1, 0))

    for way, s in order:
        hop(own(1, way), s, own_piece(s), toward[way]).start()

    strip = side_w.shape[1] // tp_count

    def map_at(first, owner):
        return side_w.at[
            pl.ds(first, maps), pl.ds(pl.multiple_of(owner * strip, strip), strip)
        ]

    map_row = 2 * kv_cols + maps

    def map_hop():
        return remote(
            map_at(2 * kv_cols, t), map_at(map_row, t), map_send.at[t], map_recv.at[t], req=across
        )

    def map_spread(target, owner):
        return remote(
            map_at(map_row, owner),
            map_at(map_row, owner),
            map_send.at[target],
            map_recv.at[owner],
            tp=target,
        )

    for load in loads[:2]:
        load.wait()
    map_hop().start()
    for s in range(2):
        hop(cross(0), s, own_piece(s), across).start()
    for load in loads[2:]:
        load.wait()
    map_hop().wait_recv()
    for o in range(1, tp_count):
        map_spread((t + o) % tp_count, t).start()

    def q_copy(zz):
        return remote(q_out.at[zz], q_in.at[zz], q_send.at[zz], q_recv.at[zz], pp=other)

    def a_copy(zz):
        return remote(a_out.at[zz], a_in.at[zz], a_send.at[zz], a_recv.at[zz], pp=other)

    def b_copy(zz):
        return remote(b_out.at[zz], b_in.at[zz], b_send.at[zz], b_recv.at[zz], pp=other)

    def late_copy(i):
        return remote(
            b_out.at[far],
            late_in.at[i],
            late_send.at[i],
            late_recv.at[i],
            req=pair,
            pp=(p, other)[i],
        )

    def project(first, places, in_own, late=False):
        count = len(places) * rows
        at = pl.ds(first * rows, count)
        side = SIDE if any(in_own) else HEAD
        got = lax.dot_general(
            blocks[at, :],
            side_w[:side],
            (((1,), (1,)), ((), ())),
            preferred_element_type=F32,
        )
        for i, (zz, mine) in enumerate(zip(places, in_own)):
            block = got[i * rows : (i + 1) * rows]
            if mine:
                a_own[zz] = block
                a_out[zz] = block.astype(BF16)
                a_copy(zz).start()
            else:
                b_own[zz] = block[:, :HEAD]
                b_out[zz] = block[:, :HEAD].astype(BF16)
                b_copy(zz).start()
                if late:
                    late_copy(0).start()
                    late_copy(1).start()

        def part_of(n, _):
            lanes = pl.ds(pl.multiple_of(n * SIDE, SIDE), SIDE)
            got = jnp.dot(blocks[at, :], weights[:, lanes], preferred_element_type=F32)
            for i, (zz, mine) in enumerate(zip(places, in_own)):
                block = got[i * rows : (i + 1) * rows]
                keep = (h == p) if mine else (h != p)

                @pl.when(keep)
                def _():
                    q_keep[zz, :, lanes] = block

                @pl.when(jnp.logical_not(keep))
                def _():
                    q_out[zz, :, lanes] = block.astype(BF16)

            return 0

        lax.fori_loop(0, cols // SIDE, part_of, 0)
        for zz, mine in zip(places, in_own):

            @pl.when((h != p) if mine else (h == p))
            def _():
                q_copy(zz).start()

    def kv_copy(hh, zz):
        return remote(
            kv_out.at[hh, zz],
            kv_in.at[hh, zz],
            kv_send.at[hh, zz],
            kv_recv.at[hh, zz],
            req=pair,
        )

    def low_copy(zz):
        return remote(
            low_out.at[zz], low_in.at[z], low_send.at[zz], low_recv.at[z], req=h * ring + zz
        )

    def low_arrival(zz):
        return remote(
            low_out.at[zz], low_in.at[zz], low_send.at[zz], low_recv.at[zz], req=h * ring + zz
        )

    near_lane = lax.broadcasted_iota(jnp.int32, (rows, HEAD), 1) < maps
    prompt_of = lax.broadcasted_iota(jnp.int32, (rows, HEAD), 0) // SLOTS
    match = jnp.zeros((rows, HEAD), F32)
    for i in range(prompts):
        adapter = adapters[t * prompts + i]
        mine = jnp.where(adapter == r, 1.0, 0.0)
        theirs = jnp.where(adapter == across, 1.0, 0.0)
        match = jnp.where(prompt_of == i, jnp.where(near_lane, mine, theirs), match)

    def finish_kv(hh, zz, total):
        kv_own[hh, zz] = total
        kv_out[hh, zz] = total.astype(BF16)
        kv_copy(hh, zz).start()

    def finish_own(zz, self_too=False):
        a_copy(zz).wait_recv()
        total = a_own[zz] + a_in[zz].astype(F32)
        finish_kv(h, zz, total[:, :HEAD])
        low = jnp.where(match > 0.0, total[:, HEAD:SIDE], 0.0)
        low = low + pltpu.roll(low, HEAD // 2, 1)
        packed = jnp.where(near_lane[:part], low[:part], low[part:]).astype(BF16)
        if self_too:
            low_in[zz] = packed
        else:
            low_out[zz] = packed
            low_copy(zz).start()

    def finish_cross(zz):
        b_copy(zz).wait_recv()
        finish_kv(1 - h, zz, b_own[zz] + b_in[zz].astype(F32))

    def ahead(k):
        return [(z + ring - k) % ring, (z + k) % ring]

    def arrive_own(k):
        for way, s in order:
            arrive(own(k, way), s)
            src = piece(own(k, way), s)
            if k < half - 1:
                hop(own(k + 1, way), s, src, toward[way]).start()
            elif s == way:
                hop(own(half), s, src, toward[way]).start()
            if k == 1:
                hop(cross(1, way), s, src, across).start()

    def arrive_cross(k):
        for way, s in order:
            arrive(cross(k, way), s)
            src = piece(cross(k, way), s)
            if k < half - 1:
                hop(cross(k + 1, way), s, src, toward[way]).start()
            elif s == way:
                hop(cross(half), s, src, toward[way]).start()

    def arrive_both(b):
        for s in range(2):
            arrive(b, s)

    both = [True, True]
    neither = [False, False]

    arrive_own(1)
    arrive_both(cross(0))
    if half > 2:
        arrive_own(2)
    for o in range(1, tp_count):
        map_spread(t, (t + o) % tp_count).wait_recv()
    project(0, [z, z], [True, False])
    if half > 2:
        project(own(1), ahead(1), both)
    for k in range(3, half):
        arrive_own(k)
        arrive_cross(k - 2)
        if k == 3:
            finish_own(z, True)
            finish_cross(z)
        project(own(k - 1), ahead(k - 1), both)
        project(cross(k - 2), ahead(k - 2), neither)
        for zz in ahead(k - 2):
            finish_own(zz)
    for i in range(prompts):
        uv_out[i] = uv[adapters[t * prompts + i]]
    uv_copy = remote(uv_out, uv_in, uv_sems.at[0], uv_sems.at[1], req=pair)
    uv_copy.start()
    arrive_both(own(half))
    project(own(half - 1), ahead(half - 1) + [far], [True] * 3)
    if half > 2:
        arrive_cross(half - 2)
        for zz in ahead(half - 2):
            finish_own(zz)
        for zz in ahead(half - 1) + [far]:
            finish_own(zz)
        project(cross(half - 2), ahead(half - 2), neither)
        if half > 3:
            for zz in ahead(half - 3):
                finish_cross(zz)
        else:
            finish_own(z, True)
            finish_cross(z)
    else:
        finish_own(z, True)
        finish_cross(z)
        for zz in ahead(half - 1) + [far]:
            finish_own(zz)
    arrive_cross(half - 1)

    def others(body):
        def one(o, _):
            body((r + o) % req_count)
            return 0

        lax.fori_loop(1, req_count, one, 0)

    def column(body):
        def one(o, _):
            body((z + o) % ring)
            return 0

        lax.fori_loop(1, ring, one, 0)

    def rank_copy(target, slot):
        return remote(
            rank_all.at[slot], rank_all.at[slot], rank_send.at[target], rank_recv.at[slot], req=target
        )

    column(lambda zz: low_arrival(zz).wait_recv())
    low = low_in[0].astype(F32)
    for zz in range(1, ring):
        low = low + low_in[zz].astype(F32)
    rank_all[r] = low.astype(BF16)
    others(lambda target: rank_copy(target, r).start())

    project(cross(half - 1), ahead(half - 1), neither)
    if half > 2:
        for zz in ahead(half - 2):
            finish_cross(zz)
    arrive_both(cross(half))
    project(cross(half), [far], [False], late=True)

    def step_copy(i):
        target = t * per_dev + i
        return remote(
            msg_ref.at[i],
            step_in.at[r % per_dev],
            step_send.at[i],
            step_got.at[r % per_dev],
            req=target,
            tp=r // per_dev,
        )

    def step_self(i):
        return (t * per_dev + i == r) & (r // per_dev == t)

    for i in range(per_dev):

        @pl.when(step_self(i))
        def _():
            step_in[r % per_dev] = msg_ref[i]

        @pl.when(jnp.logical_not(step_self(i)))
        def _():
            step_copy(i).start()

    for zz in ahead(half - 1):
        finish_cross(zz)
    b_copy(far).wait_recv()
    kv_own[1 - h, far] = b_own[far] + b_in[far].astype(F32)
    for i in range(2):
        late_copy(i).wait_recv()
    uv_copy.wait_recv()
    for hh in range(2):
        for zz in range(ring):
            there = (hh == 1 - h) & (zz == pair_far)

            @pl.when(jnp.logical_not(there))
            def _():
                kv_copy(hh, zz).wait_recv()
                kv_oth[hh, zz] = kv_in[hh, zz].astype(F32)

            @pl.when(there)
            def _():
                kv_oth[hh, zz] = late_in[0].astype(F32) + late_in[1].astype(F32)

    others(lambda source: rank_copy(source, source).wait_recv())
    for source in range(req_count):
        packed = rank_all[source].astype(F32)
        ranks[source, :part] = packed
        ranks[source, part:] = pltpu.roll(packed, HEAD // 2, 1)

    even = r % 2 == 0
    slots = req_count * SLOTS
    share = slots // 2
    low_lane = lax.broadcasted_iota(jnp.int32, (slots, HEAD), 1) < HEAD // 2
    scale = HEAD ** (-0.5)

    def assemble(n):
        at = pl.ds(pl.multiple_of(n * SLOTS, SLOTS), SLOTS)
        mine = kv_own[:, :, at, :].reshape(slots, HEAD)
        theirs = kv_oth[:, :, at, :].reshape(slots, HEAD)
        first = jnp.where(even, mine, theirs)
        second = jnp.where(even, theirs, mine)
        k = jnp.where(low_lane, first, pltpu.roll(second, HEAD // 2, 1)).astype(BF16)
        v = jnp.where(low_lane, pltpu.roll(first, HEAD // 2, 1), second)
        uv_mine, uv_theirs = uv_out[n], uv_in[n]
        up_v = jnp.concatenate(
            [jnp.where(even, uv_mine, uv_theirs), jnp.where(even, uv_theirs, uv_mine)], axis=1
        )
        rank_rows = ranks[:, at, :].reshape(slots, HEAD).astype(BF16)
        v = v + jnp.dot(rank_rows[:, rank:maps], up_v, preferred_element_type=F32)
        k_full[n] = k
        v_full[n] = v.astype(BF16)

    steps = step_out.shape[1] // heads
    qrows = heads * steps

    def step_arrival(j):
        source_req = t * per_dev + j
        return remote(
            msg_ref.at[0],
            step_in.at[j],
            step_send.at[0],
            step_got.at[j],
            req=source_req,
            tp=r // per_dev,
        )

    def out_copy(j, target):
        return remote(
            step_out.at[j],
            step_recv.at[r],
            out_send.at[j, target],
            out_got.at[r],
            req=t * per_dev + j,
            tp=target,
        )

    def out_arrival(source):
        return remote(
            step_out.at[0],
            step_recv.at[source],
            out_send.at[0, 0],
            out_got.at[source],
            req=source,
            tp=r // per_dev,
        )

    for j in range(per_dev):

        @pl.when(jnp.logical_not((t * per_dev + j == r) & (r // per_dev == t)))
        def _():
            step_arrival(j).wait_recv()

        n = 2 * j + p
        assemble(n)
        length = lens[t * prompts + n]
        k, v = k_full[n], v_full[n]
        got = step_in[j]
        qs = got[:qrows]
        tail = got[qrows:].astype(F32)
        new_k = tail[:SLOTS].astype(BF16)
        new_v = tail[SLOTS : 2 * SLOTS].astype(BF16)
        s_old = lax.dot_general(qs, k, (((1,), (1,)), ((), ())), preferred_element_type=F32) * scale
        s_new = (
            lax.dot_general(qs, new_k, (((1,), (1,)), ((), ())), preferred_element_type=F32) * scale
        )
        s_old = jnp.where(lax.broadcasted_iota(jnp.int32, (qrows, slots), 1) < length, s_old, NEG)
        at_step = lax.broadcasted_iota(jnp.int32, (qrows, SLOTS), 0) % steps
        at_new = lax.broadcasted_iota(jnp.int32, (qrows, SLOTS), 1)
        s_new = jnp.where(at_new <= at_step, s_new, NEG)
        top = jnp.maximum(
            jnp.max(s_old, axis=1, keepdims=True), jnp.max(s_new, axis=1, keepdims=True)
        )
        e_old, e_new = jnp.exp(s_old - top), jnp.exp(s_new - top)
        total = jnp.sum(e_old, axis=1, keepdims=True) + jnp.sum(e_new, axis=1, keepdims=True)
        mixed = jnp.zeros((qrows, HEAD), F32)
        for e, values in ((e_old, v), (e_new, new_v)):
            coarse = e.astype(BF16)
            fine = (e - coarse.astype(F32)).astype(BF16)
            mixed = mixed + jnp.dot(coarse, values, preferred_element_type=F32)
            mixed = mixed + jnp.dot(fine, values, preferred_element_type=F32)
        step_out[j] = (mixed / total).astype(BF16)
        for o in range(tp_count):
            target = (t + o) % tp_count
            if o == 0:

                @pl.when(t * per_dev + j == r)
                def _():
                    step_recv[r] = step_out[j]

                @pl.when(t * per_dev + j != r)
                def _():
                    out_copy(j, t).start()
            else:
                out_copy(j, target).start()

    for j in range(per_dev):
        assemble(2 * j + 1 - p)
    for zz in range(ring):
        q_copy(zz).wait_recv()
    base_q = (q_keep[...] + q_in[...].astype(F32)).reshape(ring, prompts, SLOTS, cols)
    my_ranks = ranks[pl.ds(p * ring, ring)].reshape(ring, prompts, SLOTS, HEAD)
    row_pos = lax.broadcasted_iota(jnp.int32, (heads * share, slots), 0) % share + p * share
    col_pos = lax.broadcasted_iota(jnp.int32, (heads * share, slots), 1)
    out_pos = lax.broadcasted_iota(jnp.int32, (heads * share, HEAD), 0) % share + p * share
    for i in range(prompts):
        length = lens[t * prompts + i]
        adapter = adapters[t * prompts + i]
        k, v = k_full[i], v_full[i]
        rank_q = my_ranks[:, i].reshape(share, HEAD).astype(BF16)[:, :rank]
        q = base_q[:, i].reshape(share, cols) + jnp.dot(
            rank_q, uq[adapter], preferred_element_type=F32
        )
        q = q.astype(BF16)
        q = jnp.concatenate([q[:, g * HEAD : (g + 1) * HEAD] for g in range(heads)], axis=0)
        s = lax.dot_general(q, k, (((1,), (1,)), ((), ())), preferred_element_type=F32) * scale
        s = jnp.where((col_pos <= row_pos) & (col_pos < length), s, NEG)
        e = jnp.exp(s - jnp.max(s, axis=1, keepdims=True))
        w = (e / jnp.sum(e, axis=1, keepdims=True)).astype(BF16)
        o = jnp.dot(w, v, preferred_element_type=F32)
        o = jnp.where(out_pos < length, o, 0.0).astype(BF16)
        for g in range(heads):
            prefill_ref[i, :, g * HEAD : (g + 1) * HEAD] = o[g * share : (g + 1) * share]

    for b in range(1, 2 * ring):
        for s in range(2):
            hop(b, s, own_piece(s), above).wait_send()
    for target in range(tp_count):
        map_spread(target, t).wait_send()
    for zz in range(ring):
        q_copy(zz).wait_send()
        a_copy(zz).wait_send()
        b_copy(zz).wait_send()
        for hh in range(2):

            @pl.when(jnp.logical_not((hh == 1 - h) & (zz == far)))
            def _():
                kv_copy(hh, zz).wait_send()

    for i in range(2):
        late_copy(i).wait_send()
    column(lambda zz: low_copy(zz).wait_send())
    others(lambda target: rank_copy(target, r).wait_send())
    uv_copy.wait_send()
    for i in range(per_dev):

        @pl.when(jnp.logical_not(step_self(i)))
        def _():
            step_copy(i).wait_send()

    for j in range(per_dev):
        for target in range(tp_count):

            @pl.when(jnp.logical_not((t * per_dev + j == r) & (target == t)))
            def _():
                out_copy(j, target).wait_send()

    def got_out(source, _):
        @pl.when(jnp.logical_not((source == r) & (r // per_dev == t)))
        def _():
            out_arrival(source).wait_recv()

        return 0

    lax.fori_loop(0, req_count, got_out, 0)
    decoded_ref[...] = step_recv[...]


def local(
    prompt_states,
    prompt_lengths,
    adapter_ids,
    w_query,
    w_key,
    value_weight,
    down_query,
    up_query,
    down_value,
    value_up_weight,
    step_queries,
    step_keyvals,
):
    req_count, tp_count = lax.axis_size("req"), lax.axis_size("tp")
    t = lax.axis_index("tp")
    prompts, slots, width = prompt_states.shape
    rows = prompts * slots
    cols = w_query.shape[1]
    kv_cols = w_key.shape[1]
    rank = down_query.shape[2]
    adapter_count = up_query.shape[0]
    ring = req_count // 2
    heads = cols // HEAD
    steps = step_queries.shape[1]
    per_dev = req_count // tp_count
    total_slots = req_count * slots

    qs = lax.dynamic_slice_in_dim(step_queries[0], t * per_dev * cols, per_dev * cols, 1)
    qs = qs.reshape(steps, per_dev, heads, HEAD).transpose(1, 2, 0, 3)
    qs = qs.reshape(per_dev, heads * steps, HEAD)
    kv = lax.dynamic_slice_in_dim(
        step_keyvals[0], t * per_dev * kv_cols, per_dev * kv_cols, 2
    ).reshape(steps, 2, per_dev // 2, HEAD)
    kv = jnp.repeat(kv.transpose(2, 1, 0, 3), 2, axis=0)
    kv = jnp.pad(kv, ((0, 0), (0, 0), (0, SLOTS - steps), (0, 0))).reshape(per_dev, 2 * SLOTS, HEAD)
    message = jnp.concatenate([qs, kv], axis=1)

    vmem = pl.BlockSpec(memory_space=pltpu.VMEM)
    smem = pl.BlockSpec(memory_space=pltpu.SMEM)
    hbm = pl.BlockSpec(memory_space=pl.ANY)
    dma = pltpu.SemaphoreType.DMA
    prefill, decoded = pl.pallas_call(
        functools.partial(kernel, req_count, tp_count),
        out_shape=(
            jax.ShapeDtypeStruct((prompts, total_slots // 2, cols), BF16),
            jax.ShapeDtypeStruct((req_count, heads * steps, HEAD), BF16),
        ),
        in_specs=[smem, smem] + [hbm] * 8 + [vmem],
        out_specs=(vmem, vmem),
        scratch_shapes=[
            pltpu.VMEM((req_count * rows, width), BF16),
            pltpu.VMEM((width, cols), BF16),
            pltpu.VMEM((SIDE, width), BF16),
            pltpu.VMEM((adapter_count, rank, cols), BF16),
            pltpu.VMEM((adapter_count, rank, kv_cols), BF16),
            pltpu.VMEM((ring, rows, cols), F32),
            pltpu.VMEM((ring, rows, cols), BF16),
            pltpu.VMEM((ring, rows, cols), BF16),
            pltpu.VMEM((ring, rows, SIDE), F32),
            pltpu.VMEM((ring, rows, SIDE), BF16),
            pltpu.VMEM((ring, rows, SIDE), BF16),
            pltpu.VMEM((ring, rows, HEAD), F32),
            pltpu.VMEM((ring, rows, HEAD), BF16),
            pltpu.VMEM((ring, rows, HEAD), BF16),
            pltpu.VMEM((2, ring, rows, HEAD), F32),
            pltpu.VMEM((2, ring, rows, HEAD), F32),
            pltpu.VMEM((2, ring, rows, HEAD), BF16),
            pltpu.VMEM((2, ring, rows, HEAD), BF16),
            pltpu.VMEM((2, rows, HEAD), BF16),
            pltpu.VMEM((ring, rows // 2, HEAD), BF16),
            pltpu.VMEM((ring, rows // 2, HEAD), BF16),
            pltpu.VMEM((req_count, rows // 2, HEAD), BF16),
            pltpu.VMEM((req_count, rows, HEAD), F32),
            pltpu.VMEM((prompts, rank, kv_cols), BF16),
            pltpu.VMEM((prompts, rank, kv_cols), BF16),
            pltpu.VMEM((prompts, total_slots, HEAD), BF16),
            pltpu.VMEM((prompts, total_slots, HEAD), BF16),
            pltpu.VMEM((per_dev, heads * steps + 2 * SLOTS, HEAD), BF16),
            pltpu.VMEM((per_dev, heads * steps, HEAD), BF16),
            pltpu.VMEM((req_count, heads * steps, HEAD), BF16),
            dma((8,)),
            dma((req_count, 2)),
            dma((req_count, 2)),
            dma((tp_count,)),
            dma((tp_count,)),
            dma((ring,)),
            dma((ring,)),
            dma((ring,)),
            dma((ring,)),
            dma((ring,)),
            dma((ring,)),
            dma((2, ring)),
            dma((2, ring)),
            dma((2,)),
            dma((2,)),
            dma((ring,)),
            dma((ring,)),
            dma((req_count,)),
            dma((req_count,)),
            dma((2,)),
            dma((per_dev,)),
            dma((per_dev,)),
            dma((per_dev, tp_count)),
            dma((req_count,)),
        ],
        compiler_params=pltpu.CompilerParams(
            collective_id=0, has_side_effects=True, vmem_limit_bytes=56 * 1024 * 1024
        ),
        cost_estimate=pl.CostEstimate(
            flops=2 * req_count * rows * width * (cols + SIDE),
            bytes_accessed=2 * width * (cols + SIDE),
            transcendentals=0,
        ),
    )(
        prompt_lengths,
        adapter_ids,
        prompt_states.reshape(rows, width),
        w_query,
        w_key.T,
        value_weight.T,
        down_query[0].T,
        down_value[0].T,
        up_query,
        value_up_weight,
        message,
    )
    decoded = decoded.reshape(req_count, heads, steps, HEAD).transpose(2, 0, 1, 3)
    return prefill, decoded.reshape(1, steps, req_count * cols)


def solution(mesh):
    in_specs = (
        P("tp", "req", "pp"),
        P(),
        P(),
        P("pp", "req"),
        P("pp", "req"),
        P("pp", "req"),
        P("req", "pp", None),
        P(None, None, "req"),
        P("req", "pp", None),
        P(None, None, "req"),
        P(("req", "pp"), None, None),
        P(("req", "pp"), None, None, None),
    )
    out_specs = (P("tp", "pp", "req"), P(("req", "pp"), None, None))
    return jax.shard_map(local, mesh=mesh, in_specs=in_specs, out_specs=out_specs, check_vma=False)
```

```python
import functools

import jax
import jax.numpy as jnp
from jax import lax
from jax.experimental import pallas as pl
from jax.experimental.pallas import tpu as pltpu
from jax.sharding import PartitionSpec as P

HEAD = 128
SLOTS = 8
SIDE = 256
NEG = -1e30
F32 = jnp.float32
BF16 = jnp.bfloat16
MESH = pl.DeviceIdType.MESH


def kernel(
    req_count,
    tp_count,
    lens,
    adapters,
    x_hbm,
    wq_hbm,
    wk_hbm,
    wv_hbm,
    dq_hbm,
    dv_hbm,
    uq_hbm,
    uv_hbm,
    sq_hbm,
    skv_hbm,
    prefill_ref,
    decoded_ref,
    msg_ref,
    msg_f32,
    sq,
    skv,
    blocks,
    weights,
    side_w,
    uq,
    uv,
    q_keep,
    q_out,
    q_in,
    a_own,
    a_out,
    a_in,
    b_own,
    b_out,
    b_in,
    kv_own,
    kv_oth,
    kv_out,
    kv_in,
    late_in,
    low_out,
    low_in,
    rank_all,
    ranks,
    uv_out,
    uv_in,
    k_full,
    v_full,
    step_in,
    step_out,
    step_recv,
    load_sem,
    ring_send,
    ring_recv,
    map_send,
    map_recv,
    q_send,
    q_recv,
    a_send,
    a_recv,
    b_send,
    b_recv,
    kv_send,
    kv_recv,
    late_send,
    late_recv,
    low_send,
    low_recv,
    rank_send,
    rank_recv,
    uv_sems,
    step_send,
    step_got,
    out_send,
    out_got,
):
    r, t, p = lax.axis_index("req"), lax.axis_index("tp"), lax.axis_index("pp")
    ring = req_count // 2
    half = ring // 2
    h, z = r // ring, r % ring
    rows = x_hbm.shape[0]
    part = rows // 2
    prompts = rows // SLOTS
    cols = q_keep.shape[2]
    heads = cols // HEAD
    per_dev = req_count // tp_count
    kv_cols, rank = wk_hbm.shape[0], dq_hbm.shape[0]
    maps = 2 * rank
    above = h * ring + (z + 1) % ring
    below = h * ring + (z + ring - 1) % ring
    across = (1 - h) * ring + z
    other = 1 - p
    pair = r + 1 - 2 * (r % 2)
    far = (z + half) % ring
    pair_late = [(pair + ring - half + 1) % ring, (pair + half - 1) % ring]

    def remote(src, dst, send, recv, req=None, tp=None, pp=None):
        where = (r if req is None else req, t if tp is None else tp, p if pp is None else pp)
        return pltpu.make_async_remote_copy(
            src_ref=src,
            dst_ref=dst,
            send_sem=send,
            recv_sem=recv,
            device_id=where,
            device_id_type=MESH,
        )

    loads = [
        pltpu.make_async_copy(src, dst, load_sem.at[i])
        for i, (src, dst) in enumerate(
            [
                (dq_hbm, side_w.at[pl.ds(2 * kv_cols, rank)]),
                (dv_hbm, side_w.at[pl.ds(2 * kv_cols + rank, rank)]),
                (wk_hbm, side_w.at[pl.ds(0, kv_cols)]),
                (wv_hbm, side_w.at[pl.ds(kv_cols, kv_cols)]),
                (x_hbm, blocks.at[pl.ds(0, rows)]),
                (wq_hbm, weights),
                (uq_hbm, uq),
                (uv_hbm, uv),
                (sq_hbm, sq),
                (skv_hbm, skv),
            ]
        )
    ]
    for load in loads:
        load.start()

    barrier = pltpu.get_barrier_semaphore()
    for where in ((above, t, p), (below, t, p), (across, t, p), (r, t, other)):
        pl.semaphore_signal(barrier, inc=1, device_id=where, device_id_type=MESH)
    for o in range(1, tp_count):
        pl.semaphore_signal(
            barrier, inc=1, device_id=(r, (t + o) % tp_count, p), device_id_type=MESH
        )
    pl.semaphore_wait(barrier, 3 + tp_count)

    def own(k, way=0):
        return 0 if k == 0 else 2 + 4 * (k - 1) + (way if k < half else -2)

    def cross(k, way=0):
        if k == 0:
            return 1
        if k == half:
            return 2 * ring - 1
        return 2 + 4 * (k - 1) + (2 if k < half - 1 else 3) + way

    def piece(b, s):
        return blocks.at[pl.ds(b * rows + s * part, part)]

    def own_piece(s):
        return x_hbm.at[pl.ds(s * part, part)]

    def hop(b, s, src, req):
        return remote(src, piece(b, s), ring_send.at[b, s], ring_recv.at[b, s], req=req)

    def arrive(b, s):
        hop(b, s, own_piece(s), across).wait_recv()

    toward = (above, below)
    order = ((0, 0), (1, 1), (0, 1), (1, 0))

    for way, s in order:
        hop(own(1, way), s, own_piece(s), toward[way]).start()

    strip = side_w.shape[1] // tp_count

    def map_at(first, owner):
        return side_w.at[
            pl.ds(first, maps), pl.ds(pl.multiple_of(owner * strip, strip), strip)
        ]

    map_row = 2 * kv_cols + maps

    def map_hop():
        return remote(
            map_at(2 * kv_cols, t), map_at(map_row, t), map_send.at[t], map_recv.at[t], req=across
        )

    def map_spread(target, owner):
        return remote(
            map_at(map_row, owner),
            map_at(map_row, owner),
            map_send.at[target],
            map_recv.at[owner],
            tp=target,
        )

    for load in loads[:2]:
        load.wait()
    map_hop().start()
    for s in range(2):
        hop(cross(0), s, own_piece(s), across).start()
    for load in loads[2:]:
        load.wait()
    map_hop().wait_recv()
    for o in range(1, tp_count):
        map_spread((t + o) % tp_count, t).start()

    def q_copy(zz):
        return remote(q_out.at[zz], q_in.at[zz], q_send.at[zz], q_recv.at[zz], pp=other)

    def a_copy(zz):
        return remote(a_out.at[zz], a_in.at[zz], a_send.at[zz], a_recv.at[zz], pp=other)

    def b_copy(zz):
        return remote(b_out.at[zz], b_in.at[zz], b_send.at[zz], b_recv.at[zz], pp=other)

    def late_copy(i, d):
        return remote(
            b_out.at[ahead(half - 1)[d]],
            late_in.at[i, d],
            late_send.at[i, d],
            late_recv.at[i, d],
            req=pair,
            pp=(p, other)[i],
        )

    def project(first, places, in_own, late=False):
        count = len(places) * rows
        at = pl.ds(first * rows, count)
        side = SIDE if any(in_own) else HEAD
        got = lax.dot_general(
            blocks[at, :],
            side_w[:side],
            (((1,), (1,)), ((), ())),
            preferred_element_type=F32,
        )
        for i, (zz, mine) in enumerate(zip(places, in_own)):
            block = got[i * rows : (i + 1) * rows]
            if mine:
                a_own[zz] = block
                a_out[zz] = block.astype(BF16)
                a_copy(zz).start()
            else:
                b_own[zz] = block[:, :HEAD]
                b_out[zz] = block[:, :HEAD].astype(BF16)
                b_copy(zz).start()
                if late:
                    late_copy(0, i).start()
                    late_copy(1, i).start()

        def part_of(n, _):
            lanes = pl.ds(pl.multiple_of(n * SIDE, SIDE), SIDE)
            got = jnp.dot(blocks[at, :], weights[:, lanes], preferred_element_type=F32)
            for i, (zz, mine) in enumerate(zip(places, in_own)):
                block = got[i * rows : (i + 1) * rows]
                keep = (h == p) if mine else (h != p)

                @pl.when(keep)
                def _():
                    q_keep[zz, :, lanes] = block

                @pl.when(jnp.logical_not(keep))
                def _():
                    q_out[zz, :, lanes] = block.astype(BF16)

            return 0

        lax.fori_loop(0, cols // SIDE, part_of, 0)
        for zz, mine in zip(places, in_own):

            @pl.when((h != p) if mine else (h == p))
            def _():
                q_copy(zz).start()

    def kv_copy(hh, zz):
        return remote(
            kv_out.at[hh, zz],
            kv_in.at[hh, zz],
            kv_send.at[hh, zz],
            kv_recv.at[hh, zz],
            req=pair,
        )

    def low_copy(zz):
        return remote(
            low_out.at[zz], low_in.at[z], low_send.at[zz], low_recv.at[z], req=h * ring + zz
        )

    def low_arrival(zz):
        return remote(
            low_out.at[zz], low_in.at[zz], low_send.at[zz], low_recv.at[zz], req=h * ring + zz
        )

    near_lane = lax.broadcasted_iota(jnp.int32, (rows, HEAD), 1) < maps
    prompt_of = lax.broadcasted_iota(jnp.int32, (rows, HEAD), 0) // SLOTS
    match = jnp.zeros((rows, HEAD), F32)
    for i in range(prompts):
        adapter = adapters[t * prompts + i]
        mine = jnp.where(adapter == r, 1.0, 0.0)
        theirs = jnp.where(adapter == across, 1.0, 0.0)
        match = jnp.where(prompt_of == i, jnp.where(near_lane, mine, theirs), match)

    def finish_kv(hh, zz, total):
        kv_own[hh, zz] = total
        kv_out[hh, zz] = total.astype(BF16)
        kv_copy(hh, zz).start()

    def finish_own(zz, self_too=False):
        a_copy(zz).wait_recv()
        total = a_own[zz] + a_in[zz].astype(F32)
        finish_kv(h, zz, total[:, :HEAD])
        low = jnp.where(match > 0.0, total[:, HEAD:SIDE], 0.0)
        low = low + pltpu.roll(low, HEAD // 2, 1)
        packed = jnp.where(near_lane[:part], low[:part], low[part:]).astype(BF16)
        if self_too:
            low_in[zz] = packed
        else:
            low_out[zz] = packed
            low_copy(zz).start()

    def finish_cross(zz):
        b_copy(zz).wait_recv()
        finish_kv(1 - h, zz, b_own[zz] + b_in[zz].astype(F32))

    def ahead(k):
        return [(z + ring - k) % ring, (z + k) % ring]

    def arrive_own(k):
        for way, s in order:
            arrive(own(k, way), s)
            src = piece(own(k, way), s)
            if k < half - 1:
                hop(own(k + 1, way), s, src, toward[way]).start()
            elif s == way:
                hop(own(half), s, src, toward[way]).start()
            if k == 1:
                hop(cross(k, way), s, src, across).start()

    def arrive_cross(k):
        for way, s in order:
            arrive(cross(k, way), s)
            src = piece(cross(k, way), s)
            if k < half - 1:
                hop(cross(k + 1, way), s, src, toward[way]).start()

    def arrive_both(b):
        for s in range(2):
            arrive(b, s)

    def make_messages():
        steps = sq.shape[1]
        msg_f32[...] = jnp.zeros(msg_f32.shape, F32)
        for i in range(per_dev):
            head = t * per_dev + i
            for g in range(heads):
                lanes = pl.ds(pl.multiple_of(head * cols + g * HEAD, HEAD), HEAD)
                msg_f32[i, g * steps : (g + 1) * steps] = sq[0, :, lanes].astype(F32)
            lanes = pl.ds(pl.multiple_of((head // 2) * HEAD, HEAD), HEAD)
            for s in range(steps):
                new = skv[0, s, :, lanes].astype(F32)
                first = heads * steps + s
                msg_f32[i, first : first + 1] = new[0:1]
                msg_f32[i, first + SLOTS : first + SLOTS + 1] = new[1:2]
        msg_ref[...] = msg_f32[...].astype(BF16)

    both = [True, True]
    neither = [False, False]

    arrive_own(1)
    arrive_both(cross(0))
    if half > 2:
        arrive_own(2)
    for o in range(1, tp_count):
        map_spread(t, (t + o) % tp_count).wait_recv()
    project(0, [z, z], [True, False])
    if half > 2:
        project(own(1), ahead(1), both)
    make_messages()
    for k in range(3, half):
        arrive_own(k)
        arrive_cross(k - 2)
        if k == 3:
            finish_own(z, True)
            finish_cross(z)
        project(own(k - 1), ahead(k - 1), both)
        project(cross(k - 2), ahead(k - 2), neither)
        for zz in ahead(k - 2):
            finish_own(zz)
    for i in range(prompts):
        uv_out[i] = uv[adapters[t * prompts + i]]
    uv_copy = remote(uv_out, uv_in, uv_sems.at[0], uv_sems.at[1], req=pair)
    uv_copy.start()
    for s in range(2):
        arrive(own(half), s)
        hop(cross(half), s, piece(own(half), s), across).start()
    project(own(half - 1), ahead(half - 1) + [far], [True] * 3)
    if half > 2:
        arrive_cross(half - 2)
        for zz in ahead(half - 2):
            finish_own(zz)
        for zz in ahead(half - 1) + [far]:
            finish_own(zz)
        project(cross(half - 2), ahead(half - 2), neither)
        if half > 3:
            for zz in ahead(half - 3):
                finish_cross(zz)
        else:
            finish_own(z, True)
            finish_cross(z)
    else:
        finish_own(z, True)
        finish_cross(z)
        for zz in ahead(half - 1) + [far]:
            finish_own(zz)
    arrive_both(cross(half))
    project(cross(half), [far], [False])

    distances = sorted(range(ring), key=lambda o: -min(o, ring - o))

    def others(body):
        for o in distances:
            body((1 - h) * ring + (z + o) % ring)
            if o > 0:
                body(h * ring + (z + o) % ring)

    def column(body):
        for o in distances[:-1]:
            body((z + o) % ring)

    def rank_copy(target, slot):
        return remote(
            rank_all.at[slot], rank_all.at[slot], rank_send.at[target], rank_recv.at[slot], req=target
        )

    column(lambda zz: low_arrival(zz).wait_recv())
    low = low_in[0].astype(F32)
    for zz in range(1, ring):
        low = low + low_in[zz].astype(F32)
    rank_all[r] = low.astype(BF16)
    others(lambda target: rank_copy(target, r).start())

    if half > 2:
        for zz in ahead(half - 2):
            finish_cross(zz)
    arrive_cross(half - 1)
    project(cross(half - 1), ahead(half - 1), neither, late=True)

    def step_copy(i):
        target = t * per_dev + i
        return remote(
            msg_ref.at[i],
            step_in.at[r % per_dev],
            step_send.at[i],
            step_got.at[r % per_dev],
            req=target,
            tp=r // per_dev,
        )

    def step_self(i):
        return (t * per_dev + i == r) & (r // per_dev == t)

    for i in range(per_dev):

        @pl.when(step_self(i))
        def _():
            step_in[r % per_dev] = msg_ref[i]

        @pl.when(jnp.logical_not(step_self(i)))
        def _():
            step_copy(i).start()

    finish_cross(far)
    for zz in ahead(half - 1):
        b_copy(zz).wait_recv()
        kv_own[1 - h, zz] = b_own[zz] + b_in[zz].astype(F32)
    for i in range(2):
        for d in range(2):
            late_copy(i, d).wait_recv()
    uv_copy.wait_recv()
    for hh in range(2):
        for zz in range(ring):
            there = [(hh == 1 - h) & (zz == late_zz) for late_zz in pair_late]

            @pl.when(jnp.logical_not(there[0] | there[1]))
            def _():
                kv_copy(hh, zz).wait_recv()
                kv_oth[hh, zz] = kv_in[hh, zz].astype(F32)

    for d in range(2):
        kv_oth[1 - h, pair_late[d]] = late_in[0, d].astype(F32) + late_in[1, d].astype(F32)

    others(lambda source: rank_copy(source, source).wait_recv())
    for source in range(req_count):
        packed = rank_all[source].astype(F32)
        ranks[source, :part] = packed
        ranks[source, part:] = pltpu.roll(packed, HEAD // 2, 1)

    even = r % 2 == 0
    slots = req_count * SLOTS
    share = slots // 2
    low_lane = lax.broadcasted_iota(jnp.int32, (slots, HEAD), 1) < HEAD // 2
    scale = HEAD ** (-0.5)

    def assemble(n):
        at = pl.ds(pl.multiple_of(n * SLOTS, SLOTS), SLOTS)
        mine = kv_own[:, :, at, :].reshape(slots, HEAD)
        theirs = kv_oth[:, :, at, :].reshape(slots, HEAD)
        first = jnp.where(even, mine, theirs)
        second = jnp.where(even, theirs, mine)
        k = jnp.where(low_lane, first, pltpu.roll(second, HEAD // 2, 1)).astype(BF16)
        v = jnp.where(low_lane, pltpu.roll(first, HEAD // 2, 1), second)
        uv_mine, uv_theirs = uv_out[n], uv_in[n]
        up_v = jnp.concatenate(
            [jnp.where(even, uv_mine, uv_theirs), jnp.where(even, uv_theirs, uv_mine)], axis=1
        )
        rank_rows = ranks[:, at, :].reshape(slots, HEAD).astype(BF16)
        v = v + jnp.dot(rank_rows[:, rank:maps], up_v, preferred_element_type=F32)
        k_full[n] = k
        v_full[n] = v.astype(BF16)

    steps = step_out.shape[1] // heads
    qrows = heads * steps

    def step_arrival(j):
        source_req = t * per_dev + j
        return remote(
            msg_ref.at[0],
            step_in.at[j],
            step_send.at[0],
            step_got.at[j],
            req=source_req,
            tp=r // per_dev,
        )

    def out_copy(j, target):
        return remote(
            step_out.at[j],
            step_recv.at[r],
            out_send.at[j, target],
            out_got.at[r],
            req=t * per_dev + j,
            tp=target,
        )

    def out_arrival(source):
        return remote(
            step_out.at[0],
            step_recv.at[source],
            out_send.at[0, 0],
            out_got.at[source],
            req=source,
            tp=r // per_dev,
        )

    for j in range(per_dev):

        @pl.when(jnp.logical_not((t * per_dev + j == r) & (r // per_dev == t)))
        def _():
            step_arrival(j).wait_recv()

        n = 2 * j + p
        assemble(n)
        length = lens[t * prompts + n]
        k, v = k_full[n], v_full[n]
        got = step_in[j]
        qs = got[:qrows]
        tail = got[qrows:].astype(F32)
        new_k = tail[:SLOTS].astype(BF16)
        new_v = tail[SLOTS : 2 * SLOTS].astype(BF16)
        s_old = lax.dot_general(qs, k, (((1,), (1,)), ((), ())), preferred_element_type=F32) * scale
        s_new = (
            lax.dot_general(qs, new_k, (((1,), (1,)), ((), ())), preferred_element_type=F32) * scale
        )
        s_old = jnp.where(lax.broadcasted_iota(jnp.int32, (qrows, slots), 1) < length, s_old, NEG)
        at_step = lax.broadcasted_iota(jnp.int32, (qrows, SLOTS), 0) % steps
        at_new = lax.broadcasted_iota(jnp.int32, (qrows, SLOTS), 1)
        s_new = jnp.where(at_new <= at_step, s_new, NEG)
        top = jnp.maximum(
            jnp.max(s_old, axis=1, keepdims=True), jnp.max(s_new, axis=1, keepdims=True)
        )
        e_old, e_new = jnp.exp(s_old - top), jnp.exp(s_new - top)
        total = jnp.sum(e_old, axis=1, keepdims=True) + jnp.sum(e_new, axis=1, keepdims=True)
        mixed = jnp.zeros((qrows, HEAD), F32)
        for e, values in ((e_old, v), (e_new, new_v)):
            coarse = e.astype(BF16)
            fine = (e - coarse.astype(F32)).astype(BF16)
            mixed = mixed + jnp.dot(coarse, values, preferred_element_type=F32)
            mixed = mixed + jnp.dot(fine, values, preferred_element_type=F32)
        step_out[j] = (mixed / total).astype(BF16)
        for o in sorted(range(tp_count), key=lambda o: -min(o, tp_count - o)):
            target = (t + o) % tp_count
            if o == 0:

                @pl.when(t * per_dev + j == r)
                def _():
                    step_recv[r] = step_out[j]

                @pl.when(t * per_dev + j != r)
                def _():
                    out_copy(j, t).start()
            else:
                out_copy(j, target).start()

    for j in range(per_dev):
        assemble(2 * j + 1 - p)
    for zz in range(ring):
        q_copy(zz).wait_recv()
    base_q = (q_keep[...] + q_in[...].astype(F32)).reshape(ring, prompts, SLOTS, cols)
    my_ranks = ranks[pl.ds(p * ring, ring)].reshape(ring, prompts, SLOTS, HEAD)
    row_pos = lax.broadcasted_iota(jnp.int32, (heads * share, slots), 0) % share + p * share
    col_pos = lax.broadcasted_iota(jnp.int32, (heads * share, slots), 1)
    out_pos = lax.broadcasted_iota(jnp.int32, (heads * share, HEAD), 0) % share + p * share
    for i in range(prompts):
        length = lens[t * prompts + i]
        adapter = adapters[t * prompts + i]
        k, v = k_full[i], v_full[i]
        rank_q = my_ranks[:, i].reshape(share, HEAD).astype(BF16)[:, :rank]
        q = base_q[:, i].reshape(share, cols) + jnp.dot(
            rank_q, uq[adapter], preferred_element_type=F32
        )
        q = q.astype(BF16)
        q = jnp.concatenate([q[:, g * HEAD : (g + 1) * HEAD] for g in range(heads)], axis=0)
        s = lax.dot_general(q, k, (((1,), (1,)), ((), ())), preferred_element_type=F32) * scale
        s = jnp.where((col_pos <= row_pos) & (col_pos < length), s, NEG)
        e = jnp.exp(s - jnp.max(s, axis=1, keepdims=True))
        w = (e / jnp.sum(e, axis=1, keepdims=True)).astype(BF16)
        o = jnp.dot(w, v, preferred_element_type=F32)
        o = jnp.where(out_pos < length, o, 0.0).astype(BF16)
        for g in range(heads):
            prefill_ref[i, :, g * HEAD : (g + 1) * HEAD] = o[g * share : (g + 1) * share]

    for b in range(1, 2 * ring):
        for s in range(2):
            hop(b, s, own_piece(s), above).wait_send()
    for target in range(tp_count):
        map_spread(target, t).wait_send()
    for zz in range(ring):
        q_copy(zz).wait_send()
        a_copy(zz).wait_send()
        b_copy(zz).wait_send()
        for hh in range(2):

            mine = [(hh == 1 - h) & (zz == late_zz) for late_zz in ahead(half - 1)]

            @pl.when(jnp.logical_not(mine[0] | mine[1]))
            def _():
                kv_copy(hh, zz).wait_send()

    for i in range(2):
        for d in range(2):
            late_copy(i, d).wait_send()
    column(lambda zz: low_copy(zz).wait_send())
    others(lambda target: rank_copy(target, r).wait_send())
    uv_copy.wait_send()
    for i in range(per_dev):

        @pl.when(jnp.logical_not(step_self(i)))
        def _():
            step_copy(i).wait_send()

    for j in range(per_dev):
        for target in range(tp_count):

            @pl.when(jnp.logical_not((t * per_dev + j == r) & (target == t)))
            def _():
                out_copy(j, target).wait_send()

    def got_out(source, _):
        @pl.when(jnp.logical_not((source == r) & (r // per_dev == t)))
        def _():
            out_arrival(source).wait_recv()

        return 0

    lax.fori_loop(0, req_count, got_out, 0)
    decoded_ref[...] = step_recv[...]


def deliver(prefill_in, decoded_in, prefill_ref, decoded_ref):
    prefill_ref[...] = prefill_in[...]
    steps = decoded_ref.shape[1]
    heads = decoded_in.shape[1] // steps
    for source in range(decoded_in.shape[0]):
        got = decoded_in[source].astype(F32)
        for g in range(heads):
            lanes = pl.ds((source * heads + g) * HEAD, HEAD)
            decoded_ref[0, :, lanes] = got[g * steps : (g + 1) * steps].astype(BF16)


def local(
    prompt_states,
    prompt_lengths,
    adapter_ids,
    w_query,
    w_key,
    value_weight,
    down_query,
    up_query,
    down_value,
    value_up_weight,
    step_queries,
    step_keyvals,
):
    req_count, tp_count = lax.axis_size("req"), lax.axis_size("tp")
    prompts, slots, width = prompt_states.shape
    rows = prompts * slots
    cols = w_query.shape[1]
    kv_cols = w_key.shape[1]
    rank = down_query.shape[2]
    adapter_count = up_query.shape[0]
    ring = req_count // 2
    heads = cols // HEAD
    steps = step_queries.shape[1]
    per_dev = req_count // tp_count
    total_slots = req_count * slots

    vmem = pl.BlockSpec(memory_space=pltpu.VMEM)
    smem = pl.BlockSpec(memory_space=pltpu.SMEM)
    hbm = pl.BlockSpec(memory_space=pl.ANY)
    dma = pltpu.SemaphoreType.DMA
    prefill, decoded = pl.pallas_call(
        functools.partial(kernel, req_count, tp_count),
        out_shape=(
            jax.ShapeDtypeStruct((prompts, total_slots // 2, cols), BF16),
            jax.ShapeDtypeStruct((req_count, heads * steps, HEAD), BF16),
        ),
        in_specs=[smem, smem] + [hbm] * 10,
        out_specs=(vmem, vmem),
        scratch_shapes=[
            pltpu.VMEM((per_dev, heads * steps + 2 * SLOTS, HEAD), BF16),
            pltpu.VMEM((per_dev, heads * steps + 2 * SLOTS, HEAD), F32),
            pltpu.VMEM(step_queries.shape, BF16),
            pltpu.VMEM(step_keyvals.shape, BF16),
            pltpu.VMEM((req_count * rows, width), BF16),
            pltpu.VMEM((width, cols), BF16),
            pltpu.VMEM((SIDE, width), BF16),
            pltpu.VMEM((adapter_count, rank, cols), BF16),
            pltpu.VMEM((adapter_count, rank, kv_cols), BF16),
            pltpu.VMEM((ring, rows, cols), F32),
            pltpu.VMEM((ring, rows, cols), BF16),
            pltpu.VMEM((ring, rows, cols), BF16),
            pltpu.VMEM((ring, rows, SIDE), F32),
            pltpu.VMEM((ring, rows, SIDE), BF16),
            pltpu.VMEM((ring, rows, SIDE), BF16),
            pltpu.VMEM((ring, rows, HEAD), F32),
            pltpu.VMEM((ring, rows, HEAD), BF16),
            pltpu.VMEM((ring, rows, HEAD), BF16),
            pltpu.VMEM((2, ring, rows, HEAD), F32),
            pltpu.VMEM((2, ring, rows, HEAD), F32),
            pltpu.VMEM((2, ring, rows, HEAD), BF16),
            pltpu.VMEM((2, ring, rows, HEAD), BF16),
            pltpu.VMEM((2, 2, rows, HEAD), BF16),
            pltpu.VMEM((ring, rows // 2, HEAD), BF16),
            pltpu.VMEM((ring, rows // 2, HEAD), BF16),
            pltpu.VMEM((req_count, rows // 2, HEAD), BF16),
            pltpu.VMEM((req_count, rows, HEAD), F32),
            pltpu.VMEM((prompts, rank, kv_cols), BF16),
            pltpu.VMEM((prompts, rank, kv_cols), BF16),
            pltpu.VMEM((prompts, total_slots, HEAD), BF16),
            pltpu.VMEM((prompts, total_slots, HEAD), BF16),
            pltpu.VMEM((per_dev, heads * steps + 2 * SLOTS, HEAD), BF16),
            pltpu.VMEM((per_dev, heads * steps, HEAD), BF16),
            pltpu.VMEM((req_count, heads * steps, HEAD), BF16),
            dma((10,)),
            dma((req_count, 2)),
            dma((req_count, 2)),
            dma((tp_count,)),
            dma((tp_count,)),
            dma((ring,)),
            dma((ring,)),
            dma((ring,)),
            dma((ring,)),
            dma((ring,)),
            dma((ring,)),
            dma((2, ring)),
            dma((2, ring)),
            dma((2, 2)),
            dma((2, 2)),
            dma((ring,)),
            dma((ring,)),
            dma((req_count,)),
            dma((req_count,)),
            dma((2,)),
            dma((per_dev,)),
            dma((per_dev,)),
            dma((per_dev, tp_count)),
            dma((req_count,)),
        ],
        compiler_params=pltpu.CompilerParams(
            collective_id=0, has_side_effects=True, vmem_limit_bytes=56 * 1024 * 1024
        ),
        cost_estimate=pl.CostEstimate(
            flops=2 * req_count * rows * width * (cols + SIDE),
            bytes_accessed=2 * width * (cols + SIDE),
            transcendentals=0,
        ),
    )(
        prompt_lengths,
        adapter_ids,
        prompt_states.reshape(rows, width),
        w_query,
        w_key.T,
        value_weight.T,
        down_query[0].T,
        down_value[0].T,
        up_query,
        value_up_weight,
        step_queries,
        step_keyvals,
    )
    return pl.pallas_call(
        deliver,
        out_shape=(
            jax.ShapeDtypeStruct(prefill.shape, BF16),
            jax.ShapeDtypeStruct(step_queries.shape, BF16),
        ),
        in_specs=[vmem, vmem],
        out_specs=(vmem, vmem),
    )(prefill, decoded)


def solution(mesh):
    in_specs = (
        P("tp", "req", "pp"),
        P(),
        P(),
        P("pp", "req"),
        P("pp", "req"),
        P("pp", "req"),
        P("req", "pp", None),
        P(None, None, "req"),
        P("req", "pp", None),
        P(None, None, "req"),
        P(("req", "pp"), None, None),
        P(("req", "pp"), None, None, None),
    )
    out_specs = (P("tp", "pp", "req"), P(("req", "pp"), None, None))
    return jax.shard_map(local, mesh=mesh, in_specs=in_specs, out_specs=out_specs, check_vma=False)
```

```python
import functools

import jax
import jax.numpy as jnp
from jax import lax
from jax.experimental import pallas as pl
from jax.experimental.pallas import tpu as pltpu
from jax.sharding import PartitionSpec as P

HEAD = 128
SLOTS = 8
SIDE = 256
NEG = -1e30
F32 = jnp.float32
BF16 = jnp.bfloat16
MESH = pl.DeviceIdType.MESH


def kernel(
    req_count,
    tp_count,
    lens,
    adapters,
    x_hbm,
    wq_hbm,
    wk_hbm,
    wv_hbm,
    dq_hbm,
    dv_hbm,
    uq_hbm,
    uv_hbm,
    sq_hbm,
    skv_hbm,
    prefill_ref,
    decoded_ref,
    msg_ref,
    msg_f32,
    sq,
    skv,
    blocks,
    weights,
    side_w,
    uq,
    uv,
    q_keep,
    q_out,
    q_in,
    a_own,
    a_out,
    a_in,
    b_own,
    b_out,
    b_in,
    kv_own,
    kv_oth,
    kv_out,
    kv_in,
    late_in,
    low_out,
    low_in,
    rank_all,
    ranks,
    uv_out,
    uv_in,
    k_full,
    v_full,
    step_in,
    step_out,
    step_recv,
    load_sem,
    ring_send,
    ring_recv,
    map_send,
    map_recv,
    q_send,
    q_recv,
    a_send,
    a_recv,
    b_send,
    b_recv,
    kv_send,
    kv_recv,
    late_send,
    late_recv,
    low_send,
    low_recv,
    rank_send,
    rank_recv,
    uv_sems,
    step_send,
    step_got,
    out_send,
    out_got,
    hello,
):
    r, t, p = lax.axis_index("req"), lax.axis_index("tp"), lax.axis_index("pp")
    ring = req_count // 2
    half = ring // 2
    h, z = r // ring, r % ring
    rows = x_hbm.shape[0]
    part = rows // 2
    prompts = rows // SLOTS
    cols = q_keep.shape[2]
    heads = cols // HEAD
    per_dev = req_count // tp_count
    kv_cols, rank = wk_hbm.shape[0], dq_hbm.shape[0]
    maps = 2 * rank
    above = h * ring + (z + 1) % ring
    below = h * ring + (z + ring - 1) % ring
    across = (1 - h) * ring + z
    other = 1 - p
    pair = r + 1 - 2 * (r % 2)
    far = (z + half) % ring
    pair_late = [(pair + ring - half + 1) % ring, (pair + half - 1) % ring]

    def remote(src, dst, send, recv, req=None, tp=None, pp=None):
        where = (r if req is None else req, t if tp is None else tp, p if pp is None else pp)
        return pltpu.make_async_remote_copy(
            src_ref=src,
            dst_ref=dst,
            send_sem=send,
            recv_sem=recv,
            device_id=where,
            device_id_type=MESH,
        )

    loads = [
        pltpu.make_async_copy(src, dst, load_sem.at[i])
        for i, (src, dst) in enumerate(
            [
                (dq_hbm, side_w.at[pl.ds(2 * kv_cols, rank)]),
                (dv_hbm, side_w.at[pl.ds(2 * kv_cols + rank, rank)]),
                (wk_hbm, side_w.at[pl.ds(0, kv_cols)]),
                (wv_hbm, side_w.at[pl.ds(kv_cols, kv_cols)]),
                (x_hbm, blocks.at[pl.ds(0, rows)]),
                (wq_hbm, weights),
                (uq_hbm, uq),
                (uv_hbm, uv),
                (sq_hbm, sq),
                (skv_hbm, skv),
            ]
        )
    ]
    for load in loads:
        load.start()

    barrier = pltpu.get_barrier_semaphore()
    for where in ((above, t, p), (below, t, p), (across, t, p), (r, t, other)):
        pl.semaphore_signal(barrier, inc=1, device_id=where, device_id_type=MESH)
    for o in range(1, tp_count):
        pl.semaphore_signal(
            barrier, inc=1, device_id=(r, (t + o) % tp_count, p), device_id_type=MESH
        )
    pl.semaphore_wait(barrier, 3 + tp_count)

    def own(k, way=0):
        return 0 if k == 0 else 2 + 4 * (k - 1) + (way if k < half else -2)

    def cross(k, way=0):
        if k == 0:
            return 1
        if k == half:
            return 2 * ring - 1
        return 2 + 4 * (k - 1) + (2 if k < half - 1 else 3) + way

    def piece(b, s):
        return blocks.at[pl.ds(b * rows + s * part, part)]

    def own_piece(s):
        return x_hbm.at[pl.ds(s * part, part)]

    def hop(b, s, src, req):
        return remote(src, piece(b, s), ring_send.at[b, s], ring_recv.at[b, s], req=req)

    def arrive(b, s):
        hop(b, s, own_piece(s), across).wait_recv()

    toward = (above, below)
    order = ((0, 0), (1, 1), (0, 1), (1, 0))

    for way, s in order:
        hop(own(1, way), s, own_piece(s), toward[way]).start()

    strip = side_w.shape[1] // tp_count

    def map_at(first, owner):
        return side_w.at[
            pl.ds(first, maps), pl.ds(pl.multiple_of(owner * strip, strip), strip)
        ]

    map_row = 2 * kv_cols + maps

    def map_hop():
        return remote(
            map_at(2 * kv_cols, t), map_at(map_row, t), map_send.at[t], map_recv.at[t], req=across
        )

    def map_spread(target, owner):
        return remote(
            map_at(map_row, owner),
            map_at(map_row, owner),
            map_send.at[target],
            map_recv.at[owner],
            tp=target,
        )

    for load in loads[:2]:
        load.wait()
    map_hop().start()
    for s in range(2):
        hop(cross(0), s, own_piece(s), across).start()
    for load in loads[2:]:
        load.wait()
    def make_messages():
        steps = sq.shape[1]
        msg_f32[...] = jnp.zeros(msg_f32.shape, F32)
        for i in range(per_dev):
            head = t * per_dev + i
            for g in range(heads):
                lanes = pl.ds(pl.multiple_of(head * cols + g * HEAD, HEAD), HEAD)
                msg_f32[i, g * steps : (g + 1) * steps] = sq[0, :, lanes].astype(F32)
            lanes = pl.ds(pl.multiple_of((head // 2) * HEAD, HEAD), HEAD)
            for s in range(steps):
                new = skv[0, s, :, lanes].astype(F32)
                first = heads * steps + s
                msg_f32[i, first : first + 1] = new[0:1]
                msg_f32[i, first + SLOTS : first + SLOTS + 1] = new[1:2]
        msg_ref[...] = msg_f32[...].astype(BF16)

    for i in range(prompts):
        uv_out[i] = uv[adapters[t * prompts + i]]
    uv_copy = remote(uv_out, uv_in, uv_sems.at[0], uv_sems.at[1], req=pair)
    uv_copy.start()
    make_messages()

    map_hop().wait_recv()
    for o in range(1, tp_count):
        map_spread((t + o) % tp_count, t).start()

    def q_copy(zz):
        return remote(q_out.at[zz], q_in.at[zz], q_send.at[zz], q_recv.at[zz], pp=other)

    def a_copy(zz):
        return remote(a_out.at[zz], a_in.at[zz], a_send.at[zz], a_recv.at[zz], pp=other)

    def b_copy(zz):
        return remote(b_out.at[zz], b_in.at[zz], b_send.at[zz], b_recv.at[zz], pp=other)

    def late_copy(i, d):
        return remote(
            b_out.at[ahead(half - 1)[d]],
            late_in.at[i, d],
            late_send.at[i, d],
            late_recv.at[i, d],
            req=pair,
            pp=(p, other)[i],
        )

    def project(first, places, in_own, late=False):
        count = len(places) * rows
        at = pl.ds(first * rows, count)
        side = SIDE if any(in_own) else HEAD
        got = lax.dot_general(
            blocks[at, :],
            side_w[:side],
            (((1,), (1,)), ((), ())),
            preferred_element_type=F32,
        )
        for i, (zz, mine) in enumerate(zip(places, in_own)):
            block = got[i * rows : (i + 1) * rows]
            if mine:
                a_own[zz] = block
                a_out[zz] = block.astype(BF16)
                a_copy(zz).start()
            else:
                b_own[zz] = block[:, :HEAD]
                b_out[zz] = block[:, :HEAD].astype(BF16)
                b_copy(zz).start()
                if late:
                    late_copy(0, i).start()
                    late_copy(1, i).start()

        def part_of(n, _):
            lanes = pl.ds(pl.multiple_of(n * SIDE, SIDE), SIDE)
            got = jnp.dot(blocks[at, :], weights[:, lanes], preferred_element_type=F32)
            for i, (zz, mine) in enumerate(zip(places, in_own)):
                block = got[i * rows : (i + 1) * rows]
                keep = (h == p) if mine else (h != p)

                @pl.when(keep)
                def _():
                    q_keep[zz, :, lanes] = block

                @pl.when(jnp.logical_not(keep))
                def _():
                    q_out[zz, :, lanes] = block.astype(BF16)

            return 0

        lax.fori_loop(0, cols // SIDE, part_of, 0)
        for zz, mine in zip(places, in_own):

            @pl.when((h != p) if mine else (h == p))
            def _():
                q_copy(zz).start()

    def kv_copy(hh, zz):
        return remote(
            kv_out.at[hh, zz],
            kv_in.at[hh, zz],
            kv_send.at[hh, zz],
            kv_recv.at[hh, zz],
            req=pair,
        )

    def low_copy(zz):
        return remote(
            low_out.at[zz], low_in.at[z], low_send.at[zz], low_recv.at[z], req=h * ring + zz
        )

    def low_arrival(zz):
        return remote(
            low_out.at[zz], low_in.at[zz], low_send.at[zz], low_recv.at[zz], req=h * ring + zz
        )

    near_lane = lax.broadcasted_iota(jnp.int32, (rows, HEAD), 1) < maps
    prompt_of = lax.broadcasted_iota(jnp.int32, (rows, HEAD), 0) // SLOTS
    match = jnp.zeros((rows, HEAD), F32)
    for i in range(prompts):
        adapter = adapters[t * prompts + i]
        mine = jnp.where(adapter == r, 1.0, 0.0)
        theirs = jnp.where(adapter == across, 1.0, 0.0)
        match = jnp.where(prompt_of == i, jnp.where(near_lane, mine, theirs), match)

    def finish_kv(hh, zz, total):
        kv_own[hh, zz] = total
        kv_out[hh, zz] = total.astype(BF16)
        kv_copy(hh, zz).start()

    def finish_own(zz, self_too=False):
        a_copy(zz).wait_recv()
        total = a_own[zz] + a_in[zz].astype(F32)
        finish_kv(h, zz, total[:, :HEAD])
        low = jnp.where(match > 0.0, total[:, HEAD:SIDE], 0.0)
        low = low + pltpu.roll(low, HEAD // 2, 1)
        packed = jnp.where(near_lane[:part], low[:part], low[part:]).astype(BF16)
        if self_too:
            low_in[zz] = packed
        else:
            low_out[zz] = packed
            low_copy(zz).start()

    def finish_cross(zz):
        b_copy(zz).wait_recv()
        finish_kv(1 - h, zz, b_own[zz] + b_in[zz].astype(F32))

    def ahead(k):
        return [(z + ring - k) % ring, (z + k) % ring]

    def arrive_own(k):
        for way, s in order:
            arrive(own(k, way), s)
            src = piece(own(k, way), s)
            if k < half - 1:
                hop(own(k + 1, way), s, src, toward[way]).start()
            elif s == way:
                hop(own(half), s, src, toward[way]).start()
            if k == 1:
                hop(cross(k, way), s, src, across).start()

    def arrive_cross(k, which=order):
        for way, s in which:
            arrive(cross(k, way), s)
            src = piece(cross(k, way), s)
            if k < half - 1:
                hop(cross(k + 1, way), s, src, toward[way]).start()

    def arrive_both(b):
        for s in range(2):
            arrive(b, s)

    def step_copy(i):
        target = t * per_dev + i
        return remote(
            msg_ref.at[i],
            step_in.at[r % per_dev],
            step_send.at[i],
            step_got.at[r % per_dev],
            req=target,
            tp=r // per_dev,
        )

    def step_self(i):
        return (t * per_dev + i == r) & (r // per_dev == t)

    both = [True, True]
    neither = [False, False]

    arrive_own(1)
    arrive_both(cross(0))
    if half > 2:
        arrive_own(2)
    for o in range(1, tp_count):
        map_spread(t, (t + o) % tp_count).wait_recv()
    project(0, [z, z], [True, False])
    if half > 2:
        project(own(1), ahead(1), both)
    for k in range(3, half):
        arrive_own(k)
        arrive_cross(k - 2)
        project(own(k - 1), ahead(k - 1), both)
        if k < half - 1:
            project(cross(k - 2), ahead(k - 2), neither)
    for s in range(2):
        arrive(own(half), s)
        hop(cross(half), s, piece(own(half), s), across).start()
    pl.semaphore_signal(hello, inc=1, device_id=(across, t, p), device_id_type=MESH)
    project(own(half - 1), ahead(half - 1) + [far], [True] * 3)
    pl.semaphore_wait(hello, 1)
    for i in range(per_dev):

        @pl.when(step_self(i))
        def _():
            step_in[r % per_dev] = msg_ref[i]

        @pl.when(jnp.logical_not(step_self(i)))
        def _():
            step_copy(i).start()

    if half > 3:
        project(cross(half - 3), ahead(half - 3), neither)
    finish_own(z, True)
    finish_cross(z)
    for k in range(1, half - 1):
        for zz in ahead(k):
            finish_own(zz)
    if half > 2:
        arrive_cross(half - 2, order[:2])
    for zz in ahead(half - 1) + [far]:
        finish_own(zz)
    if half > 2:
        arrive_cross(half - 2, order[2:])
        project(cross(half - 2), ahead(half - 2), neither)
    for k in range(1, half - 2):
        for zz in ahead(k):
            finish_cross(zz)
    arrive_both(cross(half))
    project(cross(half), [far], [False])

    distances = sorted(range(ring), key=lambda o: -min(o, ring - o))

    def others(body):
        for o in distances:
            body((1 - h) * ring + (z + o) % ring)
            if o > 0:
                body(h * ring + (z + o) % ring)

    def column(body):
        for o in distances[:-1]:
            body((z + o) % ring)

    def rank_copy(target, slot):
        return remote(
            rank_all.at[slot], rank_all.at[slot], rank_send.at[target], rank_recv.at[slot], req=target
        )

    column(lambda zz: low_arrival(zz).wait_recv())
    low = low_in[0].astype(F32)
    for zz in range(1, ring):
        low = low + low_in[zz].astype(F32)
    rank_all[r] = low.astype(BF16)
    others(lambda target: rank_copy(target, r).start())

    if half > 2:
        for zz in ahead(half - 2):
            finish_cross(zz)
    arrive_cross(half - 1)
    project(cross(half - 1), ahead(half - 1), neither, late=True)

    finish_cross(far)
    for zz in ahead(half - 1):
        b_copy(zz).wait_recv()
        kv_own[1 - h, zz] = b_own[zz] + b_in[zz].astype(F32)
    for i in range(2):
        for d in range(2):
            late_copy(i, d).wait_recv()
    uv_copy.wait_recv()
    for hh in range(2):
        for zz in range(ring):
            there = [(hh == 1 - h) & (zz == late_zz) for late_zz in pair_late]

            @pl.when(jnp.logical_not(there[0] | there[1]))
            def _():
                kv_copy(hh, zz).wait_recv()
                kv_oth[hh, zz] = kv_in[hh, zz].astype(F32)

    for d in range(2):
        kv_oth[1 - h, pair_late[d]] = late_in[0, d].astype(F32) + late_in[1, d].astype(F32)

    others(lambda source: rank_copy(source, source).wait_recv())
    for source in range(req_count):
        packed = rank_all[source].astype(F32)
        ranks[source, :part] = packed
        ranks[source, part:] = pltpu.roll(packed, HEAD // 2, 1)

    even = r % 2 == 0
    slots = req_count * SLOTS
    share = slots // 2
    low_lane = lax.broadcasted_iota(jnp.int32, (slots, HEAD), 1) < HEAD // 2
    scale = HEAD ** (-0.5)

    def assemble(n):
        at = pl.ds(pl.multiple_of(n * SLOTS, SLOTS), SLOTS)
        mine = kv_own[:, :, at, :].reshape(slots, HEAD)
        theirs = kv_oth[:, :, at, :].reshape(slots, HEAD)
        first = jnp.where(even, mine, theirs)
        second = jnp.where(even, theirs, mine)
        k = jnp.where(low_lane, first, pltpu.roll(second, HEAD // 2, 1)).astype(BF16)
        v = jnp.where(low_lane, pltpu.roll(first, HEAD // 2, 1), second)
        uv_mine, uv_theirs = uv_out[n], uv_in[n]
        up_v = jnp.concatenate(
            [jnp.where(even, uv_mine, uv_theirs), jnp.where(even, uv_theirs, uv_mine)], axis=1
        )
        rank_rows = ranks[:, at, :].reshape(slots, HEAD).astype(BF16)
        v = v + jnp.dot(rank_rows[:, rank:maps], up_v, preferred_element_type=F32)
        k_full[n] = k
        v_full[n] = v.astype(BF16)

    steps = step_out.shape[1] // heads
    qrows = heads * steps

    def step_arrival(j):
        source_req = t * per_dev + j
        return remote(
            msg_ref.at[0],
            step_in.at[j],
            step_send.at[0],
            step_got.at[j],
            req=source_req,
            tp=r // per_dev,
        )

    def out_copy(j, target):
        return remote(
            step_out.at[j],
            step_recv.at[r],
            out_send.at[j, target],
            out_got.at[r],
            req=t * per_dev + j,
            tp=target,
        )

    def out_arrival(source):
        return remote(
            step_out.at[0],
            step_recv.at[source],
            out_send.at[0, 0],
            out_got.at[source],
            req=source,
            tp=r // per_dev,
        )

    for j in range(per_dev):

        @pl.when(jnp.logical_not((t * per_dev + j == r) & (r // per_dev == t)))
        def _():
            step_arrival(j).wait_recv()

        n = 2 * j + p
        assemble(n)
        length = lens[t * prompts + n]
        k, v = k_full[n], v_full[n]
        got = step_in[j]
        qs = got[:qrows]
        tail = got[qrows:].astype(F32)
        new_k = tail[:SLOTS].astype(BF16)
        new_v = tail[SLOTS : 2 * SLOTS].astype(BF16)
        s_old = lax.dot_general(qs, k, (((1,), (1,)), ((), ())), preferred_element_type=F32) * scale
        s_new = (
            lax.dot_general(qs, new_k, (((1,), (1,)), ((), ())), preferred_element_type=F32) * scale
        )
        s_old = jnp.where(lax.broadcasted_iota(jnp.int32, (qrows, slots), 1) < length, s_old, NEG)
        at_step = lax.broadcasted_iota(jnp.int32, (qrows, SLOTS), 0) % steps
        at_new = lax.broadcasted_iota(jnp.int32, (qrows, SLOTS), 1)
        s_new = jnp.where(at_new <= at_step, s_new, NEG)
        top = jnp.maximum(
            jnp.max(s_old, axis=1, keepdims=True), jnp.max(s_new, axis=1, keepdims=True)
        )
        e_old, e_new = jnp.exp(s_old - top), jnp.exp(s_new - top)
        total = jnp.sum(e_old, axis=1, keepdims=True) + jnp.sum(e_new, axis=1, keepdims=True)
        mixed = jnp.zeros((qrows, HEAD), F32)
        for e, values in ((e_old, v), (e_new, new_v)):
            coarse = e.astype(BF16)
            fine = (e - coarse.astype(F32)).astype(BF16)
            mixed = mixed + jnp.dot(coarse, values, preferred_element_type=F32)
            mixed = mixed + jnp.dot(fine, values, preferred_element_type=F32)
        step_out[j] = (mixed / total).astype(BF16)
        for o in sorted(range(tp_count), key=lambda o: -min(o, tp_count - o)):
            target = (t + o) % tp_count
            if o == 0:

                @pl.when(t * per_dev + j == r)
                def _():
                    step_recv[r] = step_out[j]

                @pl.when(t * per_dev + j != r)
                def _():
                    out_copy(j, t).start()
            else:
                out_copy(j, target).start()

    for j in range(per_dev):
        assemble(2 * j + 1 - p)
    for zz in range(ring):
        q_copy(zz).wait_recv()
    base_q = (q_keep[...] + q_in[...].astype(F32)).reshape(ring, prompts, SLOTS, cols)
    my_ranks = ranks[pl.ds(p * ring, ring)].reshape(ring, prompts, SLOTS, HEAD)
    row_pos = lax.broadcasted_iota(jnp.int32, (heads * share, slots), 0) % share + p * share
    col_pos = lax.broadcasted_iota(jnp.int32, (heads * share, slots), 1)
    out_pos = lax.broadcasted_iota(jnp.int32, (heads * share, HEAD), 0) % share + p * share
    for i in range(prompts):
        length = lens[t * prompts + i]
        adapter = adapters[t * prompts + i]
        k, v = k_full[i], v_full[i]
        rank_q = my_ranks[:, i].reshape(share, HEAD).astype(BF16)[:, :rank]
        q = base_q[:, i].reshape(share, cols) + jnp.dot(
            rank_q, uq[adapter], preferred_element_type=F32
        )
        q = q.astype(BF16)
        q = jnp.concatenate([q[:, g * HEAD : (g + 1) * HEAD] for g in range(heads)], axis=0)
        s = lax.dot_general(q, k, (((1,), (1,)), ((), ())), preferred_element_type=F32) * scale
        s = jnp.where((col_pos <= row_pos) & (col_pos < length), s, NEG)
        e = jnp.exp(s - jnp.max(s, axis=1, keepdims=True))
        w = (e / jnp.sum(e, axis=1, keepdims=True)).astype(BF16)
        o = jnp.dot(w, v, preferred_element_type=F32)
        o = jnp.where(out_pos < length, o, 0.0).astype(BF16)
        for g in range(heads):
            prefill_ref[i, :, g * HEAD : (g + 1) * HEAD] = o[g * share : (g + 1) * share]

    for b in range(1, 2 * ring):
        for s in range(2):
            hop(b, s, own_piece(s), above).wait_send()
    for target in range(tp_count):
        map_spread(target, t).wait_send()
    for zz in range(ring):
        q_copy(zz).wait_send()
        a_copy(zz).wait_send()
        b_copy(zz).wait_send()
        for hh in range(2):

            mine = [(hh == 1 - h) & (zz == late_zz) for late_zz in ahead(half - 1)]

            @pl.when(jnp.logical_not(mine[0] | mine[1]))
            def _():
                kv_copy(hh, zz).wait_send()

    for i in range(2):
        for d in range(2):
            late_copy(i, d).wait_send()
    column(lambda zz: low_copy(zz).wait_send())
    others(lambda target: rank_copy(target, r).wait_send())
    uv_copy.wait_send()
    for i in range(per_dev):

        @pl.when(jnp.logical_not(step_self(i)))
        def _():
            step_copy(i).wait_send()

    for j in range(per_dev):
        for target in range(tp_count):

            @pl.when(jnp.logical_not((t * per_dev + j == r) & (target == t)))
            def _():
                out_copy(j, target).wait_send()

    def got_out(source, _):
        @pl.when(jnp.logical_not((source == r) & (r // per_dev == t)))
        def _():
            out_arrival(source).wait_recv()

        return 0

    lax.fori_loop(0, req_count, got_out, 0)
    decoded_ref[...] = step_recv[...]


def deliver(prefill_in, decoded_in, prefill_ref, decoded_ref):
    prefill_ref[...] = prefill_in[...]
    steps = decoded_ref.shape[1]
    heads = decoded_in.shape[1] // steps
    for source in range(decoded_in.shape[0]):
        got = decoded_in[source].astype(F32)
        for g in range(heads):
            lanes = pl.ds((source * heads + g) * HEAD, HEAD)
            decoded_ref[0, :, lanes] = got[g * steps : (g + 1) * steps].astype(BF16)


def local(
    prompt_states,
    prompt_lengths,
    adapter_ids,
    w_query,
    w_key,
    value_weight,
    down_query,
    up_query,
    down_value,
    value_up_weight,
    step_queries,
    step_keyvals,
):
    req_count, tp_count = lax.axis_size("req"), lax.axis_size("tp")
    prompts, slots, width = prompt_states.shape
    rows = prompts * slots
    cols = w_query.shape[1]
    kv_cols = w_key.shape[1]
    rank = down_query.shape[2]
    adapter_count = up_query.shape[0]
    ring = req_count // 2
    heads = cols // HEAD
    steps = step_queries.shape[1]
    per_dev = req_count // tp_count
    total_slots = req_count * slots

    vmem = pl.BlockSpec(memory_space=pltpu.VMEM)
    smem = pl.BlockSpec(memory_space=pltpu.SMEM)
    hbm = pl.BlockSpec(memory_space=pl.ANY)
    dma = pltpu.SemaphoreType.DMA
    prefill, decoded = pl.pallas_call(
        functools.partial(kernel, req_count, tp_count),
        out_shape=(
            jax.ShapeDtypeStruct((prompts, total_slots // 2, cols), BF16),
            jax.ShapeDtypeStruct((req_count, heads * steps, HEAD), BF16),
        ),
        in_specs=[smem, smem] + [hbm] * 10,
        out_specs=(vmem, vmem),
        scratch_shapes=[
            pltpu.VMEM((per_dev, heads * steps + 2 * SLOTS, HEAD), BF16),
            pltpu.VMEM((per_dev, heads * steps + 2 * SLOTS, HEAD), F32),
            pltpu.VMEM(step_queries.shape, BF16),
            pltpu.VMEM(step_keyvals.shape, BF16),
            pltpu.VMEM((req_count * rows, width), BF16),
            pltpu.VMEM((width, cols), BF16),
            pltpu.VMEM((SIDE, width), BF16),
            pltpu.VMEM((adapter_count, rank, cols), BF16),
            pltpu.VMEM((adapter_count, rank, kv_cols), BF16),
            pltpu.VMEM((ring, rows, cols), F32),
            pltpu.VMEM((ring, rows, cols), BF16),
            pltpu.VMEM((ring, rows, cols), BF16),
            pltpu.VMEM((ring, rows, SIDE), F32),
            pltpu.VMEM((ring, rows, SIDE), BF16),
            pltpu.VMEM((ring, rows, SIDE), BF16),
            pltpu.VMEM((ring, rows, HEAD), F32),
            pltpu.VMEM((ring, rows, HEAD), BF16),
            pltpu.VMEM((ring, rows, HEAD), BF16),
            pltpu.VMEM((2, ring, rows, HEAD), F32),
            pltpu.VMEM((2, ring, rows, HEAD), F32),
            pltpu.VMEM((2, ring, rows, HEAD), BF16),
            pltpu.VMEM((2, ring, rows, HEAD), BF16),
            pltpu.VMEM((2, 2, rows, HEAD), BF16),
            pltpu.VMEM((ring, rows // 2, HEAD), BF16),
            pltpu.VMEM((ring, rows // 2, HEAD), BF16),
            pltpu.VMEM((req_count, rows // 2, HEAD), BF16),
            pltpu.VMEM((req_count, rows, HEAD), F32),
            pltpu.VMEM((prompts, rank, kv_cols), BF16),
            pltpu.VMEM((prompts, rank, kv_cols), BF16),
            pltpu.VMEM((prompts, total_slots, HEAD), BF16),
            pltpu.VMEM((prompts, total_slots, HEAD), BF16),
            pltpu.VMEM((per_dev, heads * steps + 2 * SLOTS, HEAD), BF16),
            pltpu.VMEM((per_dev, heads * steps, HEAD), BF16),
            pltpu.VMEM((req_count, heads * steps, HEAD), BF16),
            dma((10,)),
            dma((req_count, 2)),
            dma((req_count, 2)),
            dma((tp_count,)),
            dma((tp_count,)),
            dma((ring,)),
            dma((ring,)),
            dma((ring,)),
            dma((ring,)),
            dma((ring,)),
            dma((ring,)),
            dma((2, ring)),
            dma((2, ring)),
            dma((2, 2)),
            dma((2, 2)),
            dma((ring,)),
            dma((ring,)),
            dma((req_count,)),
            dma((req_count,)),
            dma((2,)),
            dma((per_dev,)),
            dma((per_dev,)),
            dma((per_dev, tp_count)),
            dma((req_count,)),
            pltpu.SemaphoreType.REGULAR,
        ],
        compiler_params=pltpu.CompilerParams(
            collective_id=0, has_side_effects=True, vmem_limit_bytes=56 * 1024 * 1024
        ),
        cost_estimate=pl.CostEstimate(
            flops=2 * req_count * rows * width * (cols + SIDE),
            bytes_accessed=2 * width * (cols + SIDE),
            transcendentals=0,
        ),
    )(
        prompt_lengths,
        adapter_ids,
        prompt_states.reshape(rows, width),
        w_query,
        w_key.T,
        value_weight.T,
        down_query[0].T,
        down_value[0].T,
        up_query,
        value_up_weight,
        step_queries,
        step_keyvals,
    )
    return pl.pallas_call(
        deliver,
        out_shape=(
            jax.ShapeDtypeStruct(prefill.shape, BF16),
            jax.ShapeDtypeStruct(step_queries.shape, BF16),
        ),
        in_specs=[vmem, vmem],
        out_specs=(vmem, vmem),
    )(prefill, decoded)


def solution(mesh):
    in_specs = (
        P("tp", "req", "pp"),
        P(),
        P(),
        P("pp", "req"),
        P("pp", "req"),
        P("pp", "req"),
        P("req", "pp", None),
        P(None, None, "req"),
        P("req", "pp", None),
        P(None, None, "req"),
        P(("req", "pp"), None, None),
        P(("req", "pp"), None, None, None),
    )
    out_specs = (P("tp", "pp", "req"), P(("req", "pp"), None, None))
    return jax.shard_map(local, mesh=mesh, in_specs=in_specs, out_specs=out_specs, check_vma=False)
```

```python
import functools

import jax
import jax.numpy as jnp
from jax import lax
from jax.experimental import pallas as pl
from jax.experimental.pallas import tpu as pltpu
from jax.sharding import PartitionSpec as P

HEAD = 128
SLOTS = 8
SIDE = 256
NEG = -1e30
F32 = jnp.float32
BF16 = jnp.bfloat16
MESH = pl.DeviceIdType.MESH


def kernel(
    req_count,
    tp_count,
    lens,
    adapters,
    x_hbm,
    wq_hbm,
    wk_hbm,
    wv_hbm,
    dq_hbm,
    dv_hbm,
    uq_hbm,
    uv_hbm,
    sq_hbm,
    skv_hbm,
    prefill_ref,
    decoded_ref,
    msg_ref,
    msg_f32,
    sq,
    skv,
    blocks,
    weights,
    side_w,
    uq,
    uv,
    q_keep,
    q_out,
    q_in,
    a_own,
    a_out,
    a_in,
    b_own,
    b_out,
    b_in,
    kv_own,
    kv_oth,
    kv_out,
    kv_in,
    late_in,
    low_out,
    low_in,
    far_in,
    rank_all,
    ranks,
    uv_out,
    uv_in,
    k_full,
    v_full,
    step_in,
    step_out,
    step_recv,
    load_sem,
    ring_send,
    ring_recv,
    map_send,
    map_recv,
    q_send,
    q_recv,
    a_send,
    a_recv,
    b_send,
    b_recv,
    kv_send,
    kv_recv,
    late_send,
    late_recv,
    low_send,
    low_recv,
    far_send,
    far_recv,
    rank_send,
    rank_recv,
    uv_sems,
    step_send,
    step_got,
    out_send,
    out_got,
    hello,
    prefill,
    prefill_sem,
):
    r, t, p = lax.axis_index("req"), lax.axis_index("tp"), lax.axis_index("pp")
    ring = req_count // 2
    half = ring // 2
    h, z = r // ring, r % ring
    rows = x_hbm.shape[0]
    part = rows // 2
    prompts = rows // SLOTS
    cols = q_keep.shape[2]
    heads = cols // HEAD
    per_dev = req_count // tp_count
    kv_cols, rank = wk_hbm.shape[0], dq_hbm.shape[0]
    maps = 2 * rank
    above = h * ring + (z + 1) % ring
    below = h * ring + (z + ring - 1) % ring
    across = (1 - h) * ring + z
    other = 1 - p
    pair = r + 1 - 2 * (r % 2)
    far = (z + half) % ring
    pair_late = [(pair + ring - half + 1) % ring, (pair + half - 1) % ring]

    def remote(src, dst, send, recv, req=None, tp=None, pp=None):
        where = (r if req is None else req, t if tp is None else tp, p if pp is None else pp)
        return pltpu.make_async_remote_copy(
            src_ref=src,
            dst_ref=dst,
            send_sem=send,
            recv_sem=recv,
            device_id=where,
            device_id_type=MESH,
        )

    loads = [
        pltpu.make_async_copy(src, dst, load_sem.at[i])
        for i, (src, dst) in enumerate(
            [
                (dq_hbm, side_w.at[pl.ds(2 * kv_cols, rank)]),
                (dv_hbm, side_w.at[pl.ds(2 * kv_cols + rank, rank)]),
                (wk_hbm, side_w.at[pl.ds(0, kv_cols)]),
                (wv_hbm, side_w.at[pl.ds(kv_cols, kv_cols)]),
                (x_hbm, blocks.at[pl.ds(0, rows)]),
                (wq_hbm, weights),
                (uq_hbm, uq),
                (uv_hbm, uv),
                (sq_hbm, sq),
                (skv_hbm, skv),
            ]
        )
    ]
    for load in loads:
        load.start()

    barrier = pltpu.get_barrier_semaphore()
    for where in ((above, t, p), (below, t, p), (across, t, p), (r, t, other)):
        pl.semaphore_signal(barrier, inc=1, device_id=where, device_id_type=MESH)
    for o in range(1, tp_count):
        pl.semaphore_signal(
            barrier, inc=1, device_id=(r, (t + o) % tp_count, p), device_id_type=MESH
        )
    pl.semaphore_wait(barrier, 3 + tp_count)

    def own(k, way=0):
        return 0 if k == 0 else 2 + 4 * (k - 1) + (way if k < half else -2)

    def cross(k, way=0):
        if k == 0:
            return 1
        if k == half:
            return 2 * ring - 1
        return 2 + 4 * (k - 1) + (2 if k < half - 1 else 3) + way

    def piece(b, s):
        return blocks.at[pl.ds(b * rows + s * part, part)]

    def own_piece(s):
        return x_hbm.at[pl.ds(s * part, part)]

    def hop(b, s, src, req):
        return remote(src, piece(b, s), ring_send.at[b, s], ring_recv.at[b, s], req=req)

    def arrive(b, s):
        hop(b, s, own_piece(s), across).wait_recv()

    toward = (above, below)
    order = ((0, 0), (1, 1), (0, 1), (1, 0))

    for way, s in order:
        hop(own(1, way), s, own_piece(s), toward[way]).start()

    strip = side_w.shape[1] // tp_count

    def map_at(first, owner):
        return side_w.at[
            pl.ds(first, maps), pl.ds(pl.multiple_of(owner * strip, strip), strip)
        ]

    map_row = 2 * kv_cols + maps

    def map_hop():
        return remote(
            map_at(2 * kv_cols, t), map_at(map_row, t), map_send.at[t], map_recv.at[t], req=across
        )

    def map_spread(target, owner):
        return remote(
            map_at(map_row, owner),
            map_at(map_row, owner),
            map_send.at[target],
            map_recv.at[owner],
            tp=target,
        )

    for load in loads[:2]:
        load.wait()
    map_hop().start()
    for s in range(2):
        hop(cross(0), s, own_piece(s), across).start()
    for load in loads[2:]:
        load.wait()
    def make_messages():
        steps = sq.shape[1]
        msg_f32[...] = jnp.zeros(msg_f32.shape, F32)
        for i in range(per_dev):
            head = t * per_dev + i
            for g in range(heads):
                lanes = pl.ds(pl.multiple_of(head * cols + g * HEAD, HEAD), HEAD)
                msg_f32[i, g * steps : (g + 1) * steps] = sq[0, :, lanes].astype(F32)
            lanes = pl.ds(pl.multiple_of((head // 2) * HEAD, HEAD), HEAD)
            for s in range(steps):
                new = skv[0, s, :, lanes].astype(F32)
                first = heads * steps + s
                msg_f32[i, first : first + 1] = new[0:1]
                msg_f32[i, first + SLOTS : first + SLOTS + 1] = new[1:2]
        msg_ref[...] = msg_f32[...].astype(BF16)

    for i in range(prompts):
        uv_out[i] = uv[adapters[t * prompts + i]]
    uv_copy = remote(uv_out, uv_in, uv_sems.at[0], uv_sems.at[1], req=pair)
    uv_copy.start()
    make_messages()

    map_hop().wait_recv()
    for o in range(1, tp_count):
        map_spread((t + o) % tp_count, t).start()

    def q_copy(zz):
        return remote(q_out.at[zz], q_in.at[zz], q_send.at[zz], q_recv.at[zz], pp=other)

    def a_copy(zz):
        return remote(a_out.at[zz], a_in.at[zz], a_send.at[zz], a_recv.at[zz], pp=other)

    def b_copy(zz):
        return remote(b_out.at[zz], b_in.at[zz], b_send.at[zz], b_recv.at[zz], pp=other)

    def late_copy(i, d):
        return remote(
            b_out.at[ahead(half - 1)[d]],
            late_in.at[i, d],
            late_send.at[i, d],
            late_recv.at[i, d],
            req=pair,
            pp=(p, other)[i],
        )

    def low_copy(zz):
        return remote(
            low_out.at[zz], low_in.at[z], low_send.at[zz], low_recv.at[z], req=h * ring + zz
        )

    def low_arrival(zz):
        return remote(
            low_out.at[zz], low_in.at[zz], low_send.at[zz], low_recv.at[zz], req=h * ring + zz
        )

    def far_low(zz, source):
        return remote(
            low_out.at[zz],
            far_in.at[source],
            far_send.at[zz],
            far_recv.at[source],
            req=h * ring + zz,
            pp=other,
        )

    near_lane = lax.broadcasted_iota(jnp.int32, (rows, HEAD), 1) < maps
    prompt_of = lax.broadcasted_iota(jnp.int32, (rows, HEAD), 0) // SLOTS
    match = jnp.zeros((rows, HEAD), F32)
    for i in range(prompts):
        adapter = adapters[t * prompts + i]
        mine = jnp.where(adapter == r, 1.0, 0.0)
        theirs = jnp.where(adapter == across, 1.0, 0.0)
        match = jnp.where(prompt_of == i, jnp.where(near_lane, mine, theirs), match)

    def packed_low(both_maps):
        low = jnp.where(match > 0.0, both_maps, 0.0)
        low = low + pltpu.roll(low, HEAD // 2, 1)
        return jnp.where(near_lane[:part], low[:part], low[part:]).astype(BF16)

    waiting = []

    def project(first, places, in_own, late=False, far_ranks=False):
        count = len(places) * rows
        at = pl.ds(first * rows, count)
        side = SIDE if any(in_own) else HEAD
        got = lax.dot_general(
            blocks[at, :],
            side_w[:side],
            (((1,), (1,)), ((), ())),
            preferred_element_type=F32,
        )
        for i, (zz, mine) in enumerate(zip(places, in_own)):
            block = got[i * rows : (i + 1) * rows]
            if mine:
                a_own[zz] = block
                a_out[zz] = block.astype(BF16)
                if far_ranks:
                    low_out[zz] = packed_low(block[:, HEAD:])
                    low_copy(zz).start()
                    far_low(zz, z).start()
                a_copy(zz).start()
            else:
                b_own[zz] = block[:, :HEAD]
                b_out[zz] = block[:, :HEAD].astype(BF16)
                b_copy(zz).start()
                if late:
                    late_copy(0, i).start()
                    late_copy(1, i).start()

        def part_of(n, _):
            lanes = pl.ds(pl.multiple_of(n * SIDE, SIDE), SIDE)
            got = jnp.dot(blocks[at, :], weights[:, lanes], preferred_element_type=F32)
            for i, (zz, mine) in enumerate(zip(places, in_own)):
                block = got[i * rows : (i + 1) * rows]
                keep = (h == p) if mine else (h != p)

                @pl.when(keep)
                def _():
                    q_keep[zz, :, lanes] = block

                @pl.when(jnp.logical_not(keep))
                def _():
                    q_out[zz, :, lanes] = block.astype(BF16)

            return 0

        lax.fori_loop(0, cols // SIDE, part_of, 0)
        for zz, mine in zip(places, in_own):
            if False:

                @pl.when((h != p) if mine else (h == p))
                def _():
                    q_copy(zz).start()

            else:
                waiting.append((zz, mine))

    def kv_copy(hh, zz):
        return remote(
            kv_out.at[hh, zz],
            kv_in.at[hh, zz],
            kv_send.at[hh, zz],
            kv_recv.at[hh, zz],
            req=pair,
        )

    def finish_kv(hh, zz, total):
        kv_own[hh, zz] = total
        kv_out[hh, zz] = total.astype(BF16)
        kv_copy(hh, zz).start()

    def finish_own(zz, self_too=False, sent=False):
        a_copy(zz).wait_recv()
        total = a_own[zz] + a_in[zz].astype(F32)
        finish_kv(h, zz, total[:, :HEAD])
        if self_too:
            low_in[zz] = packed_low(total[:, HEAD:SIDE])
        elif not sent:
            low_out[zz] = packed_low(total[:, HEAD:SIDE])
            low_copy(zz).start()

    def finish_cross(zz):
        b_copy(zz).wait_recv()
        finish_kv(1 - h, zz, b_own[zz] + b_in[zz].astype(F32))

    def ahead(k):
        return [(z + ring - k) % ring, (z + k) % ring]

    def arrive_own(k):
        for way, s in order:
            arrive(own(k, way), s)
            src = piece(own(k, way), s)
            if k < half - 1:
                hop(own(k + 1, way), s, src, toward[way]).start()
            elif s == way:
                hop(own(half), s, src, toward[way]).start()
            if k == 1:
                hop(cross(k, way), s, src, across).start()

    def arrive_cross(k, which=order):
        for way, s in which:
            arrive(cross(k, way), s)
            src = piece(cross(k, way), s)
            if k < half - 1:
                hop(cross(k + 1, way), s, src, toward[way]).start()

    def arrive_both(b):
        for s in range(2):
            arrive(b, s)

    def step_copy(i):
        target = t * per_dev + i
        return remote(
            msg_ref.at[i],
            step_in.at[r % per_dev],
            step_send.at[i],
            step_got.at[r % per_dev],
            req=target,
            tp=r // per_dev,
        )

    def step_self(i):
        return (t * per_dev + i == r) & (r // per_dev == t)

    both = [True, True]
    neither = [False, False]

    arrive_own(1)
    arrive_both(cross(0))
    if half > 2:
        arrive_own(2)
    for o in range(1, tp_count):
        map_spread(t, (t + o) % tp_count).wait_recv()
    project(0, [z, z], [True, False])
    if half > 2:
        project(own(1), ahead(1), both)
    for k in range(3, half):
        arrive_own(k)
        arrive_cross(k - 2)
        project(own(k - 1), ahead(k - 1), both)
        if k < half - 1:
            project(cross(k - 2), ahead(k - 2), neither)
    for s in range(2):
        arrive(own(half), s)
        hop(cross(half), s, piece(own(half), s), across).start()
    pl.semaphore_signal(hello, inc=1, device_id=(across, t, p), device_id_type=MESH)
    project(own(half - 1), ahead(half - 1) + [far], [True] * 3, far_ranks=True)
    pl.semaphore_wait(hello, 1)
    for i in range(per_dev):

        @pl.when(step_self(i))
        def _():
            step_in[r % per_dev] = msg_ref[i]

        @pl.when(jnp.logical_not(step_self(i)))
        def _():
            step_copy(i).start()

    if half > 3:
        project(cross(half - 3), ahead(half - 3), neither)
    finish_own(z, True)
    finish_cross(z)
    for k in range(1, half - 1):
        for zz in ahead(k):
            finish_own(zz)
    if half > 2:
        arrive_cross(half - 2, order[:2])
    for zz in ahead(half - 1) + [far]:
        finish_own(zz, sent=True)
    if half > 2:
        arrive_cross(half - 2, order[2:])
        project(cross(half - 2), ahead(half - 2), neither)

    distances = sorted(range(ring), key=lambda o: -min(o, ring - o))

    def others(body):
        for o in distances:
            body((1 - h) * ring + (z + o) % ring)
            if o > 0:
                body(h * ring + (z + o) % ring)

    def column(body):
        for o in distances[:-1]:
            body((z + o) % ring)

    def rank_copy(target, slot):
        return remote(
            rank_all.at[slot], rank_all.at[slot], rank_send.at[target], rank_recv.at[slot], req=target
        )

    column(lambda zz: low_arrival(zz).wait_recv())
    for zz in ahead(half - 1) + [far]:
        far_low(zz, zz).wait_recv()
    low = low_in[0].astype(F32)
    for zz in range(1, ring):
        low = low + low_in[zz].astype(F32)
    for zz in ahead(half - 1) + [far]:
        low = low + far_in[zz].astype(F32)
    rank_all[r] = low.astype(BF16)
    others(lambda target: rank_copy(target, r).start())

    for k in range(1, half - 2):
        for zz in ahead(k):
            finish_cross(zz)
    arrive_both(cross(half))
    project(cross(half), [far], [False])

    if half > 2:
        for zz in ahead(half - 2):
            finish_cross(zz)
    def take_pair(hh, zz):
        kv_copy(hh, zz).wait_recv()
        kv_oth[hh, zz] = kv_in[hh, zz].astype(F32)

    uv_copy.wait_recv()
    for o in range(ring):
        take_pair(h, (z + o) % ring)
    for o in (0, 1, ring - 1):
        if o not in (half - 1, half + 1):
            take_pair(1 - h, (pair + o) % ring)
    arrive_cross(half - 1)
    project(cross(half - 1), ahead(half - 1), neither, late=True)
    for zz, mine in waiting:

        @pl.when((h != p) if mine else (h == p))
        def _():
            q_copy(zz).start()


    finish_cross(far)
    for zz in ahead(half - 1):
        b_copy(zz).wait_recv()
        kv_own[1 - h, zz] = b_own[zz] + b_in[zz].astype(F32)
    for i in range(2):
        for d in range(2):
            late_copy(i, d).wait_recv()
    for d in range(2):
        kv_oth[1 - h, pair_late[d]] = late_in[0, d].astype(F32) + late_in[1, d].astype(F32)
    for o in range(2, ring - 1):
        if o not in (half - 1, half + 1):
            take_pair(1 - h, (pair + o) % ring)

    even = r % 2 == 0
    slots = req_count * SLOTS
    share = slots // 2
    low_lane = lax.broadcasted_iota(jnp.int32, (slots, HEAD), 1) < HEAD // 2
    scale = HEAD ** (-0.5)

    def halves(n):
        at = pl.ds(pl.multiple_of(n * SLOTS, SLOTS), SLOTS)
        mine = kv_own[:, :, at, :].reshape(slots, HEAD)
        theirs = kv_oth[:, :, at, :].reshape(slots, HEAD)
        return jnp.where(even, mine, theirs), jnp.where(even, theirs, mine)

    def keys_of(n):
        first, second = halves(n)
        return jnp.where(low_lane, first, pltpu.roll(second, HEAD // 2, 1)).astype(BF16)

    def values_of(n):
        first, second = halves(n)
        v = jnp.where(low_lane, pltpu.roll(first, HEAD // 2, 1), second)
        uv_mine, uv_theirs = uv_out[n], uv_in[n]
        up_v = jnp.concatenate(
            [jnp.where(even, uv_mine, uv_theirs), jnp.where(even, uv_theirs, uv_mine)], axis=1
        )
        at = pl.ds(pl.multiple_of(n * SLOTS, SLOTS), SLOTS)
        rank_rows = ranks[:, at, :].reshape(slots, HEAD).astype(BF16)
        v = v + jnp.dot(rank_rows[:, rank:maps], up_v, preferred_element_type=F32)
        return v.astype(BF16)

    steps = step_out.shape[1] // heads
    qrows = heads * steps

    def step_arrival(j):
        source_req = t * per_dev + j
        return remote(
            msg_ref.at[0],
            step_in.at[j],
            step_send.at[0],
            step_got.at[j],
            req=source_req,
            tp=r // per_dev,
        )

    def out_copy(j, target):
        return remote(
            step_out.at[j],
            step_recv.at[r],
            out_send.at[j, target],
            out_got.at[r],
            req=t * per_dev + j,
            tp=target,
        )

    def out_arrival(source):
        return remote(
            step_out.at[0],
            step_recv.at[source],
            out_send.at[0, 0],
            out_got.at[source],
            req=source,
            tp=r // per_dev,
        )

    for j in range(per_dev):

        @pl.when(jnp.logical_not((t * per_dev + j == r) & (r // per_dev == t)))
        def _():
            step_arrival(j).wait_recv()

    weighed = []
    for j in range(per_dev):
        n = 2 * j + p
        length = lens[t * prompts + n]
        k = keys_of(n)
        k_full[n] = k
        got = step_in[j]
        qs = got[:qrows]
        tail = got[qrows:].astype(F32)
        new_k = tail[:SLOTS].astype(BF16)
        new_v = tail[SLOTS : 2 * SLOTS].astype(BF16)
        s_old = lax.dot_general(qs, k, (((1,), (1,)), ((), ())), preferred_element_type=F32) * scale
        s_new = (
            lax.dot_general(qs, new_k, (((1,), (1,)), ((), ())), preferred_element_type=F32) * scale
        )
        s_old = jnp.where(lax.broadcasted_iota(jnp.int32, (qrows, slots), 1) < length, s_old, NEG)
        at_step = lax.broadcasted_iota(jnp.int32, (qrows, SLOTS), 0) % steps
        at_new = lax.broadcasted_iota(jnp.int32, (qrows, SLOTS), 1)
        s_new = jnp.where(at_new <= at_step, s_new, NEG)
        top = jnp.maximum(
            jnp.max(s_old, axis=1, keepdims=True), jnp.max(s_new, axis=1, keepdims=True)
        )
        e_old, e_new = jnp.exp(s_old - top), jnp.exp(s_new - top)
        total = jnp.sum(e_old, axis=1, keepdims=True) + jnp.sum(e_new, axis=1, keepdims=True)

        def weigh(e, values):
            coarse = e.astype(BF16)
            fine = (e - coarse.astype(F32)).astype(BF16)
            return jnp.dot(coarse, values, preferred_element_type=F32) + jnp.dot(
                fine, values, preferred_element_type=F32
            )

        weighed.append((weigh, e_old, weigh(e_new, new_v), 1.0 / total))

    others(lambda source: rank_copy(source, source).wait_recv())
    for source in range(req_count):
        packed = rank_all[source].astype(F32)
        ranks[source, :part] = packed
        ranks[source, part:] = pltpu.roll(packed, HEAD // 2, 1)
    for j in range(per_dev):
        n = 2 * j + p
        v = values_of(n)
        v_full[n] = v
        weigh, e_old, new_part, inverse = weighed[j]
        step_out[j] = ((weigh(e_old, v) + new_part) * inverse).astype(BF16)
    for o in sorted(range(tp_count), key=lambda o: -min(o, tp_count - o)):
        target = (t + o) % tp_count
        for j in range(per_dev):
            if o == 0:

                @pl.when(t * per_dev + j == r)
                def _():
                    step_recv[r] = step_out[j]

                @pl.when(t * per_dev + j != r)
                def _():
                    out_copy(j, t).start()
            else:
                out_copy(j, target).start()

    for j in range(per_dev):
        n = 2 * j + 1 - p
        k_full[n] = keys_of(n)
        v_full[n] = values_of(n)
    for zz in range(ring):
        q_copy(zz).wait_recv()
    base_q = (q_keep[...] + q_in[...].astype(F32)).reshape(ring, prompts, SLOTS, cols)
    my_ranks = ranks[pl.ds(p * ring, ring)].reshape(ring, prompts, SLOTS, HEAD)
    row_pos = lax.broadcasted_iota(jnp.int32, (heads * share, slots), 0) % share + p * share
    col_pos = lax.broadcasted_iota(jnp.int32, (heads * share, slots), 1)
    out_pos = lax.broadcasted_iota(jnp.int32, (heads * share, HEAD), 0) % share + p * share
    def prefill_copy(i):
        return pltpu.make_async_copy(prefill.at[i], prefill_ref.at[i], prefill_sem.at[i])

    for i in range(prompts):
        length = lens[t * prompts + i]
        adapter = adapters[t * prompts + i]
        k, v = k_full[i], v_full[i]
        rank_q = my_ranks[:, i].reshape(share, HEAD).astype(BF16)[:, :rank]
        q = base_q[:, i].reshape(share, cols) + jnp.dot(
            rank_q, uq[adapter], preferred_element_type=F32
        )
        q = q.astype(BF16)
        q = jnp.concatenate([q[:, g * HEAD : (g + 1) * HEAD] for g in range(heads)], axis=0)
        s = lax.dot_general(q, k, (((1,), (1,)), ((), ())), preferred_element_type=F32) * scale
        s = jnp.where((col_pos <= row_pos) & (col_pos < length), s, NEG)
        e = jnp.exp(s - jnp.max(s, axis=1, keepdims=True))
        w = (e / jnp.sum(e, axis=1, keepdims=True)).astype(BF16)
        o = jnp.dot(w, v, preferred_element_type=F32)
        o = jnp.where(out_pos < length, o, 0.0).astype(BF16)
        for g in range(heads):
            prefill[i, :, g * HEAD : (g + 1) * HEAD] = o[g * share : (g + 1) * share]
        prefill_copy(i).start()

    for b in range(1, 2 * ring):
        for s in range(2):
            hop(b, s, own_piece(s), above).wait_send()
    for target in range(tp_count):
        map_spread(target, t).wait_send()
    for zz in range(ring):
        q_copy(zz).wait_send()
        a_copy(zz).wait_send()
        b_copy(zz).wait_send()
        for hh in range(2):

            mine = [(hh == 1 - h) & (zz == late_zz) for late_zz in ahead(half - 1)]

            @pl.when(jnp.logical_not(mine[0] | mine[1]))
            def _():
                kv_copy(hh, zz).wait_send()

    for i in range(2):
        for d in range(2):
            late_copy(i, d).wait_send()
    column(lambda zz: low_copy(zz).wait_send())
    for zz in ahead(half - 1) + [far]:
        far_low(zz, z).wait_send()
    others(lambda target: rank_copy(target, r).wait_send())
    uv_copy.wait_send()
    for i in range(per_dev):

        @pl.when(jnp.logical_not(step_self(i)))
        def _():
            step_copy(i).wait_send()

    for j in range(per_dev):
        for target in range(tp_count):

            @pl.when(jnp.logical_not((t * per_dev + j == r) & (target == t)))
            def _():
                out_copy(j, target).wait_send()

    def got_out(source, _):
        @pl.when(jnp.logical_not((source == r) & (r // per_dev == t)))
        def _():
            out_arrival(source).wait_recv()

        return 0

    lax.fori_loop(0, req_count, got_out, 0)
    decoded_ref[...] = step_recv[...]
    for i in range(prompts):
        prefill_copy(i).wait()


def deliver(prefill_in, decoded_in, prefill_ref, decoded_ref):
    prefill_ref[...] = prefill_in[...]
    steps = decoded_ref.shape[1]
    heads = decoded_in.shape[1] // steps
    for source in range(decoded_in.shape[0]):
        got = decoded_in[source].astype(F32)
        for g in range(heads):
            lanes = pl.ds((source * heads + g) * HEAD, HEAD)
            decoded_ref[0, :, lanes] = got[g * steps : (g + 1) * steps].astype(BF16)


def local(
    prompt_states,
    prompt_lengths,
    adapter_ids,
    w_query,
    w_key,
    value_weight,
    down_query,
    up_query,
    down_value,
    value_up_weight,
    step_queries,
    step_keyvals,
):
    req_count, tp_count = lax.axis_size("req"), lax.axis_size("tp")
    prompts, slots, width = prompt_states.shape
    rows = prompts * slots
    cols = w_query.shape[1]
    kv_cols = w_key.shape[1]
    rank = down_query.shape[2]
    adapter_count = up_query.shape[0]
    ring = req_count // 2
    heads = cols // HEAD
    steps = step_queries.shape[1]
    per_dev = req_count // tp_count
    total_slots = req_count * slots

    vmem = pl.BlockSpec(memory_space=pltpu.VMEM)
    smem = pl.BlockSpec(memory_space=pltpu.SMEM)
    hbm = pl.BlockSpec(memory_space=pl.ANY)
    dma = pltpu.SemaphoreType.DMA
    prefill, decoded = pl.pallas_call(
        functools.partial(kernel, req_count, tp_count),
        out_shape=(
            jax.ShapeDtypeStruct((prompts, total_slots // 2, cols), BF16),
            jax.ShapeDtypeStruct((req_count, heads * steps, HEAD), BF16),
        ),
        in_specs=[smem, smem] + [hbm] * 10,
        out_specs=(hbm, vmem),
        scratch_shapes=[
            pltpu.VMEM((per_dev, heads * steps + 2 * SLOTS, HEAD), BF16),
            pltpu.VMEM((per_dev, heads * steps + 2 * SLOTS, HEAD), F32),
            pltpu.VMEM(step_queries.shape, BF16),
            pltpu.VMEM(step_keyvals.shape, BF16),
            pltpu.VMEM((req_count * rows, width), BF16),
            pltpu.VMEM((width, cols), BF16),
            pltpu.VMEM((SIDE, width), BF16),
            pltpu.VMEM((adapter_count, rank, cols), BF16),
            pltpu.VMEM((adapter_count, rank, kv_cols), BF16),
            pltpu.VMEM((ring, rows, cols), F32),
            pltpu.VMEM((ring, rows, cols), BF16),
            pltpu.VMEM((ring, rows, cols), BF16),
            pltpu.VMEM((ring, rows, SIDE), F32),
            pltpu.VMEM((ring, rows, SIDE), BF16),
            pltpu.VMEM((ring, rows, SIDE), BF16),
            pltpu.VMEM((ring, rows, HEAD), F32),
            pltpu.VMEM((ring, rows, HEAD), BF16),
            pltpu.VMEM((ring, rows, HEAD), BF16),
            pltpu.VMEM((2, ring, rows, HEAD), F32),
            pltpu.VMEM((2, ring, rows, HEAD), F32),
            pltpu.VMEM((2, ring, rows, HEAD), BF16),
            pltpu.VMEM((2, ring, rows, HEAD), BF16),
            pltpu.VMEM((2, 2, rows, HEAD), BF16),
            pltpu.VMEM((ring, rows // 2, HEAD), BF16),
            pltpu.VMEM((ring, rows // 2, HEAD), BF16),
            pltpu.VMEM((ring, rows // 2, HEAD), BF16),
            pltpu.VMEM((req_count, rows // 2, HEAD), BF16),
            pltpu.VMEM((req_count, rows, HEAD), F32),
            pltpu.VMEM((prompts, rank, kv_cols), BF16),
            pltpu.VMEM((prompts, rank, kv_cols), BF16),
            pltpu.VMEM((prompts, total_slots, HEAD), BF16),
            pltpu.VMEM((prompts, total_slots, HEAD), BF16),
            pltpu.VMEM((per_dev, heads * steps + 2 * SLOTS, HEAD), BF16),
            pltpu.VMEM((per_dev, heads * steps, HEAD), BF16),
            pltpu.VMEM((req_count, heads * steps, HEAD), BF16),
            dma((10,)),
            dma((req_count, 2)),
            dma((req_count, 2)),
            dma((tp_count,)),
            dma((tp_count,)),
            dma((ring,)),
            dma((ring,)),
            dma((ring,)),
            dma((ring,)),
            dma((ring,)),
            dma((ring,)),
            dma((2, ring)),
            dma((2, ring)),
            dma((2, 2)),
            dma((2, 2)),
            dma((ring,)),
            dma((ring,)),
            dma((ring,)),
            dma((ring,)),
            dma((req_count,)),
            dma((req_count,)),
            dma((2,)),
            dma((per_dev,)),
            dma((per_dev,)),
            dma((per_dev, tp_count)),
            dma((req_count,)),
            pltpu.SemaphoreType.REGULAR,
            pltpu.VMEM((prompts, total_slots // 2, cols), BF16),
            dma((prompts,)),
        ],
        compiler_params=pltpu.CompilerParams(
            collective_id=0, has_side_effects=True, vmem_limit_bytes=56 * 1024 * 1024
        ),
        cost_estimate=pl.CostEstimate(
            flops=2 * req_count * rows * width * (cols + SIDE),
            bytes_accessed=2 * width * (cols + SIDE),
            transcendentals=0,
        ),
    )(
        prompt_lengths,
        adapter_ids,
        prompt_states.reshape(rows, width),
        w_query,
        w_key.T,
        value_weight.T,
        down_query[0].T,
        down_value[0].T,
        up_query,
        value_up_weight,
        step_queries,
        step_keyvals,
    )
    return pl.pallas_call(
        deliver,
        out_shape=(
            jax.ShapeDtypeStruct(prefill.shape, BF16),
            jax.ShapeDtypeStruct(step_queries.shape, BF16),
        ),
        in_specs=[vmem, vmem],
        out_specs=(vmem, vmem),
    )(prefill, decoded)


def solution(mesh):
    in_specs = (
        P("tp", "req", "pp"),
        P(),
        P(),
        P("pp", "req"),
        P("pp", "req"),
        P("pp", "req"),
        P("req", "pp", None),
        P(None, None, "req"),
        P("req", "pp", None),
        P(None, None, "req"),
        P(("req", "pp"), None, None),
        P(("req", "pp"), None, None, None),
    )
    out_specs = (P("tp", "pp", "req"), P(("req", "pp"), None, None))
    return jax.shard_map(local, mesh=mesh, in_specs=in_specs, out_specs=out_specs, check_vma=False)
```

```python
import functools

import jax
import jax.numpy as jnp
from jax import lax
from jax.experimental import pallas as pl
from jax.experimental.pallas import tpu as pltpu
from jax.sharding import PartitionSpec as P

HEAD = 128
SLOTS = 8
SIDE = 256
NEG = -1e30
F32 = jnp.float32
BF16 = jnp.bfloat16
MESH = pl.DeviceIdType.MESH


def kernel(
    req_count,
    tp_count,
    lens,
    adapters,
    x_hbm,
    wq_hbm,
    wk_hbm,
    wv_hbm,
    dq_hbm,
    dv_hbm,
    uq_hbm,
    uv_hbm,
    sq_hbm,
    skv_hbm,
    prefill_ref,
    decoded_ref,
    msg_ref,
    msg_f32,
    sq,
    skv,
    blocks,
    weights,
    side_w,
    uq,
    uv,
    q_keep,
    q_out,
    q_in,
    a_own,
    a_out,
    a_in,
    b_own,
    b_out,
    b_in,
    kv_own,
    kv_oth,
    kv_out,
    kv_in,
    late_in,
    low_out,
    low_in,
    far_in,
    rank_all,
    ranks,
    uv_out,
    uv_in,
    k_full,
    v_full,
    step_in,
    step_out,
    step_recv,
    load_sem,
    ring_send,
    ring_recv,
    map_send,
    map_recv,
    q_send,
    q_recv,
    a_send,
    a_recv,
    b_send,
    b_recv,
    kv_send,
    kv_recv,
    late_send,
    late_recv,
    low_send,
    low_recv,
    far_send,
    far_recv,
    rank_send,
    rank_recv,
    uv_sems,
    step_send,
    step_got,
    out_send,
    out_got,
    hello,
    prefill,
    prefill_sem,
):
    r, t, p = lax.axis_index("req"), lax.axis_index("tp"), lax.axis_index("pp")
    ring = req_count // 2
    half = ring // 2
    h, z = r // ring, r % ring
    rows = x_hbm.shape[0]
    part = rows // 2
    prompts = rows // SLOTS
    cols = q_keep.shape[2]
    heads = cols // HEAD
    per_dev = req_count // tp_count
    kv_cols, rank = wk_hbm.shape[0], dq_hbm.shape[0]
    maps = 2 * rank
    above = h * ring + (z + 1) % ring
    below = h * ring + (z + ring - 1) % ring
    across = (1 - h) * ring + z
    other = 1 - p
    pair = r + 1 - 2 * (r % 2)
    far = (z + half) % ring
    pair_late = [(pair + ring - half + 1) % ring, (pair + half - 1) % ring]

    def remote(src, dst, send, recv, req=None, tp=None, pp=None):
        where = (r if req is None else req, t if tp is None else tp, p if pp is None else pp)
        return pltpu.make_async_remote_copy(
            src_ref=src,
            dst_ref=dst,
            send_sem=send,
            recv_sem=recv,
            device_id=where,
            device_id_type=MESH,
        )

    loads = [
        pltpu.make_async_copy(src, dst, load_sem.at[i])
        for i, (src, dst) in enumerate(
            [
                (dq_hbm, side_w.at[pl.ds(2 * kv_cols, rank)]),
                (dv_hbm, side_w.at[pl.ds(2 * kv_cols + rank, rank)]),
                (wk_hbm, side_w.at[pl.ds(0, kv_cols)]),
                (wv_hbm, side_w.at[pl.ds(kv_cols, kv_cols)]),
                (x_hbm, blocks.at[pl.ds(0, rows)]),
                (wq_hbm, weights),
                (uq_hbm, uq),
                (uv_hbm, uv),
                (sq_hbm, sq),
                (skv_hbm, skv),
            ]
        )
    ]
    for load in loads:
        load.start()

    barrier = pltpu.get_barrier_semaphore()
    for where in ((above, t, p), (below, t, p), (across, t, p), (r, t, other)):
        pl.semaphore_signal(barrier, inc=1, device_id=where, device_id_type=MESH)
    for o in range(1, tp_count):
        pl.semaphore_signal(
            barrier, inc=1, device_id=(r, (t + o) % tp_count, p), device_id_type=MESH
        )
    pl.semaphore_wait(barrier, 3 + tp_count)

    def own(k, way=0):
        return 0 if k == 0 else 2 + 4 * (k - 1) + (way if k < half else -2)

    def cross(k, way=0):
        if k == 0:
            return 1
        if k == half:
            return 2 * ring - 1
        return 2 + 4 * (k - 1) + (2 if k < half - 1 else 3) + way

    def piece(b, s):
        return blocks.at[pl.ds(b * rows + s * part, part)]

    def own_piece(s):
        return x_hbm.at[pl.ds(s * part, part)]

    def hop(b, s, src, req):
        return remote(src, piece(b, s), ring_send.at[b, s], ring_recv.at[b, s], req=req)

    def arrive(b, s):
        hop(b, s, own_piece(s), across).wait_recv()

    toward = (above, below)
    order = ((0, 0), (1, 1), (0, 1), (1, 0))

    for way, s in order:
        hop(own(1, way), s, own_piece(s), toward[way]).start()

    strip = side_w.shape[1] // tp_count

    def map_at(first, owner):
        return side_w.at[
            pl.ds(first, maps), pl.ds(pl.multiple_of(owner * strip, strip), strip)
        ]

    map_row = 2 * kv_cols + maps

    def map_hop():
        return remote(
            map_at(2 * kv_cols, t), map_at(map_row, t), map_send.at[t], map_recv.at[t], req=across
        )

    def map_spread(target, owner):
        return remote(
            map_at(map_row, owner),
            map_at(map_row, owner),
            map_send.at[target],
            map_recv.at[owner],
            tp=target,
        )

    for load in loads[:2]:
        load.wait()
    map_hop().start()
    for s in range(2):
        hop(cross(0), s, own_piece(s), across).start()
    for load in loads[2:]:
        load.wait()
    def make_messages():
        steps = sq.shape[1]
        msg_f32[...] = jnp.zeros(msg_f32.shape, F32)
        for i in range(per_dev):
            head = t * per_dev + i
            for g in range(heads):
                lanes = pl.ds(pl.multiple_of(head * cols + g * HEAD, HEAD), HEAD)
                msg_f32[i, g * steps : (g + 1) * steps] = sq[0, :, lanes].astype(F32)
            lanes = pl.ds(pl.multiple_of((head // 2) * HEAD, HEAD), HEAD)
            for s in range(steps):
                new = skv[0, s, :, lanes].astype(F32)
                first = heads * steps + s
                msg_f32[i, first : first + 1] = new[0:1]
                msg_f32[i, first + SLOTS : first + SLOTS + 1] = new[1:2]
        msg_ref[...] = msg_f32[...].astype(BF16)

    for i in range(prompts):
        uv_out[i] = uv[adapters[t * prompts + i]]
    uv_copy = remote(uv_out, uv_in, uv_sems.at[0], uv_sems.at[1], req=pair)
    uv_copy.start()
    make_messages()

    map_hop().wait_recv()
    for o in range(1, tp_count):
        map_spread((t + o) % tp_count, t).start()

    def q_copy(zz):
        return remote(q_out.at[zz], q_in.at[zz], q_send.at[zz], q_recv.at[zz], pp=other)

    def a_copy(zz):
        return remote(a_out.at[zz], a_in.at[zz], a_send.at[zz], a_recv.at[zz], pp=other)

    def b_copy(zz):
        return remote(b_out.at[zz], b_in.at[zz], b_send.at[zz], b_recv.at[zz], pp=other)

    def late_copy(i, d):
        return remote(
            b_out.at[ahead(half - 1)[d]],
            late_in.at[i, d],
            late_send.at[i, d],
            late_recv.at[i, d],
            req=pair,
            pp=(p, other)[i],
        )

    def low_copy(zz):
        return remote(
            low_out.at[zz], low_in.at[z], low_send.at[zz], low_recv.at[z], req=h * ring + zz
        )

    def low_arrival(zz):
        return remote(
            low_out.at[zz], low_in.at[zz], low_send.at[zz], low_recv.at[zz], req=h * ring + zz
        )

    def far_low(zz, source):
        return remote(
            low_out.at[zz],
            far_in.at[source],
            far_send.at[zz],
            far_recv.at[source],
            req=h * ring + zz,
            pp=other,
        )

    near_lane = lax.broadcasted_iota(jnp.int32, (rows, HEAD), 1) < maps
    prompt_of = lax.broadcasted_iota(jnp.int32, (rows, HEAD), 0) // SLOTS
    match = jnp.zeros((rows, HEAD), F32)
    for i in range(prompts):
        adapter = adapters[t * prompts + i]
        mine = jnp.where(adapter == r, 1.0, 0.0)
        theirs = jnp.where(adapter == across, 1.0, 0.0)
        match = jnp.where(prompt_of == i, jnp.where(near_lane, mine, theirs), match)

    def packed_low(both_maps):
        low = jnp.where(match > 0.0, both_maps, 0.0)
        low = low + pltpu.roll(low, HEAD // 2, 1)
        return jnp.where(near_lane[:part], low[:part], low[part:]).astype(BF16)

    waiting = []

    def project(first, places, in_own, late=False, far_ranks=False):
        count = len(places) * rows
        at = pl.ds(first * rows, count)
        side = SIDE if any(in_own) else HEAD
        got = lax.dot_general(
            blocks[at, :],
            side_w[:side],
            (((1,), (1,)), ((), ())),
            preferred_element_type=F32,
        )
        for i, (zz, mine) in enumerate(zip(places, in_own)):
            block = got[i * rows : (i + 1) * rows]
            if mine:
                a_own[zz] = block
                a_out[zz] = block.astype(BF16)
                if far_ranks:
                    low_out[zz] = packed_low(block[:, HEAD:])
                    low_copy(zz).start()
                    far_low(zz, z).start()
                a_copy(zz).start()
            else:
                b_own[zz] = block[:, :HEAD]
                b_out[zz] = block[:, :HEAD].astype(BF16)
                b_copy(zz).start()
                if late:
                    late_copy(0, i).start()
                    late_copy(1, i).start()

        def part_of(n, _):
            lanes = pl.ds(pl.multiple_of(n * SIDE, SIDE), SIDE)
            got = jnp.dot(blocks[at, :], weights[:, lanes], preferred_element_type=F32)
            for i, (zz, mine) in enumerate(zip(places, in_own)):
                block = got[i * rows : (i + 1) * rows]
                keep = (h == p) if mine else (h != p)

                @pl.when(keep)
                def _():
                    q_keep[zz, :, lanes] = block

                @pl.when(jnp.logical_not(keep))
                def _():
                    q_out[zz, :, lanes] = block.astype(BF16)

            return 0

        lax.fori_loop(0, cols // SIDE, part_of, 0)
        for zz, mine in zip(places, in_own):
            if False:

                @pl.when((h != p) if mine else (h == p))
                def _():
                    q_copy(zz).start()

            else:
                waiting.append((zz, mine))

    def kv_copy(hh, zz):
        return remote(
            kv_out.at[hh, zz],
            kv_in.at[hh, zz],
            kv_send.at[hh, zz],
            kv_recv.at[hh, zz],
            req=pair,
        )

    def finish_kv(hh, zz, total):
        kv_own[hh, zz] = total
        kv_out[hh, zz] = total.astype(BF16)
        kv_copy(hh, zz).start()

    def finish_own(zz, self_too=False, sent=False):
        a_copy(zz).wait_recv()
        total = a_own[zz] + a_in[zz].astype(F32)
        finish_kv(h, zz, total[:, :HEAD])
        if self_too:
            low_in[zz] = packed_low(total[:, HEAD:SIDE])
        elif not sent:
            low_out[zz] = packed_low(total[:, HEAD:SIDE])
            low_copy(zz).start()

    def finish_cross(zz):
        b_copy(zz).wait_recv()
        finish_kv(1 - h, zz, b_own[zz] + b_in[zz].astype(F32))

    def ahead(k):
        return [(z + ring - k) % ring, (z + k) % ring]

    def arrive_own(k):
        for way, s in order:
            arrive(own(k, way), s)
            src = piece(own(k, way), s)
            if k < half - 1:
                hop(own(k + 1, way), s, src, toward[way]).start()
            elif s == way:
                hop(own(half), s, src, toward[way]).start()
            if k == 1:
                hop(cross(k, way), s, src, across).start()

    def arrive_cross(k, which=order):
        for way, s in which:
            arrive(cross(k, way), s)
            src = piece(cross(k, way), s)
            if k < half - 1:
                hop(cross(k + 1, way), s, src, toward[way]).start()

    def arrive_both(b):
        for s in range(2):
            arrive(b, s)

    def step_copy(i):
        target = t * per_dev + i
        return remote(
            msg_ref.at[i],
            step_in.at[r % per_dev],
            step_send.at[i],
            step_got.at[r % per_dev],
            req=target,
            tp=r // per_dev,
        )

    def step_self(i):
        return (t * per_dev + i == r) & (r // per_dev == t)

    both = [True, True]
    neither = [False, False]

    arrive_own(1)
    arrive_both(cross(0))
    if half > 2:
        arrive_own(2)
    for o in range(1, tp_count):
        map_spread(t, (t + o) % tp_count).wait_recv()
    project(0, [z, z], [True, False])
    if half > 2:
        project(own(1), ahead(1), both)
    for k in range(3, half):
        arrive_own(k)
        arrive_cross(k - 2)
        project(own(k - 1), ahead(k - 1), both)
        if k < half - 1:
            project(cross(k - 2), ahead(k - 2), neither)
    for s in range(2):
        arrive(own(half), s)
        hop(cross(half), s, piece(own(half), s), across).start()
    pl.semaphore_signal(hello, inc=1, device_id=(across, t, p), device_id_type=MESH)
    project(own(half - 1), ahead(half - 1) + [far], [True] * 3, far_ranks=True)
    pl.semaphore_wait(hello, 1)
    for i in range(per_dev):

        @pl.when(step_self(i))
        def _():
            step_in[r % per_dev] = msg_ref[i]

        @pl.when(jnp.logical_not(step_self(i)))
        def _():
            step_copy(i).start()

    if half > 3:
        project(cross(half - 3), ahead(half - 3), neither)
    finish_own(z, True)
    finish_cross(z)
    for k in range(1, half - 1):
        for zz in ahead(k):
            finish_own(zz)
    if half > 2:
        arrive_cross(half - 2, order[:2])
    for zz in ahead(half - 1) + [far]:
        finish_own(zz, sent=True)
    if half > 2:
        arrive_cross(half - 2, order[2:])

    distances = sorted(range(ring), key=lambda o: -min(o, ring - o))

    def others(body):
        for o in distances:
            body((1 - h) * ring + (z + o) % ring)
            if o > 0:
                body(h * ring + (z + o) % ring)

    def column(body):
        for o in distances[:-1]:
            body((z + o) % ring)

    def rank_copy(target, slot):
        return remote(
            rank_all.at[slot], rank_all.at[slot], rank_send.at[target], rank_recv.at[slot], req=target
        )

    column(lambda zz: low_arrival(zz).wait_recv())
    for zz in ahead(half - 1) + [far]:
        far_low(zz, zz).wait_recv()
    low = low_in[0].astype(F32)
    for zz in range(1, ring):
        low = low + low_in[zz].astype(F32)
    for zz in ahead(half - 1) + [far]:
        low = low + far_in[zz].astype(F32)
    rank_all[r] = low.astype(BF16)
    others(lambda target: rank_copy(target, r).start())

    if half > 2:
        project(cross(half - 2), ahead(half - 2), neither)

    for k in range(1, half - 2):
        for zz in ahead(k):
            finish_cross(zz)
    arrive_both(cross(half))
    project(cross(half), [far], [False])

    if half > 2:
        for zz in ahead(half - 2):
            finish_cross(zz)
    def take_pair(hh, zz):
        kv_copy(hh, zz).wait_recv()
        kv_oth[hh, zz] = kv_in[hh, zz].astype(F32)

    uv_copy.wait_recv()
    for o in range(ring):
        take_pair(h, (z + o) % ring)
    for o in (0, 1, ring - 1):
        if o not in (half - 1, half + 1):
            take_pair(1 - h, (pair + o) % ring)
    arrive_cross(half - 1)
    project(cross(half - 1), ahead(half - 1), neither, late=True)
    for zz, mine in waiting:

        @pl.when((h != p) if mine else (h == p))
        def _():
            q_copy(zz).start()


    finish_cross(far)
    for zz in ahead(half - 1):
        b_copy(zz).wait_recv()
        kv_own[1 - h, zz] = b_own[zz] + b_in[zz].astype(F32)
    for i in range(2):
        for d in range(2):
            late_copy(i, d).wait_recv()
    for d in range(2):
        kv_oth[1 - h, pair_late[d]] = late_in[0, d].astype(F32) + late_in[1, d].astype(F32)
    for o in range(2, ring - 1):
        if o not in (half - 1, half + 1):
            take_pair(1 - h, (pair + o) % ring)

    even = r % 2 == 0
    slots = req_count * SLOTS
    share = slots // 2
    low_lane = lax.broadcasted_iota(jnp.int32, (slots, HEAD), 1) < HEAD // 2
    scale = HEAD ** (-0.5)

    def halves(n):
        at = pl.ds(pl.multiple_of(n * SLOTS, SLOTS), SLOTS)
        mine = kv_own[:, :, at, :].reshape(slots, HEAD)
        theirs = kv_oth[:, :, at, :].reshape(slots, HEAD)
        return jnp.where(even, mine, theirs), jnp.where(even, theirs, mine)

    def keys_of(n):
        first, second = halves(n)
        return jnp.where(low_lane, first, pltpu.roll(second, HEAD // 2, 1)).astype(BF16)

    def values_of(n):
        first, second = halves(n)
        v = jnp.where(low_lane, pltpu.roll(first, HEAD // 2, 1), second)
        uv_mine, uv_theirs = uv_out[n], uv_in[n]
        up_v = jnp.concatenate(
            [jnp.where(even, uv_mine, uv_theirs), jnp.where(even, uv_theirs, uv_mine)], axis=1
        )
        at = pl.ds(pl.multiple_of(n * SLOTS, SLOTS), SLOTS)
        rank_rows = ranks[:, at, :].reshape(slots, HEAD).astype(BF16)
        v = v + jnp.dot(rank_rows[:, rank:maps], up_v, preferred_element_type=F32)
        return v.astype(BF16)

    steps = step_out.shape[1] // heads
    qrows = heads * steps

    def step_arrival(j):
        source_req = t * per_dev + j
        return remote(
            msg_ref.at[0],
            step_in.at[j],
            step_send.at[0],
            step_got.at[j],
            req=source_req,
            tp=r // per_dev,
        )

    def out_copy(j, target):
        return remote(
            step_out.at[j],
            step_recv.at[r],
            out_send.at[j, target],
            out_got.at[r],
            req=t * per_dev + j,
            tp=target,
        )

    def out_arrival(source):
        return remote(
            step_out.at[0],
            step_recv.at[source],
            out_send.at[0, 0],
            out_got.at[source],
            req=source,
            tp=r // per_dev,
        )

    for j in range(per_dev):

        @pl.when(jnp.logical_not((t * per_dev + j == r) & (r // per_dev == t)))
        def _():
            step_arrival(j).wait_recv()

    weighed = []
    for j in range(per_dev):
        n = 2 * j + p
        length = lens[t * prompts + n]
        k = keys_of(n)
        k_full[n] = k
        got = step_in[j]
        qs = got[:qrows]
        tail = got[qrows:].astype(F32)
        new_k = tail[:SLOTS].astype(BF16)
        new_v = tail[SLOTS : 2 * SLOTS].astype(BF16)
        s_old = lax.dot_general(qs, k, (((1,), (1,)), ((), ())), preferred_element_type=F32) * scale
        s_new = (
            lax.dot_general(qs, new_k, (((1,), (1,)), ((), ())), preferred_element_type=F32) * scale
        )
        s_old = jnp.where(lax.broadcasted_iota(jnp.int32, (qrows, slots), 1) < length, s_old, NEG)
        at_step = lax.broadcasted_iota(jnp.int32, (qrows, SLOTS), 0) % steps
        at_new = lax.broadcasted_iota(jnp.int32, (qrows, SLOTS), 1)
        s_new = jnp.where(at_new <= at_step, s_new, NEG)
        top = jnp.maximum(
            jnp.max(s_old, axis=1, keepdims=True), jnp.max(s_new, axis=1, keepdims=True)
        )
        e_old, e_new = jnp.exp(s_old - top), jnp.exp(s_new - top)
        total = jnp.sum(e_old, axis=1, keepdims=True) + jnp.sum(e_new, axis=1, keepdims=True)

        def weigh(e, values):
            coarse = e.astype(BF16)
            fine = (e - coarse.astype(F32)).astype(BF16)
            return jnp.dot(coarse, values, preferred_element_type=F32) + jnp.dot(
                fine, values, preferred_element_type=F32
            )

        weighed.append((weigh, e_old, weigh(e_new, new_v), 1.0 / total))

    others(lambda source: rank_copy(source, source).wait_recv())
    for source in range(req_count):
        packed = rank_all[source].astype(F32)
        ranks[source, :part] = packed
        ranks[source, part:] = pltpu.roll(packed, HEAD // 2, 1)
    for j in range(per_dev):
        n = 2 * j + p
        v = values_of(n)
        v_full[n] = v
        weigh, e_old, new_part, inverse = weighed[j]
        step_out[j] = ((weigh(e_old, v) + new_part) * inverse).astype(BF16)
    for o in sorted(range(tp_count), key=lambda o: -min(o, tp_count - o)):
        target = (t + o) % tp_count
        for j in range(per_dev):
            if o == 0:

                @pl.when(t * per_dev + j == r)
                def _():
                    step_recv[r] = step_out[j]

                @pl.when(t * per_dev + j != r)
                def _():
                    out_copy(j, t).start()
            else:
                out_copy(j, target).start()

    for j in range(per_dev):
        n = 2 * j + 1 - p
        k_full[n] = keys_of(n)
        v_full[n] = values_of(n)
    for zz in range(ring):
        q_copy(zz).wait_recv()
    base_q = (q_keep[...] + q_in[...].astype(F32)).reshape(ring, prompts, SLOTS, cols)
    my_ranks = ranks[pl.ds(p * ring, ring)].reshape(ring, prompts, SLOTS, HEAD)
    row_pos = lax.broadcasted_iota(jnp.int32, (heads * share, slots), 0) % share + p * share
    col_pos = lax.broadcasted_iota(jnp.int32, (heads * share, slots), 1)
    out_pos = lax.broadcasted_iota(jnp.int32, (heads * share, HEAD), 0) % share + p * share
    def prefill_copy(i):
        return pltpu.make_async_copy(prefill.at[i], prefill_ref.at[i], prefill_sem.at[i])

    for i in range(prompts):
        length = lens[t * prompts + i]
        adapter = adapters[t * prompts + i]
        k, v = k_full[i], v_full[i]
        rank_q = my_ranks[:, i].reshape(share, HEAD).astype(BF16)[:, :rank]
        q = base_q[:, i].reshape(share, cols) + jnp.dot(
            rank_q, uq[adapter], preferred_element_type=F32
        )
        q = q.astype(BF16)
        q = jnp.concatenate([q[:, g * HEAD : (g + 1) * HEAD] for g in range(heads)], axis=0)
        s = lax.dot_general(q, k, (((1,), (1,)), ((), ())), preferred_element_type=F32) * scale
        s = jnp.where((col_pos <= row_pos) & (col_pos < length), s, NEG)
        e = jnp.exp(s - jnp.max(s, axis=1, keepdims=True))
        w = (e / jnp.sum(e, axis=1, keepdims=True)).astype(BF16)
        o = jnp.dot(w, v, preferred_element_type=F32)
        o = jnp.where(out_pos < length, o, 0.0).astype(BF16)
        for g in range(heads):
            prefill[i, :, g * HEAD : (g + 1) * HEAD] = o[g * share : (g + 1) * share]
        prefill_copy(i).start()

    for b in range(1, 2 * ring):
        for s in range(2):
            hop(b, s, own_piece(s), above).wait_send()
    for target in range(tp_count):
        map_spread(target, t).wait_send()
    for zz in range(ring):
        q_copy(zz).wait_send()
        a_copy(zz).wait_send()
        b_copy(zz).wait_send()
        for hh in range(2):

            mine = [(hh == 1 - h) & (zz == late_zz) for late_zz in ahead(half - 1)]

            @pl.when(jnp.logical_not(mine[0] | mine[1]))
            def _():
                kv_copy(hh, zz).wait_send()

    for i in range(2):
        for d in range(2):
            late_copy(i, d).wait_send()
    column(lambda zz: low_copy(zz).wait_send())
    for zz in ahead(half - 1) + [far]:
        far_low(zz, z).wait_send()
    others(lambda target: rank_copy(target, r).wait_send())
    uv_copy.wait_send()
    for i in range(per_dev):

        @pl.when(jnp.logical_not(step_self(i)))
        def _():
            step_copy(i).wait_send()

    for j in range(per_dev):
        for target in range(tp_count):

            @pl.when(jnp.logical_not((t * per_dev + j == r) & (target == t)))
            def _():
                out_copy(j, target).wait_send()

    def got_out(source, _):
        @pl.when(jnp.logical_not((source == r) & (r // per_dev == t)))
        def _():
            out_arrival(source).wait_recv()

        return 0

    lax.fori_loop(0, req_count, got_out, 0)
    decoded_ref[...] = step_recv[...]
    for i in range(prompts):
        prefill_copy(i).wait()


def deliver(prefill_in, decoded_in, prefill_ref, decoded_ref):
    prefill_ref[...] = prefill_in[...]
    steps = decoded_ref.shape[1]
    heads = decoded_in.shape[1] // steps
    for source in range(decoded_in.shape[0]):
        got = decoded_in[source].astype(F32)
        for g in range(heads):
            lanes = pl.ds((source * heads + g) * HEAD, HEAD)
            decoded_ref[0, :, lanes] = got[g * steps : (g + 1) * steps].astype(BF16)


def local(
    prompt_states,
    prompt_lengths,
    adapter_ids,
    w_query,
    w_key,
    value_weight,
    down_query,
    up_query,
    down_value,
    value_up_weight,
    step_queries,
    step_keyvals,
):
    req_count, tp_count = lax.axis_size("req"), lax.axis_size("tp")
    prompts, slots, width = prompt_states.shape
    rows = prompts * slots
    cols = w_query.shape[1]
    kv_cols = w_key.shape[1]
    rank = down_query.shape[2]
    adapter_count = up_query.shape[0]
    ring = req_count // 2
    heads = cols // HEAD
    steps = step_queries.shape[1]
    per_dev = req_count // tp_count
    total_slots = req_count * slots

    vmem = pl.BlockSpec(memory_space=pltpu.VMEM)
    smem = pl.BlockSpec(memory_space=pltpu.SMEM)
    hbm = pl.BlockSpec(memory_space=pl.ANY)
    dma = pltpu.SemaphoreType.DMA
    prefill, decoded = pl.pallas_call(
        functools.partial(kernel, req_count, tp_count),
        out_shape=(
            jax.ShapeDtypeStruct((prompts, total_slots // 2, cols), BF16),
            jax.ShapeDtypeStruct((req_count, heads * steps, HEAD), BF16),
        ),
        in_specs=[smem, smem] + [hbm] * 10,
        out_specs=(hbm, vmem),
        scratch_shapes=[
            pltpu.VMEM((per_dev, heads * steps + 2 * SLOTS, HEAD), BF16),
            pltpu.VMEM((per_dev, heads * steps + 2 * SLOTS, HEAD), F32),
            pltpu.VMEM(step_queries.shape, BF16),
            pltpu.VMEM(step_keyvals.shape, BF16),
            pltpu.VMEM((req_count * rows, width), BF16),
            pltpu.VMEM((width, cols), BF16),
            pltpu.VMEM((SIDE, width), BF16),
            pltpu.VMEM((adapter_count, rank, cols), BF16),
            pltpu.VMEM((adapter_count, rank, kv_cols), BF16),
            pltpu.VMEM((ring, rows, cols), F32),
            pltpu.VMEM((ring, rows, cols), BF16),
            pltpu.VMEM((ring, rows, cols), BF16),
            pltpu.VMEM((ring, rows, SIDE), F32),
            pltpu.VMEM((ring, rows, SIDE), BF16),
            pltpu.VMEM((ring, rows, SIDE), BF16),
            pltpu.VMEM((ring, rows, HEAD), F32),
            pltpu.VMEM((ring, rows, HEAD), BF16),
            pltpu.VMEM((ring, rows, HEAD), BF16),
            pltpu.VMEM((2, ring, rows, HEAD), F32),
            pltpu.VMEM((2, ring, rows, HEAD), F32),
            pltpu.VMEM((2, ring, rows, HEAD), BF16),
            pltpu.VMEM((2, ring, rows, HEAD), BF16),
            pltpu.VMEM((2, 2, rows, HEAD), BF16),
            pltpu.VMEM((ring, rows // 2, HEAD), BF16),
            pltpu.VMEM((ring, rows // 2, HEAD), BF16),
            pltpu.VMEM((ring, rows // 2, HEAD), BF16),
            pltpu.VMEM((req_count, rows // 2, HEAD), BF16),
            pltpu.VMEM((req_count, rows, HEAD), F32),
            pltpu.VMEM((prompts, rank, kv_cols), BF16),
            pltpu.VMEM((prompts, rank, kv_cols), BF16),
            pltpu.VMEM((prompts, total_slots, HEAD), BF16),
            pltpu.VMEM((prompts, total_slots, HEAD), BF16),
            pltpu.VMEM((per_dev, heads * steps + 2 * SLOTS, HEAD), BF16),
            pltpu.VMEM((per_dev, heads * steps, HEAD), BF16),
            pltpu.VMEM((req_count, heads * steps, HEAD), BF16),
            dma((10,)),
            dma((req_count, 2)),
            dma((req_count, 2)),
            dma((tp_count,)),
            dma((tp_count,)),
            dma((ring,)),
            dma((ring,)),
            dma((ring,)),
            dma((ring,)),
            dma((ring,)),
            dma((ring,)),
            dma((2, ring)),
            dma((2, ring)),
            dma((2, 2)),
            dma((2, 2)),
            dma((ring,)),
            dma((ring,)),
            dma((ring,)),
            dma((ring,)),
            dma((req_count,)),
            dma((req_count,)),
            dma((2,)),
            dma((per_dev,)),
            dma((per_dev,)),
            dma((per_dev, tp_count)),
            dma((req_count,)),
            pltpu.SemaphoreType.REGULAR,
            pltpu.VMEM((prompts, total_slots // 2, cols), BF16),
            dma((prompts,)),
        ],
        compiler_params=pltpu.CompilerParams(
            collective_id=0, has_side_effects=True, vmem_limit_bytes=56 * 1024 * 1024
        ),
        cost_estimate=pl.CostEstimate(
            flops=2 * req_count * rows * width * (cols + SIDE),
            bytes_accessed=2 * width * (cols + SIDE),
            transcendentals=0,
        ),
    )(
        prompt_lengths,
        adapter_ids,
        prompt_states.reshape(rows, width),
        w_query,
        w_key.T,
        value_weight.T,
        down_query[0].T,
        down_value[0].T,
        up_query,
        value_up_weight,
        step_queries,
        step_keyvals,
    )
    return pl.pallas_call(
        deliver,
        out_shape=(
            jax.ShapeDtypeStruct(prefill.shape, BF16),
            jax.ShapeDtypeStruct(step_queries.shape, BF16),
        ),
        in_specs=[vmem, vmem],
        out_specs=(vmem, vmem),
    )(prefill, decoded)


def solution(mesh):
    in_specs = (
        P("tp", "req", "pp"),
        P(),
        P(),
        P("pp", "req"),
        P("pp", "req"),
        P("pp", "req"),
        P("req", "pp", None),
        P(None, None, "req"),
        P("req", "pp", None),
        P(None, None, "req"),
        P(("req", "pp"), None, None),
        P(("req", "pp"), None, None, None),
    )
    out_specs = (P("tp", "pp", "req"), P(("req", "pp"), None, None))
    return jax.shard_map(local, mesh=mesh, in_specs=in_specs, out_specs=out_specs, check_vma=False)
```
